32 devices in a mesh: rep: 2 (over x), ctx: 16 (over z, y, core).
Axes of the slice: x: 2, y: 2, z: 4, core: 2. Of those that a mesh axis runs over, the one named last changes fastest.
Arguments:
- q_nope: bfloat16 [2048, 16384], P(('rep', 'ctx')), parts along dimension 0, may hold values from -40 to 40
- q_rope: bfloat16 [2048, 2048], P(('rep', 'ctx')), parts along dimension 0, may hold values from -3 to 3
- c_kv: bfloat16 [2048, 512], P(('rep', 'ctx')), parts along dimension 0, may hold values from -4 to 4
- k_rope: bfloat16 [2048, 64], P(('rep', 'ctx')), parts along dimension 0, may hold values from -4 to 4
- w_value: bfloat16 [32, 512, 128], replicated, may hold values from -0.25 to 0.25
- norm_gain: float32 [4096], replicated, may hold values from 0.5 to 1.5
- expert_ids: int32 [2048, 1], P(('rep', 'ctx')), parts along dimension 0, may hold values from 0 to 1; in each aligned block of 64 rows (0 to 63, 64 to 127, ...) at most 64 rows name the same one
- gate_fixed: int32 [2048, 1], P(('rep', 'ctx')), parts along dimension 0, may hold values from 16384 to 65535
- w_gate: bfloat16 [16, 4096, 256], P('ctx'), may hold values from -0.09375 to 0.09375
- w_up: bfloat16 [16, 4096, 256], P('ctx'), may hold values from -0.09375 to 0.09375
- w_down: bfloat16 [16, 256, 4096], P('ctx'), may hold values from -0.125 to 0.125
Outputs:
- mixed_out: bfloat16 [2048, 4096], P(('rep', 'ctx')), parts along dimension 0
The draws below stay inside these ranges and needn't reach their ends.
There are 2 independent parts, one for each index of `rep`. The reference program is written for one: setup_inputs(seed, part) draws one part's arguments, and reference() takes and returns one part's arrays. A program takes and returns all parts, laid end to end along the dimension named above; an argument that names none is the same for every part. Nothing has to cross between parts.
Inputs may be any that keep to these rules, and one draw needn't show every extreme that they name: `expert_ids`: in the rows of one device no expert is named more than 64 times, and in every draw some device names some expert exactly 64 times.
All inputs are finite; a program needn't handle non-finite values.
Results may differ from the reference program's by a relative error of at most 0.018.
Values may be sent and summed in bfloat16 or wider, within the bound.
No kernel may reach another device: no remote copies, remote signals or barrier semaphores. Data moves between devices by JAX's collectives and lax.ppermute only.
A program may use at most 128 MiB of HBM per device.

```python
import math
import jax
import jax.numpy as jnp
import numpy as np
from jax import lax

HEADS = 32
LAT = 512
ROPE = 64
VD = 128
DV = 4096
F = 2048
SPAN = 8
F_DEV = 256
TOP = 1
TOK_DEV = 64
LEN = 1024
TOKENS = 1024
PROMPTS = 1
EXPERTS = 2
SHARDS = 16
CAP = 64
N_CTX = 16


def shared_latent(key):
    return jnp.clip(jax.random.normal(jax.random.fold_in(key, 5), (TOKENS, LAT), jnp.float32), -4.0, 4.0)


def draw_c_kv(key, part):
    latent = shared_latent(key)
    return latent.astype(jnp.bfloat16)


def draw_q_nope(key, part):
    key = jax.random.fold_in(key, 13)
    drawn = 0.6 * jnp.clip(jax.random.normal(key, (TOKENS, HEADS, LAT), jnp.float32), -4.0, 4.0)
    return drawn.reshape(TOKENS, HEADS * LAT).astype(jnp.bfloat16)


def with_ends(drawn, key, smallest, high):
    spot = [jax.random.randint(jax.random.fold_in(key, axis), (), 0, length) for axis, length in enumerate(drawn.shape)]
    longest = drawn.shape.index(max(drawn.shape))
    neighbour = spot[:longest] + [(spot[longest] + 1) % drawn.shape[longest]] + spot[longest + 1:]
    return drawn.at[tuple(spot)].set(smallest).at[tuple(neighbour)].set(high)


def levels(rng, shape, shards, least, largest):
    def one(axis_at, blocks):
        draws = jax.random.uniform(jax.random.fold_in(jax.random.fold_in(rng, 6), axis_at), (blocks,), jnp.float32, least / len(shards), largest / len(shards))
        return jnp.repeat(jnp.exp(draws), shape[axis_at] // blocks).reshape((-1,) + (1,) * (len(shape) - axis_at - 1))

    loudness = one(*shards[0])
    for cut in shards[1:]:
        loudness = loudness * one(*cut)
    return loudness


def shared_out(own_key, own, number, rows, number_of, top, limit, lean):
    order = jax.random.permutation(own_key, number_of)
    crowded, usual = shares(number_of, rows * top, limit, lean, True), shares(number_of, rows * top, limit, lean, False)
    places = jnp.arange(number_of)

    def named(tallies, rotation):
        used = int((tallies > 0).sum())
        fixed = max(1, used // 4)
        passed = fixed + (places - fixed + rotation * (used - fixed)) % max(1, number_of - fixed)
        return jnp.zeros((number_of,), jnp.int32).at[order[jnp.where(places < fixed, places, passed)]].set(jnp.asarray(tallies, jnp.int32))

    tallies = jnp.where(number % 4 == 0, named(crowded, number // 4), named(usual, number - number // 4 - 1))
    mixed = jax.random.permutation(jax.random.fold_in(own, 3), number_of)
    source_of, taker = mixed[0:number_of // 2 * 2:2], mixed[1:number_of // 2 * 2:2]
    slack = jnp.minimum(tallies[source_of] - 1, limit - tallies[taker]) // 2
    slack = jnp.where((source_of == order[0]) | (taker == order[0]) | (tallies[taker] == 0), 0, jnp.maximum(slack, 0))
    passed = jax.random.randint(jax.random.fold_in(own, 4), (number_of // 2,), 0, 1 << 20) % (slack + 1)
    tallies = tallies.at[source_of].add(-passed).at[taker].add(passed)
    labels = jnp.searchsorted(jnp.cumsum(tallies), jnp.arange(rows * top), side="right").astype(jnp.int32)
    grid = labels.reshape(top, rows).T
    grid = grid[jax.random.permutation(jax.random.fold_in(own, 1), rows)]
    rotation = jax.random.randint(jax.random.fold_in(own, 2), (rows, 1), 0, top)
    return jnp.take_along_axis(grid, (jnp.arange(top)[None, :] + rotation) % top, axis=1)


def shares(count, total, limit, lean, full):
    loads = [(1 << 20) // math.isqrt(rank ** lean) + 1 for rank in range(1, count + 1)]
    largest = limit if full else min(limit, max(-(-total // count), total * loads[0] // sum(loads)))
    least = 1 if total - largest >= count - 1 else 0
    holding, rest = [largest] + [least] * (count - 1), total - largest - least * (count - 1)
    while rest > 0:
        movable = [i for i in range(1, count) if holding[i] < largest] or [i for i in range(1, count) if holding[i] < limit]
        mass, remaining = sum([loads[i] for i in movable]), rest
        for i in movable:
            addition = min(limit - holding[i], max(1, remaining * loads[i] // mass), rest)
            holding[i] = holding[i] + addition
            rest = rest - addition
    return np.array(holding)


def normal_values(stream_key, shape, scale, most, cuts=(), kind=jnp.bfloat16):
    array = scale * jax.random.normal(stream_key, shape, jnp.float32)
    if cuts:
        array = array * levels(stream_key, shape, cuts, -0.22, 0.18)
    return jnp.clip(array, -most, most).astype(kind)


def setup_inputs(seed: int = 0, part: int = 0) -> dict:
    arg_keys = jax.random.split(jax.random.key(seed), 12)
    part_keys = jax.random.split(jax.random.fold_in(arg_keys[11], part), 12)
    q_nope = draw_q_nope(jax.random.fold_in(jax.random.fold_in(arg_keys[11], part), 71), part)
    q_rope = normal_values(part_keys[1], (TOKENS, HEADS * ROPE), 0.6, 3.0, ((0, 16),))
    c_kv = draw_c_kv(jax.random.fold_in(jax.random.fold_in(arg_keys[11], part), 71), part)
    k_rope = normal_values(part_keys[3], (TOKENS, ROPE), 1.0, 4.0, ((0, 16),))
    w_value = normal_values(arg_keys[4], (HEADS, LAT, VD), LAT ** -0.5, 0.25)
    norm_gain = jnp.clip(1.0 + 0.1 * jax.random.normal(arg_keys[5], (DV,), jnp.float32), 0.5, 1.5)
    expert_ids_keys = jax.random.split(jax.random.fold_in(part_keys[6], 1), TOKENS // TOK_DEV)
    expert_ids_turns = jax.random.permutation(jax.random.fold_in(part_keys[6], 3), TOKENS // TOK_DEV)
    expert_ids = jax.vmap(lambda own, number: shared_out(jax.random.fold_in(part_keys[6], 2), own, number, TOK_DEV, EXPERTS, TOP, CAP, 2))(expert_ids_keys, expert_ids_turns).reshape((TOKENS, TOP))
    gate_fixed = with_ends(jax.random.randint(part_keys[7], (TOKENS, TOP), 16384, 65536), jax.random.fold_in(part_keys[7], 1), 16384, 65535).astype(jnp.int32)
    w_gate = normal_values(arg_keys[8], (SHARDS, DV, F_DEV), DV ** -0.5, 0.09375, ((0, 16),))
    w_up = normal_values(arg_keys[9], (SHARDS, DV, F_DEV), DV ** -0.5, 0.09375, ((0, 16),))
    w_down = normal_values(arg_keys[10], (SHARDS, F_DEV, DV), F ** -0.5, 0.125, ((0, 16),))
    return dict(q_nope=q_nope, q_rope=q_rope, c_kv=c_kv, k_rope=k_rope, w_value=w_value, norm_gain=norm_gain, expert_ids=expert_ids, gate_fixed=gate_fixed, w_gate=w_gate, w_up=w_up, w_down=w_down)


SCORE_SCALE = 192.0 ** (-0.5)
NORM_EPS = 1e-06
NEG_FILL = -1e+30

def attend_prompt(packed):
    query_lat, query_rope, latent_keys, rope_keys = packed
    scores = jnp.einsum('thc,sc->hts', query_lat.astype(jnp.float32), latent_keys.astype(jnp.float32))
    scores = (scores + jnp.einsum('thr,sr->hts', query_rope.astype(jnp.float32), rope_keys.astype(jnp.float32))) * SCORE_SCALE
    positions = jnp.arange(latent_keys.shape[0])
    allowed = (positions[None, :] <= positions[:, None])[None]
    scores = jnp.where(allowed, scores, NEG_FILL)
    row_max = lax.optimization_barrier(jnp.max(scores, axis=2, keepdims=True))
    weights_f = jnp.where(allowed, jnp.exp(scores - row_max), 0.0)
    row_sum = lax.optimization_barrier(jnp.sum(weights_f, axis=2))
    weights = weights_f.astype(jnp.bfloat16)
    mix_acc = jnp.einsum('hts,sc->thc', weights.astype(jnp.float32), latent_keys.astype(jnp.float32))
    return (mix_acc / jnp.transpose(row_sum)[:, :, None]).astype(jnp.bfloat16)

def reference(q_nope, q_rope, c_kv, k_rope, w_value, norm_gain, expert_ids, gate_fixed, w_gate, w_up, w_down):
    query_lat = q_nope.reshape(PROMPTS, LEN, HEADS, LAT)
    query_rope = q_rope.reshape(PROMPTS, LEN, HEADS, ROPE)
    latent_keys = c_kv.reshape(PROMPTS, LEN, LAT)
    rope_keys = k_rope.reshape(PROMPTS, LEN, ROPE)
    latent_out = lax.map(attend_prompt, (query_lat, query_rope, latent_keys, rope_keys)).reshape(TOKENS, HEADS, LAT)
    values = jnp.einsum('thc,hcv->thv', latent_out.astype(jnp.float32), w_value.astype(jnp.float32))
    values = values.astype(jnp.bfloat16).reshape(TOKENS, DV)
    values_f = values.astype(jnp.float32)
    normed = values_f * lax.rsqrt(lax.optimization_barrier(jnp.mean(values_f * values_f, axis=1, keepdims=True)) + NORM_EPS) * norm_gain
    normed = normed.astype(jnp.bfloat16)
    pair_ids = expert_ids.reshape(N_CTX, TOK_DEV * TOP)
    one_hot = (pair_ids[:, :, None] == jnp.arange(EXPERTS)[None, None, :]).astype(jnp.int32)
    earlier = jnp.cumsum(one_hot, axis=1) - one_hot
    pair_slot = lax.optimization_barrier(jnp.sum(earlier * one_hot, axis=2)).astype(jnp.int32)
    source = jnp.broadcast_to(jnp.arange(N_CTX, dtype=jnp.int32)[:, None], pair_ids.shape)
    pair_rows = jnp.repeat(normed.reshape(N_CTX, TOK_DEV, DV), TOP, axis=1)
    buffers = jnp.zeros((EXPERTS, N_CTX, CAP, DV), jnp.bfloat16).at[pair_ids, source, pair_slot].set(pair_rows)
    gate_split = w_gate.reshape(EXPERTS, SPAN, DV, F_DEV)
    up_split = w_up.reshape(EXPERTS, SPAN, DV, F_DEV)
    down_split = w_down.reshape(EXPERTS, SPAN, F_DEV, DV)

    def run_expert(packed):
        rows, gate_w, up_w, down_w = packed
        rows_f = rows.astype(jnp.float32)
        gate_act = jnp.einsum('rd,jdf->jrf', rows_f, gate_w.astype(jnp.float32))
        up_act = jnp.einsum('rd,jdf->jrf', rows_f, up_w.astype(jnp.float32))
        hidden = (jax.nn.silu(gate_act) * up_act).astype(jnp.bfloat16)
        part = jnp.einsum('jrf,jfd->jrd', hidden.astype(jnp.float32), down_w.astype(jnp.float32)).astype(jnp.bfloat16)
        return lax.optimization_barrier(jnp.sum(part.astype(jnp.float32), axis=0))
    expert_out = lax.map(run_expert, (buffers.reshape(EXPERTS, N_CTX * CAP, DV), gate_split, up_split, down_split))
    expert_out = expert_out.reshape(EXPERTS, N_CTX, CAP, DV)
    picked = expert_out[pair_ids, source, pair_slot].reshape(TOKENS, TOP, DV)
    gate_weight = gate_fixed.astype(jnp.float32) / 65536.0
    branch = lax.optimization_barrier(jnp.sum(gate_weight[:, :, None] * picked, axis=1))
    return (values_f + branch).astype(jnp.bfloat16)
```

```python
import functools

import jax
import jax.numpy as jnp
from jax import lax
from jax.experimental import pallas as pl
from jax.experimental.pallas import tpu as pltpu
from jax.sharding import PartitionSpec as P

HEADS = 32
LAT = 512
ROPE = 64
VD = 128
SPAN = 8
CORES = 2

SCORE_SCALE = 192.0 ** (-0.5)
NORM_EPS = 1e-06
NEG_FILL = -1e30

HEAD_GROUP = 8
KEY_BLOCK = 512


def attention_kernel(
    index_ref, q_ref, qr_ref, keys_ref, wv_ref, gain_ref, values_ref, normed_ref, stack_ref,
    max_ref, sum_ref, acc_ref, *, tok, key_block,
):
    group = pl.program_id(0)
    my_index = index_ref[0]
    rows = HEAD_GROUP * tok
    lane = lax.broadcasted_iota(jnp.int32, (tok, 2 * ROPE), 1)
    for head in range(HEAD_GROUP):
        at = pl.ds(head * tok, tok)
        stack_ref[at, 0:LAT] = q_ref[:, head * LAT : (head + 1) * LAT]
        pair = qr_ref[:, (head // 2) * 2 * ROPE : (head // 2 + 1) * 2 * ROPE]
        keep = (lane < ROPE) if head % 2 == 0 else (lane >= ROPE)
        stack_ref[at, LAT : LAT + 2 * ROPE] = jnp.where(keep, pair, jnp.zeros_like(pair))
    max_ref[...] = jnp.full_like(max_ref, NEG_FILL)
    sum_ref[...] = jnp.zeros_like(sum_ref)
    acc_ref[...] = jnp.zeros_like(acc_ref)
    row_pos = my_index * tok + lax.rem(
        lax.broadcasted_iota(jnp.int32, (rows, key_block), 0), jnp.int32(tok)
    )
    key_iota = lax.broadcasted_iota(jnp.int32, (rows, key_block), 1)

    def step(block, carry):
        start = pl.multiple_of(block * key_block, key_block)
        keys = keys_ref[pl.ds(start, key_block), :]
        scores = lax.dot_general(
            stack_ref[...], keys, (((1,), (1,)), ((), ())), preferred_element_type=jnp.float32
        )
        scores = jnp.where(key_iota + start <= row_pos, scores * SCORE_SCALE, NEG_FILL)
        old_max = max_ref[...]
        new_max = jnp.maximum(old_max, jnp.max(scores, axis=1, keepdims=True))
        weights = jnp.exp(scores - new_max)
        rescale = jnp.exp(old_max - new_max)
        max_ref[...] = new_max
        sum_ref[...] = sum_ref[...] * rescale + jnp.sum(weights, axis=1, keepdims=True)
        acc_ref[...] = acc_ref[...] * rescale + jnp.dot(
            weights.astype(jnp.bfloat16), keys[:, 0:LAT], preferred_element_type=jnp.float32
        )
        return carry

    blocks = ((my_index + 1) * tok + key_block - 1) // key_block
    lax.fori_loop(0, blocks, step, 0)
    latent = (acc_ref[...] / sum_ref[...]).astype(jnp.bfloat16)
    parts = [
        jnp.dot(
            latent[head * tok : (head + 1) * tok], wv_ref[head], preferred_element_type=jnp.float32
        ).astype(jnp.bfloat16)
        for head in range(HEAD_GROUP)
    ]
    wide = HEAD_GROUP * VD
    values_ref[:, pl.ds(pl.multiple_of(group * wide, wide), wide)] = jnp.concatenate(parts, axis=1)

    @pl.when(group == HEADS // HEAD_GROUP - 1)
    def _():
        values = values_ref[...].astype(jnp.float32)
        square = jnp.mean(values * values, axis=1, keepdims=True)
        normed = values * lax.rsqrt(square + NORM_EPS) * gain_ref[...]
        normed_ref[...] = normed.astype(jnp.bfloat16)


def attention(my_index, q_nope, q_rope, keys, w_value, norm_gain):
    tok = q_nope.shape[0]
    total = keys.shape[0]
    key_block = min(KEY_BLOCK, total)
    rows = HEAD_GROUP * tok
    grid_spec = pltpu.PrefetchScalarGridSpec(
        num_scalar_prefetch=1,
        grid=(HEADS // HEAD_GROUP,),
        in_specs=[
            pl.BlockSpec((tok, HEAD_GROUP * LAT), lambda g, i: (0, g)),
            pl.BlockSpec((tok, HEAD_GROUP * ROPE), lambda g, i: (0, g)),
            pl.BlockSpec(keys.shape, lambda g, i: (0, 0)),
            pl.BlockSpec((HEAD_GROUP, LAT, VD), lambda g, i: (g, 0, 0)),
            pl.BlockSpec((1, HEADS * VD), lambda g, i: (0, 0)),
        ],
        out_specs=[
            pl.BlockSpec((tok, HEADS * VD), lambda g, i: (0, 0)),
            pl.BlockSpec((tok, HEADS * VD), lambda g, i: (0, 0)),
        ],
        scratch_shapes=[
            pltpu.VMEM((rows, LAT + 2 * ROPE), jnp.bfloat16),
            pltpu.VMEM((rows, 1), jnp.float32),
            pltpu.VMEM((rows, 1), jnp.float32),
            pltpu.VMEM((rows, LAT), jnp.float32),
        ],
    )
    shape = jax.ShapeDtypeStruct((tok, HEADS * VD), jnp.bfloat16)
    work = HEADS * tok * total
    return pl.pallas_call(
        functools.partial(attention_kernel, tok=tok, key_block=key_block),
        grid_spec=grid_spec,
        out_shape=[shape, shape],
        compiler_params=pltpu.CompilerParams(vmem_limit_bytes=40 << 20),
        cost_estimate=pl.CostEstimate(
            flops=2 * work * (2 * LAT + 2 * ROPE), bytes_accessed=8 << 20, transcendentals=work
        ),
    )(my_index.reshape(1), q_nope, q_rope, keys, w_value, norm_gain.reshape(1, HEADS * VD))


def local(
    q_nope, q_rope, c_kv, k_rope, w_value, norm_gain, expert_ids, gate_fixed, w_gate, w_up, w_down
):
    tok = c_kv.shape[0]
    n_ctx = lax.axis_size("ctx")
    chips = n_ctx // CORES
    my_index = lax.axis_index("ctx")
    my_expert = my_index // SPAN
    same_core = [[chip * CORES + core for chip in range(chips)] for core in range(CORES)]
    siblings = [(i, i ^ 1) for i in range(n_ctx)]

    keys = jnp.concatenate([c_kv, k_rope, k_rope], axis=1)
    keys = lax.all_gather(keys, "ctx", axis=0, tiled=True)
    row_ids = lax.all_gather(expert_ids, "ctx", axis=0, tiled=True, axis_index_groups=same_core)
    other_gate, other_up, other_down = (
        lax.ppermute(w, "ctx", siblings) for w in (w_gate[0], w_up[0], w_down[0])
    )

    values, normed = attention(my_index, q_nope, q_rope, keys, w_value, norm_gain)

    rows = lax.all_gather(normed, "ctx", axis=0, tiled=True, axis_index_groups=same_core)

    def hidden_of(gate_w, up_w):
        gate_act = jnp.dot(rows, gate_w, preferred_element_type=jnp.float32)
        up_act = jnp.dot(rows, up_w, preferred_element_type=jnp.float32)
        act = jax.nn.silu(gate_act) * up_act
        return jnp.where(row_ids == my_expert, act, 0.0).astype(jnp.bfloat16)

    part = jnp.dot(hidden_of(w_gate[0], w_up[0]), w_down[0], preferred_element_type=jnp.float32)
    part = part + jnp.dot(
        hidden_of(other_gate, other_up), other_down, preferred_element_type=jnp.float32
    )
    expert_out = lax.psum_scatter(
        part.astype(jnp.bfloat16), "ctx", scatter_dimension=0, tiled=True,
        axis_index_groups=same_core,
    )
    gate_weight = gate_fixed.astype(jnp.float32) / 65536.0
    mixed = values.astype(jnp.float32) + gate_weight * expert_out.astype(jnp.float32)
    return mixed.astype(jnp.bfloat16)


def solution(mesh):
    in_specs = (
        P(("rep", "ctx"), None),
        P(("rep", "ctx"), None),
        P(("rep", "ctx"), None),
        P(("rep", "ctx"), None),
        P(),
        P(),
        P(("rep", "ctx"), None),
        P(("rep", "ctx"), None),
        P("ctx", None, None),
        P("ctx", None, None),
        P("ctx", None, None),
    )
    out_specs = P(("rep", "ctx"), None)
    return jax.shard_map(local, mesh=mesh, in_specs=in_specs, out_specs=out_specs, check_vma=False)
```

```python
import functools

import jax
import jax.numpy as jnp
from jax import lax
from jax.experimental import pallas as pl
from jax.experimental.pallas import tpu as pltpu
from jax.sharding import PartitionSpec as P

HEADS = 32
LAT = 512
ROPE = 64
VD = 128
SPAN = 8
CORES = 2

SCORE_SCALE = 192.0 ** (-0.5)
NORM_EPS = 1e-06
NEG_FILL = -1e30

HEAD_GROUP = 8
CHIP_BLOCK = 4


def attention_kernel(
    index_ref, q_ref, qr_ref, mine_ref, other_ref, wv_ref, gain_ref, values_ref, normed_ref,
    stack_ref, max_ref, sum_ref, acc_ref, *, tok, chip_block,
):
    group = pl.program_id(0)
    my_index = index_ref[0]
    my_chip, my_core = my_index // CORES, lax.rem(my_index, CORES)
    rows = HEAD_GROUP * tok
    part = chip_block * tok
    lane = lax.broadcasted_iota(jnp.int32, (tok, 2 * ROPE), 1)
    for head in range(HEAD_GROUP):
        at = pl.ds(head * tok, tok)
        stack_ref[at, 0:LAT] = q_ref[:, head * LAT : (head + 1) * LAT]
        pair = qr_ref[:, (head // 2) * 2 * ROPE : (head // 2 + 1) * 2 * ROPE]
        if head % 2:
            pair = jnp.concatenate([pair[:, ROPE:], pair[:, :ROPE]], axis=1)
        stack_ref[at, LAT : LAT + 2 * ROPE] = jnp.where(lane < ROPE, pair, jnp.zeros_like(pair))
    max_ref[...] = jnp.full_like(max_ref, NEG_FILL)
    sum_ref[...] = jnp.zeros_like(sum_ref)
    acc_ref[...] = jnp.zeros_like(acc_ref)
    row_tok = lax.rem(lax.broadcasted_iota(jnp.int32, (rows, part), 0), jnp.int32(tok))
    key_iota = lax.broadcasted_iota(jnp.int32, (rows, part), 1)
    key_chip, key_tok = key_iota // tok, lax.rem(key_iota, jnp.int32(tok))

    def scores_of(keys, core, first_chip):
        scores = lax.dot_general(
            stack_ref[...], keys, (((1,), (1,)), ((), ())), preferred_element_type=jnp.float32
        )
        key_pos = ((key_chip + first_chip) * CORES + core) * tok + key_tok
        return jnp.where(key_pos <= row_tok + my_index * tok, scores * SCORE_SCALE, NEG_FILL)

    def step(block, carry):
        start = pl.multiple_of(block * part, part)
        mine, other = mine_ref[pl.ds(start, part), :], other_ref[pl.ds(start, part), :]
        scores_a = scores_of(mine, my_core, block * chip_block)
        scores_b = scores_of(other, 1 - my_core, block * chip_block)
        old_max = max_ref[...]
        new_max = jnp.maximum(
            old_max, jnp.max(jnp.maximum(scores_a, scores_b), axis=1, keepdims=True)
        )
        weights_a = jnp.exp(scores_a - new_max)
        weights_b = jnp.exp(scores_b - new_max)
        rescale = jnp.exp(old_max - new_max)
        max_ref[...] = new_max
        sum_ref[...] = sum_ref[...] * rescale + jnp.sum(
            weights_a + weights_b, axis=1, keepdims=True
        )
        mixed = jnp.dot(
            weights_a.astype(jnp.bfloat16), mine[:, 0:LAT], preferred_element_type=jnp.float32
        ) + jnp.dot(
            weights_b.astype(jnp.bfloat16), other[:, 0:LAT], preferred_element_type=jnp.float32
        )
        acc_ref[...] = acc_ref[...] * rescale + mixed
        return carry

    lax.fori_loop(0, my_chip // chip_block + 1, step, 0)
    latent = (acc_ref[...] / sum_ref[...]).astype(jnp.bfloat16)
    parts = [
        jnp.dot(
            latent[head * tok : (head + 1) * tok], wv_ref[head], preferred_element_type=jnp.float32
        ).astype(jnp.bfloat16)
        for head in range(HEAD_GROUP)
    ]
    wide = HEAD_GROUP * VD
    values_ref[:, pl.ds(pl.multiple_of(group * wide, wide), wide)] = jnp.concatenate(parts, axis=1)

    @pl.when(group == HEADS // HEAD_GROUP - 1)
    def _():
        values = values_ref[...].astype(jnp.float32)
        square = jnp.mean(values * values, axis=1, keepdims=True)
        normed = values * lax.rsqrt(square + NORM_EPS) * gain_ref[...]
        normed_ref[...] = normed.astype(jnp.bfloat16)


def attention(my_index, q_nope, q_rope, mine, other, w_value, norm_gain):
    tok = q_nope.shape[0]
    total = mine.shape[0]
    chip_block = min(CHIP_BLOCK, total // tok)
    rows = HEAD_GROUP * tok
    grid_spec = pltpu.PrefetchScalarGridSpec(
        num_scalar_prefetch=1,
        grid=(HEADS // HEAD_GROUP,),
        in_specs=[
            pl.BlockSpec((tok, HEAD_GROUP * LAT), lambda g, i: (0, g)),
            pl.BlockSpec((tok, HEAD_GROUP * ROPE), lambda g, i: (0, g)),
            pl.BlockSpec(mine.shape, lambda g, i: (0, 0)),
            pl.BlockSpec(mine.shape, lambda g, i: (0, 0)),
            pl.BlockSpec((HEAD_GROUP, LAT, VD), lambda g, i: (g, 0, 0)),
            pl.BlockSpec((1, HEADS * VD), lambda g, i: (0, 0)),
        ],
        out_specs=[
            pl.BlockSpec((tok, HEADS * VD), lambda g, i: (0, 0)),
            pl.BlockSpec((tok, HEADS * VD), lambda g, i: (0, 0)),
        ],
        scratch_shapes=[
            pltpu.VMEM((rows, LAT + 2 * ROPE), jnp.bfloat16),
            pltpu.VMEM((rows, 1), jnp.float32),
            pltpu.VMEM((rows, 1), jnp.float32),
            pltpu.VMEM((rows, LAT), jnp.float32),
        ],
    )
    shape = jax.ShapeDtypeStruct((tok, HEADS * VD), jnp.bfloat16)
    work = HEADS * tok * total * CORES
    return pl.pallas_call(
        functools.partial(attention_kernel, tok=tok, chip_block=chip_block),
        grid_spec=grid_spec,
        out_shape=[shape, shape],
        compiler_params=pltpu.CompilerParams(vmem_limit_bytes=56 << 20),
        cost_estimate=pl.CostEstimate(
            flops=2 * work * (2 * LAT + 2 * ROPE), bytes_accessed=8 << 20, transcendentals=work
        ),
    )(my_index.reshape(1), q_nope, q_rope, mine, other, w_value, norm_gain.reshape(1, HEADS * VD))


def expert_kernel(up_rows, down_rows, mask, gate_a, gate_b, up_a, up_b, down_a, down_b, out_a, out_b):
    half = up_rows.shape[0]
    rows = jnp.concatenate([up_rows[...], down_rows[...]], axis=0)
    keep = mask[...] > 0.0

    def hidden(gate_ref, up_ref):
        gate_act = jnp.dot(rows, gate_ref[...], preferred_element_type=jnp.float32)
        up_act = jnp.dot(rows, up_ref[...], preferred_element_type=jnp.float32)
        act = gate_act * (1.0 / (1.0 + jnp.exp(-gate_act))) * up_act
        return jnp.where(keep, act, 0.0).astype(jnp.bfloat16)

    hidden_a, hidden_b = hidden(gate_a, up_a), hidden(gate_b, up_b)
    part = jnp.dot(hidden_a, down_a[...], preferred_element_type=jnp.float32)
    part = part + jnp.dot(hidden_b, down_b[...], preferred_element_type=jnp.float32)
    out_a[...] = part[:half]
    out_b[...] = part[half:]


def expert_part(rows_up, rows_down, mask, weights):
    half, features = rows_up.shape
    units = 2 * weights[0].shape[1]
    shape = jax.ShapeDtypeStruct((half, features), jnp.float32)
    return pl.pallas_call(
        expert_kernel,
        in_specs=[pl.BlockSpec(memory_space=pltpu.VMEM)] * 9,
        out_specs=[pl.BlockSpec(memory_space=pltpu.VMEM)] * 2,
        out_shape=[shape, shape],
        compiler_params=pltpu.CompilerParams(vmem_limit_bytes=24 << 20),
        cost_estimate=pl.CostEstimate(
            flops=12 * half * features * units, bytes_accessed=14 << 20, transcendentals=0
        ),
    )(rows_up, rows_down, mask, *weights)


def local(
    q_nope, q_rope, c_kv, k_rope, w_value, norm_gain, expert_ids, gate_fixed, w_gate, w_up, w_down
):
    tok = c_kv.shape[0]
    half = tok // 2
    n_ctx = lax.axis_size("ctx")
    chips = n_ctx // CORES
    my_index = lax.axis_index("ctx")
    my_chip, my_core = my_index // CORES, my_index % CORES
    my_expert = my_index // SPAN
    same_core = [[chip * CORES + core for chip in range(chips)] for core in range(CORES)]
    siblings = [(i, i ^ 1) for i in range(n_ctx)]
    ring = list(range(0, chips, 2)) + list(range(1, chips, 2))[::-1]
    place = [ring.index(chip) for chip in range(chips)]
    ahead = [
        (ring[p] * CORES + core, ring[(p + 1) % chips] * CORES + core)
        for p in range(chips) for core in range(CORES)
    ]
    behind = [(there, here) for here, there in ahead]

    ids = jnp.broadcast_to(expert_ids.astype(jnp.bfloat16), (tok, ROPE))
    block = jnp.concatenate([c_kv, k_rope, ids], axis=1)
    mine = lax.all_gather(block, "ctx", axis=0, tiled=True, axis_index_groups=same_core)
    other = lax.ppermute(mine, "ctx", siblings)

    own, mine, other = lax.optimization_barrier(((w_gate[0], w_up[0], w_down[0]), mine, other))
    swapped = tuple(lax.ppermute(w, "ctx", siblings) for w in own)
    weights = (own[0], swapped[0], own[1], swapped[1], own[2], swapped[2])

    values, normed = attention(my_index, q_nope, q_rope, mine, other, w_value, norm_gain)

    row_ids = mine[:, LAT + ROPE].reshape(chips, tok)
    hits = (row_ids == my_expert.astype(jnp.bfloat16)).astype(jnp.float32)
    my_place = jnp.asarray(place, jnp.int32)[my_chip]
    hops = jnp.arange(chips, dtype=jnp.int32)
    order = jnp.asarray(ring, jnp.int32)
    from_behind = order[(my_place - hops) % chips]
    from_ahead = order[(my_place + hops) % chips]
    masks = jnp.concatenate([hits[from_behind, :half], hits[from_ahead, half:]], axis=1)
    masks = masks[:, :, None]

    rows_up, rows_down = normed[:half], normed[half:]
    home_up, home_down = expert_part(rows_up, rows_down, masks[0], weights)
    sum_up = sum_down = None
    for hop in range(1, chips):
        rows_up = lax.ppermute(rows_up, "ctx", ahead)
        rows_down = lax.ppermute(rows_down, "ctx", behind)
        part_up, part_down = expert_part(rows_up, rows_down, masks[hop], weights)
        if hop > 1:
            part_up = part_up + sum_up.astype(jnp.float32)
            part_down = part_down + sum_down.astype(jnp.float32)
        sum_up = lax.ppermute(part_up.astype(jnp.bfloat16), "ctx", ahead)
        sum_down = lax.ppermute(part_down.astype(jnp.bfloat16), "ctx", behind)
    expert_out = jnp.concatenate(
        [home_up + sum_up.astype(jnp.float32), home_down + sum_down.astype(jnp.float32)], axis=0
    )
    gate_weight = gate_fixed.astype(jnp.float32) / 65536.0
    return (values.astype(jnp.float32) + gate_weight * expert_out).astype(jnp.bfloat16)


def solution(mesh):
    in_specs = (
        P(("rep", "ctx"), None),
        P(("rep", "ctx"), None),
        P(("rep", "ctx"), None),
        P(("rep", "ctx"), None),
        P(),
        P(),
        P(("rep", "ctx"), None),
        P(("rep", "ctx"), None),
        P("ctx", None, None),
        P("ctx", None, None),
        P("ctx", None, None),
    )
    out_specs = P(("rep", "ctx"), None)
    return jax.shard_map(local, mesh=mesh, in_specs=in_specs, out_specs=out_specs, check_vma=False)
```

```python
import functools
import math

import jax
import jax.numpy as jnp
from jax import lax
from jax.experimental import pallas as pl
from jax.experimental.pallas import tpu as pltpu
from jax.sharding import PartitionSpec as P

HEADS = 32
LAT = 512
ROPE = 64
VD = 128
SPAN = 8
CORES = 2

SCORE_SCALE = 192.0 ** (-0.5)
NORM_EPS = 1e-06
NEG_FILL = -1e30

HEAD_GROUP = 8
SUB_HEADS = 4
LOG2_SCALE = SCORE_SCALE * math.log2(math.e)


def attention_kernel(
    index_ref, q_ref, qr_ref, mine_ref, other_ref, wv_ref, gain_ref, values_ref, normed_ref,
    hits_ref, stack_ref, bias_a_ref, bias_b_ref, *, tok,
):
    group = pl.program_id(0)
    my_index = index_ref[0]
    my_chip, my_core = my_index // CORES, lax.rem(my_index, CORES)
    keys = mine_ref.shape[0]

    @pl.when(group == 0)
    def _():
        row_pos = my_index * tok + lax.broadcasted_iota(jnp.int32, (tok, keys), 0)
        key_iota = lax.broadcasted_iota(jnp.int32, (tok, keys), 1)
        key_chip = (key_iota // tok) ^ my_chip
        key_tok = lax.rem(key_iota, jnp.int32(tok))
        for core, bias_ref in ((my_core, bias_a_ref), (1 - my_core, bias_b_ref)):
            key_pos = (key_chip * CORES + core) * tok + key_tok
            bias_ref[...] = jnp.where(key_pos <= row_pos, 0.0, NEG_FILL)
        last = mine_ref[:, LAT : LAT + 2 * ROPE].astype(jnp.float32)
        lane = lax.broadcasted_iota(jnp.int32, last.shape, 1)
        named = jnp.max(jnp.where(lane >= ROPE, last, -1.0), axis=1, keepdims=True)
        my_expert = (my_index // SPAN).astype(jnp.float32)
        hits_ref[...] = jnp.where(named == my_expert, 1.0, 0.0)

    lane = lax.broadcasted_iota(jnp.int32, (tok, 2 * ROPE), 1)
    for head in range(HEAD_GROUP):
        at = pl.ds(head * tok, tok)
        stack_ref[at, 0:LAT] = q_ref[:, head * LAT : (head + 1) * LAT]
        pair = qr_ref[:, (head // 2) * 2 * ROPE : (head // 2 + 1) * 2 * ROPE]
        if head % 2:
            pair = jnp.concatenate([pair[:, ROPE:], pair[:, :ROPE]], axis=1)
        stack_ref[at, LAT : LAT + 2 * ROPE] = jnp.where(lane < ROPE, pair, jnp.zeros_like(pair))

    rows = SUB_HEADS * tok
    parts = []
    for sub in range(HEAD_GROUP // SUB_HEADS):
        queries = stack_ref[sub * rows : (sub + 1) * rows, :]

        def scores_of(keys_ref, bias_ref):
            scores = lax.dot_general(
                queries, keys_ref[...], (((1,), (1,)), ((), ())),
                preferred_element_type=jnp.float32,
            )
            return scores.reshape(SUB_HEADS, tok, keys) * LOG2_SCALE + bias_ref[...][None]

        scores_a = scores_of(mine_ref, bias_a_ref)
        scores_b = scores_of(other_ref, bias_b_ref)
        top = jnp.max(jnp.maximum(scores_a, scores_b), axis=2, keepdims=True)
        weights_a = jnp.exp2(scores_a - top)
        weights_b = jnp.exp2(scores_b - top)
        total = jnp.sum(weights_a + weights_b, axis=2, keepdims=True)
        mixed = jnp.dot(
            weights_a.astype(jnp.bfloat16).reshape(rows, keys), mine_ref[:, 0:LAT],
            preferred_element_type=jnp.float32,
        ) + jnp.dot(
            weights_b.astype(jnp.bfloat16).reshape(rows, keys), other_ref[:, 0:LAT],
            preferred_element_type=jnp.float32,
        )
        latent = (mixed.reshape(SUB_HEADS, tok, LAT) / total).astype(jnp.bfloat16)
        for head in range(SUB_HEADS):
            value = jnp.dot(
                latent[head], wv_ref[sub * SUB_HEADS + head], preferred_element_type=jnp.float32
            )
            parts.append(value.astype(jnp.bfloat16))
    wide = HEAD_GROUP * VD
    values_ref[:, pl.ds(pl.multiple_of(group * wide, wide), wide)] = jnp.concatenate(parts, axis=1)

    @pl.when(group == HEADS // HEAD_GROUP - 1)
    def _():
        values = values_ref[...].astype(jnp.float32)
        square = jnp.mean(values * values, axis=1, keepdims=True)
        normed = values * lax.rsqrt(square + NORM_EPS) * gain_ref[...]
        normed_ref[...] = normed.astype(jnp.bfloat16)


def attention(my_index, q_nope, q_rope, mine, other, w_value, norm_gain):
    tok = q_nope.shape[0]
    total = mine.shape[0]
    rows = HEAD_GROUP * tok
    grid_spec = pltpu.PrefetchScalarGridSpec(
        num_scalar_prefetch=1,
        grid=(HEADS // HEAD_GROUP,),
        in_specs=[
            pl.BlockSpec((tok, HEAD_GROUP * LAT), lambda g, i: (0, g)),
            pl.BlockSpec((tok, HEAD_GROUP * ROPE), lambda g, i: (0, g)),
            pl.BlockSpec(mine.shape, lambda g, i: (0, 0)),
            pl.BlockSpec(mine.shape, lambda g, i: (0, 0)),
            pl.BlockSpec((HEAD_GROUP, LAT, VD), lambda g, i: (g, 0, 0)),
            pl.BlockSpec((1, HEADS * VD), lambda g, i: (0, 0)),
        ],
        out_specs=[
            pl.BlockSpec((tok, HEADS * VD), lambda g, i: (0, 0)),
            pl.BlockSpec((tok, HEADS * VD), lambda g, i: (0, 0)),
            pl.BlockSpec((total, 1), lambda g, i: (0, 0)),
        ],
        scratch_shapes=[
            pltpu.VMEM((rows, LAT + 2 * ROPE), jnp.bfloat16),
            pltpu.VMEM((tok, total), jnp.float32),
            pltpu.VMEM((tok, total), jnp.float32),
        ],
    )
    shape = jax.ShapeDtypeStruct((tok, HEADS * VD), jnp.bfloat16)
    work = HEADS * tok * total * CORES
    return pl.pallas_call(
        functools.partial(attention_kernel, tok=tok),
        grid_spec=grid_spec,
        out_shape=[shape, shape, jax.ShapeDtypeStruct((total, 1), jnp.float32)],
        compiler_params=pltpu.CompilerParams(vmem_limit_bytes=56 << 20),
        cost_estimate=pl.CostEstimate(
            flops=2 * work * (2 * LAT + 2 * ROPE), bytes_accessed=8 << 20, transcendentals=work
        ),
    )(my_index.reshape(1), q_nope, q_rope, mine, other, w_value, norm_gain.reshape(1, HEADS * VD))


def ring_place(chip, chips):
    return jnp.where(chip % 2 == 0, chip // 2, chips - 1 - chip // 2)


def ring_chip(place, chips):
    return jnp.where(place < chips // 2, 2 * place, 2 * (chips - 1 - place) + 1)


def expert_kernel(
    index_ref, up_rows, down_rows, hits_ref, gate_a, gate_b, up_a, up_b, down_a, down_b, out_a,
    out_b, *, hop, chips,
):
    half = up_rows.shape[0]
    my_chip = index_ref[0] // CORES
    place = ring_place(my_chip, chips)
    from_behind = ring_chip(lax.rem(place - hop + chips, chips), chips) ^ my_chip
    from_ahead = ring_chip(lax.rem(place + hop, chips), chips) ^ my_chip
    tok = 2 * half
    keep = jnp.concatenate(
        [
            hits_ref[pl.ds(pl.multiple_of(from_behind * tok, half), half), :],
            hits_ref[pl.ds(pl.multiple_of(from_ahead * tok + half, half), half), :],
        ],
        axis=0,
    ) > 0.0
    rows = jnp.concatenate([up_rows[...], down_rows[...]], axis=0)

    def hidden(gate_ref, up_ref):
        gate_act = jnp.dot(rows, gate_ref[...], preferred_element_type=jnp.float32)
        up_act = jnp.dot(rows, up_ref[...], preferred_element_type=jnp.float32)
        act = gate_act * (1.0 / (1.0 + jnp.exp(-gate_act))) * up_act
        return jnp.where(keep, act, 0.0).astype(jnp.bfloat16)

    hidden_a, hidden_b = hidden(gate_a, up_a), hidden(gate_b, up_b)
    part = jnp.dot(hidden_a, down_a[...], preferred_element_type=jnp.float32)
    part = part + jnp.dot(hidden_b, down_b[...], preferred_element_type=jnp.float32)
    out_a[...] = part[:half]
    out_b[...] = part[half:]


def expert_part(my_index, rows_up, rows_down, hits, weights, hop, chips):
    half, features = rows_up.shape
    units = 2 * weights[0].shape[1]
    shape = jax.ShapeDtypeStruct((half, features), jnp.float32)
    return pl.pallas_call(
        functools.partial(expert_kernel, hop=hop, chips=chips),
        in_specs=[pl.BlockSpec(memory_space=pltpu.SMEM)]
        + [pl.BlockSpec(memory_space=pltpu.VMEM)] * 9,
        out_specs=[pl.BlockSpec(memory_space=pltpu.VMEM)] * 2,
        out_shape=[shape, shape],
        compiler_params=pltpu.CompilerParams(vmem_limit_bytes=24 << 20),
        cost_estimate=pl.CostEstimate(
            flops=12 * half * features * units, bytes_accessed=14 << 20, transcendentals=0
        ),
    )(my_index.reshape(1), rows_up, rows_down, hits, *weights)


def local(
    q_nope, q_rope, c_kv, k_rope, w_value, norm_gain, expert_ids, gate_fixed, w_gate, w_up, w_down
):
    tok = c_kv.shape[0]
    half = tok // 2
    n_ctx = lax.axis_size("ctx")
    chips = n_ctx // CORES
    my_index = lax.axis_index("ctx")
    siblings = [(i, i ^ 1) for i in range(n_ctx)]
    ring = list(range(0, chips, 2)) + list(range(1, chips, 2))[::-1]
    ahead = [
        (ring[p] * CORES + core, ring[(p + 1) % chips] * CORES + core)
        for p in range(chips) for core in range(CORES)
    ]
    behind = [(there, here) for here, there in ahead]

    def from_chip(block, step):
        return lax.ppermute(block, "ctx", [(i, i ^ (step * CORES)) for i in range(n_ctx)])

    ids = jnp.broadcast_to(expert_ids.astype(jnp.bfloat16), (tok, ROPE))
    block = jnp.concatenate([c_kv, k_rope, ids], axis=1)
    across = from_chip(block, chips // 2)
    near = [block] + [from_chip(block, step) for step in range(1, chips // 2)]
    far = [across] + [from_chip(across, step) for step in range(1, chips // 2)]
    mine = jnp.concatenate(near + far, axis=0)
    other = lax.ppermute(mine, "ctx", siblings)

    own, mine, other = lax.optimization_barrier(((w_gate[0], w_up[0], w_down[0]), mine, other))
    swapped = tuple(lax.ppermute(w, "ctx", siblings) for w in own)
    values, normed, hits = attention(my_index, q_nope, q_rope, mine, other, w_value, norm_gain)
    normed, swapped = lax.optimization_barrier((normed, swapped))
    weights = (own[0], swapped[0], own[1], swapped[1], own[2], swapped[2])

    def part_of(rows, hop):
        return expert_part(my_index, rows[0], rows[1], hits, weights, hop, chips)

    def move(pair):
        return (lax.ppermute(pair[0], "ctx", ahead), lax.ppermute(pair[1], "ctx", behind))

    def rounded(pair):
        return tuple(x.astype(jnp.bfloat16) for x in pair)

    start = (normed[:half], normed[half:])
    rows = move(start)
    home = part_of(start, 0)
    rows, home = lax.optimization_barrier((rows, home))
    later = move(rows) if chips > 2 else None
    sums = rounded(part_of(rows, 1))
    for hop in range(1, chips):
        rows = later
        if hop + 2 < chips:
            rows, sums = lax.optimization_barrier((rows, sums))
            later = move(rows)
        arrived = move(sums)
        if hop + 1 < chips:
            part = part_of(rows, hop + 1)
            sums = rounded(tuple(p + a.astype(jnp.float32) for p, a in zip(part, arrived)))
    expert_out = jnp.concatenate(
        [h + a.astype(jnp.float32) for h, a in zip(home, arrived)], axis=0
    )
    gate_weight = gate_fixed.astype(jnp.float32) / 65536.0
    return (values.astype(jnp.float32) + gate_weight * expert_out).astype(jnp.bfloat16)


def solution(mesh):
    in_specs = (
        P(("rep", "ctx"), None),
        P(("rep", "ctx"), None),
        P(("rep", "ctx"), None),
        P(("rep", "ctx"), None),
        P(),
        P(),
        P(("rep", "ctx"), None),
        P(("rep", "ctx"), None),
        P("ctx", None, None),
        P("ctx", None, None),
        P("ctx", None, None),
    )
    out_specs = P(("rep", "ctx"), None)
    return jax.shard_map(local, mesh=mesh, in_specs=in_specs, out_specs=out_specs, check_vma=False)
```

```python
import functools
import math

import jax
import jax.numpy as jnp
from jax import lax
from jax.experimental import pallas as pl
from jax.experimental.pallas import tpu as pltpu
from jax.sharding import PartitionSpec as P

HEADS = 32
LAT = 512
ROPE = 64
VD = 128
SPAN = 8
CORES = 2

SCORE_SCALE = 192.0 ** (-0.5)
NORM_EPS = 1e-06
NEG_FILL = -1e30

HEAD_GROUP = 8
SUB_HEADS = 4
LOG2_SCALE = SCORE_SCALE * math.log2(math.e)


def attention_kernel(
    index_ref, q_ref, qr_ref, mine_ref, other_ref, wv_ref, gain_ref, values_ref, up_ref,
    down_ref, hits_ref, stack_ref, bias_a_ref, bias_b_ref, *, tok,
):
    group = pl.program_id(0)
    my_index = index_ref[0]
    my_chip, my_core = my_index // CORES, lax.rem(my_index, CORES)
    keys = mine_ref.shape[0]

    @pl.when(group == 0)
    def _():
        row_pos = my_index * tok + lax.broadcasted_iota(jnp.int32, (tok, keys), 0)
        key_iota = lax.broadcasted_iota(jnp.int32, (tok, keys), 1)
        key_chip = (key_iota // tok) ^ my_chip
        key_tok = lax.rem(key_iota, jnp.int32(tok))
        for core, bias_ref in ((my_core, bias_a_ref), (1 - my_core, bias_b_ref)):
            key_pos = (key_chip * CORES + core) * tok + key_tok
            bias_ref[...] = jnp.where(key_pos <= row_pos, 0.0, NEG_FILL)
        last = mine_ref[:, LAT : LAT + 2 * ROPE].astype(jnp.float32)
        lane = lax.broadcasted_iota(jnp.int32, last.shape, 1)
        named = jnp.max(jnp.where(lane >= ROPE, last, -1.0), axis=1, keepdims=True)
        my_expert = (my_index // SPAN).astype(jnp.float32)
        hits_ref[...] = jnp.where(named == my_expert, 1.0, 0.0)

    lane = lax.broadcasted_iota(jnp.int32, (tok, 2 * ROPE), 1)
    for head in range(HEAD_GROUP):
        at = pl.ds(head * tok, tok)
        stack_ref[at, 0:LAT] = q_ref[:, head * LAT : (head + 1) * LAT]
        pair = qr_ref[:, (head // 2) * 2 * ROPE : (head // 2 + 1) * 2 * ROPE]
        if head % 2:
            pair = jnp.concatenate([pair[:, ROPE:], pair[:, :ROPE]], axis=1)
        stack_ref[at, LAT : LAT + 2 * ROPE] = jnp.where(lane < ROPE, pair, jnp.zeros_like(pair))

    rows = SUB_HEADS * tok
    parts = []
    for sub in range(HEAD_GROUP // SUB_HEADS):
        queries = stack_ref[sub * rows : (sub + 1) * rows, :]

        def scores_of(keys_ref, bias_ref):
            scores = lax.dot_general(
                queries, keys_ref[...], (((1,), (1,)), ((), ())),
                preferred_element_type=jnp.float32,
            )
            return scores.reshape(SUB_HEADS, tok, keys) * LOG2_SCALE + bias_ref[...][None]

        scores_a = scores_of(mine_ref, bias_a_ref)
        scores_b = scores_of(other_ref, bias_b_ref)
        top = jnp.max(jnp.maximum(scores_a, scores_b), axis=2, keepdims=True)
        weights_a = jnp.exp2(scores_a - top)
        weights_b = jnp.exp2(scores_b - top)
        total = jnp.sum(weights_a + weights_b, axis=2, keepdims=True)
        mixed = jnp.dot(
            weights_a.astype(jnp.bfloat16).reshape(rows, keys), mine_ref[:, 0:LAT],
            preferred_element_type=jnp.float32,
        ) + jnp.dot(
            weights_b.astype(jnp.bfloat16).reshape(rows, keys), other_ref[:, 0:LAT],
            preferred_element_type=jnp.float32,
        )
        latent = (mixed.reshape(SUB_HEADS, tok, LAT) / total).astype(jnp.bfloat16)
        for head in range(SUB_HEADS):
            value = jnp.dot(
                latent[head], wv_ref[sub * SUB_HEADS + head], preferred_element_type=jnp.float32
            )
            parts.append(value.astype(jnp.bfloat16))
    wide = HEAD_GROUP * VD
    values_ref[:, pl.ds(pl.multiple_of(group * wide, wide), wide)] = jnp.concatenate(parts, axis=1)

    @pl.when(group == HEADS // HEAD_GROUP - 1)
    def _():
        values = values_ref[...].astype(jnp.float32)
        square = jnp.mean(values * values, axis=1, keepdims=True)
        normed = values * lax.rsqrt(square + NORM_EPS) * gain_ref[...]
        normed = normed.astype(jnp.bfloat16)
        up_ref[...] = normed[: tok // 2]
        down_ref[...] = normed[tok // 2 :]


def attention(my_index, q_nope, q_rope, mine, other, w_value, norm_gain):
    tok = q_nope.shape[0]
    total = mine.shape[0]
    rows = HEAD_GROUP * tok
    grid_spec = pltpu.PrefetchScalarGridSpec(
        num_scalar_prefetch=1,
        grid=(HEADS // HEAD_GROUP,),
        in_specs=[
            pl.BlockSpec((tok, HEAD_GROUP * LAT), lambda g, i: (0, g)),
            pl.BlockSpec((tok, HEAD_GROUP * ROPE), lambda g, i: (0, g)),
            pl.BlockSpec(mine.shape, lambda g, i: (0, 0)),
            pl.BlockSpec(mine.shape, lambda g, i: (0, 0)),
            pl.BlockSpec((HEAD_GROUP, LAT, VD), lambda g, i: (g, 0, 0)),
            pl.BlockSpec((1, HEADS * VD), lambda g, i: (0, 0)),
        ],
        out_specs=[
            pl.BlockSpec((tok, HEADS * VD), lambda g, i: (0, 0)),
            pl.BlockSpec((tok // 2, HEADS * VD), lambda g, i: (0, 0)),
            pl.BlockSpec((tok // 2, HEADS * VD), lambda g, i: (0, 0)),
            pl.BlockSpec((total, 1), lambda g, i: (0, 0)),
        ],
        scratch_shapes=[
            pltpu.VMEM((rows, LAT + 2 * ROPE), jnp.bfloat16),
            pltpu.VMEM((tok, total), jnp.float32),
            pltpu.VMEM((tok, total), jnp.float32),
        ],
    )
    shape = jax.ShapeDtypeStruct((tok, HEADS * VD), jnp.bfloat16)
    half_shape = jax.ShapeDtypeStruct((tok // 2, HEADS * VD), jnp.bfloat16)
    hits_shape = jax.ShapeDtypeStruct((total, 1), jnp.float32)
    work = HEADS * tok * total * CORES
    return pl.pallas_call(
        functools.partial(attention_kernel, tok=tok),
        grid_spec=grid_spec,
        out_shape=[shape, half_shape, half_shape, hits_shape],
        compiler_params=pltpu.CompilerParams(vmem_limit_bytes=56 << 20),
        cost_estimate=pl.CostEstimate(
            flops=2 * work * (2 * LAT + 2 * ROPE), bytes_accessed=8 << 20, transcendentals=work
        ),
    )(my_index.reshape(1), q_nope, q_rope, mine, other, w_value, norm_gain.reshape(1, HEADS * VD))


def ring_place(chip, chips):
    return jnp.where(chip % 2 == 0, chip // 2, chips - 1 - chip // 2)


def ring_chip(place, chips):
    return jnp.where(place < chips // 2, 2 * place, 2 * (chips - 1 - place) + 1)


def expert_kernel(
    index_ref, up_rows, down_rows, hits_ref, gate_a, gate_b, up_a, up_b, down_a, down_b, out_a,
    out_b, *, hop, chips,
):
    half = up_rows.shape[0]
    my_chip = index_ref[0] // CORES
    place = ring_place(my_chip, chips)
    from_behind = ring_chip(lax.rem(place - hop + chips, chips), chips) ^ my_chip
    from_ahead = ring_chip(lax.rem(place + hop, chips), chips) ^ my_chip
    tok = 2 * half
    keep = jnp.concatenate(
        [
            hits_ref[pl.ds(pl.multiple_of(from_behind * tok, half), half), :],
            hits_ref[pl.ds(pl.multiple_of(from_ahead * tok + half, half), half), :],
        ],
        axis=0,
    ) > 0.0
    rows = jnp.concatenate([up_rows[...], down_rows[...]], axis=0)

    def hidden(gate_ref, up_ref):
        gate_act = jnp.dot(rows, gate_ref[...], preferred_element_type=jnp.float32)
        up_act = jnp.dot(rows, up_ref[...], preferred_element_type=jnp.float32)
        act = gate_act * (1.0 / (1.0 + jnp.exp(-gate_act))) * up_act
        return jnp.where(keep, act, 0.0).astype(jnp.bfloat16)

    hidden_a, hidden_b = hidden(gate_a, up_a), hidden(gate_b, up_b)
    part = jnp.dot(hidden_a, down_a[...], preferred_element_type=jnp.float32)
    part = part + jnp.dot(hidden_b, down_b[...], preferred_element_type=jnp.float32)
    out_a[...] = part[:half]
    out_b[...] = part[half:]


def expert_part(my_index, rows_up, rows_down, hits, weights, hop, chips):
    half, features = rows_up.shape
    units = 2 * weights[0].shape[1]
    shape = jax.ShapeDtypeStruct((half, features), jnp.float32)
    return pl.pallas_call(
        functools.partial(expert_kernel, hop=hop, chips=chips),
        in_specs=[pl.BlockSpec(memory_space=pltpu.SMEM)]
        + [pl.BlockSpec(memory_space=pltpu.VMEM)] * 9,
        out_specs=[pl.BlockSpec(memory_space=pltpu.VMEM)] * 2,
        out_shape=[shape, shape],
        compiler_params=pltpu.CompilerParams(vmem_limit_bytes=24 << 20),
        cost_estimate=pl.CostEstimate(
            flops=12 * half * features * units, bytes_accessed=14 << 20, transcendentals=0
        ),
    )(my_index.reshape(1), rows_up, rows_down, hits, *weights)


def local(
    q_nope, q_rope, c_kv, k_rope, w_value, norm_gain, expert_ids, gate_fixed, w_gate, w_up, w_down
):
    tok = c_kv.shape[0]
    n_ctx = lax.axis_size("ctx")
    chips = n_ctx // CORES
    my_index = lax.axis_index("ctx")
    siblings = [(i, i ^ 1) for i in range(n_ctx)]
    ring = list(range(0, chips, 2)) + list(range(1, chips, 2))[::-1]
    ahead = [
        (ring[p] * CORES + core, ring[(p + 1) % chips] * CORES + core)
        for p in range(chips) for core in range(CORES)
    ]
    behind = [(there, here) for here, there in ahead]

    def from_chip(block, step):
        return lax.ppermute(block, "ctx", [(i, i ^ (step * CORES)) for i in range(n_ctx)])

    ids = jnp.broadcast_to(expert_ids.astype(jnp.bfloat16), (tok, ROPE))
    block = jnp.concatenate([c_kv, k_rope, ids], axis=1)
    across = from_chip(block, chips // 2)
    near = [block] + [from_chip(block, step) for step in range(1, chips // 2)]
    far = [across] + [from_chip(across, step) for step in range(1, chips // 2)]
    mine = jnp.concatenate(near + far, axis=0)
    other = lax.ppermute(mine, "ctx", siblings)

    own, mine, other = lax.optimization_barrier(((w_gate[0], w_up[0], w_down[0]), mine, other))
    swapped = tuple(lax.ppermute(w, "ctx", siblings) for w in own)
    values, start_up, start_down, hits = attention(
        my_index, q_nope, q_rope, mine, other, w_value, norm_gain
    )
    start, swapped = lax.optimization_barrier(((start_up, start_down), swapped))
    weights = (own[0], swapped[0], own[1], swapped[1], own[2], swapped[2])

    def part_of(rows, hop):
        return expert_part(my_index, rows[0], rows[1], hits, weights, hop, chips)

    def move(pair):
        return (lax.ppermute(pair[0], "ctx", ahead), lax.ppermute(pair[1], "ctx", behind))

    def rounded(pair):
        return tuple(x.astype(jnp.bfloat16) for x in pair)

    def after(pair, first):
        return lax.optimization_barrier((pair, first))[0]

    rows = move(start)
    later = move(rows) if chips > 2 else None
    sums = rounded(part_of(rows, 1))
    for hop in range(1, chips):
        arrived = move(sums)
        rows = later
        if hop + 2 < chips:
            later = move(after(rows, sums))
        if hop + 1 < chips:
            part = part_of(rows, hop + 1)
            sums = rounded(tuple(p + a.astype(jnp.float32) for p, a in zip(part, arrived)))
    home = part_of(after(start, sums), 0)
    expert_out = jnp.concatenate(
        [h + a.astype(jnp.float32) for h, a in zip(home, arrived)], axis=0
    )
    gate_weight = gate_fixed.astype(jnp.float32) / 65536.0
    return (values.astype(jnp.float32) + gate_weight * expert_out).astype(jnp.bfloat16)


def solution(mesh):
    in_specs = (
        P(("rep", "ctx"), None),
        P(("rep", "ctx"), None),
        P(("rep", "ctx"), None),
        P(("rep", "ctx"), None),
        P(),
        P(),
        P(("rep", "ctx"), None),
        P(("rep", "ctx"), None),
        P("ctx", None, None),
        P("ctx", None, None),
        P("ctx", None, None),
    )
    out_specs = P(("rep", "ctx"), None)
    return jax.shard_map(local, mesh=mesh, in_specs=in_specs, out_specs=out_specs, check_vma=False)
```

```python
import functools
import math

import jax
import jax.numpy as jnp
from jax import lax
from jax.experimental import pallas as pl
from jax.experimental.pallas import tpu as pltpu
from jax.sharding import PartitionSpec as P

HEADS = 32
LAT = 512
ROPE = 64
VD = 128
SPAN = 8
CORES = 2

SCORE_SCALE = 192.0 ** (-0.5)
NORM_EPS = 1e-06
NEG_FILL = -1e30

HEAD_GROUP = 8
SUB_HEADS = 4
LOG2_SCALE = SCORE_SCALE * math.log2(math.e)


def attention_kernel(
    index_ref, q_ref, qr_ref, mine_ref, other_ref, wv_ref, gain_ref, values_ref, normed_ref,
    hits_ref, stack_ref, bias_a_ref, bias_b_ref, *, tok,
):
    group = pl.program_id(0)
    my_index = index_ref[0]
    my_chip, my_core = my_index // CORES, lax.rem(my_index, CORES)
    keys = mine_ref.shape[0]

    @pl.when(group == 0)
    def _():
        row_pos = my_index * tok + lax.broadcasted_iota(jnp.int32, (tok, keys), 0)
        key_iota = lax.broadcasted_iota(jnp.int32, (tok, keys), 1)
        key_chip = (key_iota // tok) ^ my_chip
        key_tok = lax.rem(key_iota, jnp.int32(tok))
        for core, bias_ref in ((my_core, bias_a_ref), (1 - my_core, bias_b_ref)):
            key_pos = (key_chip * CORES + core) * tok + key_tok
            bias_ref[...] = jnp.where(key_pos <= row_pos, 0.0, NEG_FILL)
        last = mine_ref[:, LAT : LAT + 2 * ROPE].astype(jnp.float32)
        lane = lax.broadcasted_iota(jnp.int32, last.shape, 1)
        named = jnp.max(jnp.where(lane >= ROPE, last, -1.0), axis=1, keepdims=True)
        my_expert = (my_index // SPAN).astype(jnp.float32)
        hits_ref[...] = jnp.where(named == my_expert, 1.0, 0.0)

    lane = lax.broadcasted_iota(jnp.int32, (tok, 2 * ROPE), 1)
    for head in range(HEAD_GROUP):
        at = pl.ds(head * tok, tok)
        stack_ref[at, 0:LAT] = q_ref[:, head * LAT : (head + 1) * LAT]
        pair = qr_ref[:, (head // 2) * 2 * ROPE : (head // 2 + 1) * 2 * ROPE]
        if head % 2:
            pair = jnp.concatenate([pair[:, ROPE:], pair[:, :ROPE]], axis=1)
        stack_ref[at, LAT : LAT + 2 * ROPE] = jnp.where(lane < ROPE, pair, jnp.zeros_like(pair))

    rows = SUB_HEADS * tok
    parts = []
    for sub in range(HEAD_GROUP // SUB_HEADS):
        queries = stack_ref[sub * rows : (sub + 1) * rows, :]

        def scores_of(keys_ref, bias_ref):
            scores = lax.dot_general(
                queries, keys_ref[...], (((1,), (1,)), ((), ())),
                preferred_element_type=jnp.float32,
            )
            return scores.reshape(SUB_HEADS, tok, keys) * LOG2_SCALE + bias_ref[...][None]

        scores_a = scores_of(mine_ref, bias_a_ref)
        scores_b = scores_of(other_ref, bias_b_ref)
        top = jnp.max(jnp.maximum(scores_a, scores_b), axis=2, keepdims=True)
        weights_a = jnp.exp2(scores_a - top)
        weights_b = jnp.exp2(scores_b - top)
        total = jnp.sum(weights_a + weights_b, axis=2, keepdims=True)
        mixed = jnp.dot(
            weights_a.astype(jnp.bfloat16).reshape(rows, keys), mine_ref[:, 0:LAT],
            preferred_element_type=jnp.float32,
        ) + jnp.dot(
            weights_b.astype(jnp.bfloat16).reshape(rows, keys), other_ref[:, 0:LAT],
            preferred_element_type=jnp.float32,
        )
        latent = (mixed.reshape(SUB_HEADS, tok, LAT) / total).astype(jnp.bfloat16)
        for head in range(SUB_HEADS):
            value = jnp.dot(
                latent[head], wv_ref[sub * SUB_HEADS + head], preferred_element_type=jnp.float32
            )
            parts.append(value.astype(jnp.bfloat16))
    wide = HEAD_GROUP * VD
    values_ref[:, pl.ds(pl.multiple_of(group * wide, wide), wide)] = jnp.concatenate(parts, axis=1)

    @pl.when(group == HEADS // HEAD_GROUP - 1)
    def _():
        values = values_ref[...].astype(jnp.float32)
        square = jnp.mean(values * values, axis=1, keepdims=True)
        normed = values * lax.rsqrt(square + NORM_EPS) * gain_ref[...]
        normed_ref[...] = normed.astype(jnp.bfloat16)


def attention(my_index, q_nope, q_rope, mine, other, w_value, norm_gain):
    tok = q_nope.shape[0]
    total = mine.shape[0]
    rows = HEAD_GROUP * tok
    grid_spec = pltpu.PrefetchScalarGridSpec(
        num_scalar_prefetch=1,
        grid=(HEADS // HEAD_GROUP,),
        in_specs=[
            pl.BlockSpec((tok, HEAD_GROUP * LAT), lambda g, i: (0, g)),
            pl.BlockSpec((tok, HEAD_GROUP * ROPE), lambda g, i: (0, g)),
            pl.BlockSpec(mine.shape, lambda g, i: (0, 0)),
            pl.BlockSpec(mine.shape, lambda g, i: (0, 0)),
            pl.BlockSpec((HEAD_GROUP, LAT, VD), lambda g, i: (g, 0, 0)),
            pl.BlockSpec((1, HEADS * VD), lambda g, i: (0, 0)),
        ],
        out_specs=[
            pl.BlockSpec((tok, HEADS * VD), lambda g, i: (0, 0)),
            pl.BlockSpec((tok, HEADS * VD), lambda g, i: (0, 0)),
            pl.BlockSpec((total, 1), lambda g, i: (0, 0)),
        ],
        scratch_shapes=[
            pltpu.VMEM((rows, LAT + 2 * ROPE), jnp.bfloat16),
            pltpu.VMEM((tok, total), jnp.float32),
            pltpu.VMEM((tok, total), jnp.float32),
        ],
    )
    shape = jax.ShapeDtypeStruct((tok, HEADS * VD), jnp.bfloat16)
    hits_shape = jax.ShapeDtypeStruct((total, 1), jnp.float32)
    work = HEADS * tok * total * CORES
    return pl.pallas_call(
        functools.partial(attention_kernel, tok=tok),
        grid_spec=grid_spec,
        out_shape=[shape, shape, hits_shape],
        compiler_params=pltpu.CompilerParams(vmem_limit_bytes=56 << 20),
        cost_estimate=pl.CostEstimate(
            flops=2 * work * (2 * LAT + 2 * ROPE), bytes_accessed=8 << 20, transcendentals=work
        ),
    )(my_index.reshape(1), q_nope, q_rope, mine, other, w_value, norm_gain.reshape(1, HEADS * VD))


def ring_place(chip, chips):
    return jnp.where(chip % 2 == 0, chip // 2, chips - 1 - chip // 2)


def ring_chip(place, chips):
    return jnp.where(place < chips // 2, 2 * place, 2 * (chips - 1 - place) + 1)


def expert_kernel(
    index_ref, rows_ref, hits_ref, gate_a, up_a, down_a, gate_hbm, up_hbm, down_hbm, out_ref,
    gate_b, up_b, down_b, sems, *, hop, chips,
):
    copies = [
        pltpu.make_async_copy(there, here, sems.at[i])
        for i, (there, here) in enumerate(((gate_hbm, gate_b), (up_hbm, up_b), (down_hbm, down_b)))
    ]
    for copy in copies:
        copy.start()
    tok = rows_ref.shape[0]
    my_chip, my_core = index_ref[0] // CORES, lax.rem(index_ref[0], CORES)
    place = ring_place(my_chip, chips) + chips + hop * (2 * my_core - 1)
    source = ring_chip(lax.rem(place, chips), chips) ^ my_chip
    keep = hits_ref[pl.ds(pl.multiple_of(source * tok, tok), tok), :] > 0.0
    rows = rows_ref[...]

    def hidden(gate_ref, up_ref):
        gate_act = jnp.dot(rows, gate_ref[...], preferred_element_type=jnp.float32)
        up_act = jnp.dot(rows, up_ref[...], preferred_element_type=jnp.float32)
        act = gate_act * (1.0 / (1.0 + jnp.exp(-gate_act))) * up_act
        return jnp.where(keep, act, 0.0).astype(jnp.bfloat16)

    part = jnp.dot(hidden(gate_a, up_a), down_a[...], preferred_element_type=jnp.float32)
    copies[0].wait()
    copies[1].wait()
    hidden_b = hidden(gate_b, up_b)
    copies[2].wait()
    out_ref[...] = part + jnp.dot(hidden_b, down_b[...], preferred_element_type=jnp.float32)


def expert_part(my_index, rows, hits, own, swapped, hop, chips):
    tok, features = rows.shape
    units = 2 * own[0].shape[1]
    vmem, anywhere = pl.BlockSpec(memory_space=pltpu.VMEM), pl.BlockSpec(memory_space=pl.ANY)
    return pl.pallas_call(
        functools.partial(expert_kernel, hop=hop, chips=chips),
        in_specs=[pl.BlockSpec(memory_space=pltpu.SMEM)] + [vmem] * 5 + [anywhere] * 3,
        out_specs=vmem,
        out_shape=jax.ShapeDtypeStruct((tok, features), jnp.float32),
        scratch_shapes=[pltpu.VMEM(w.shape, w.dtype) for w in swapped]
        + [pltpu.SemaphoreType.DMA((3,))],
        compiler_params=pltpu.CompilerParams(vmem_limit_bytes=24 << 20),
        cost_estimate=pl.CostEstimate(
            flops=6 * tok * features * units, bytes_accessed=14 << 20, transcendentals=0
        ),
    )(my_index.reshape(1), rows, hits, *own, *swapped)


def local(
    q_nope, q_rope, c_kv, k_rope, w_value, norm_gain, expert_ids, gate_fixed, w_gate, w_up, w_down
):
    tok = c_kv.shape[0]
    n_ctx = lax.axis_size("ctx")
    chips = n_ctx // CORES
    my_index = lax.axis_index("ctx")
    siblings = [(i, i ^ 1) for i in range(n_ctx)]
    ring = list(range(0, chips, 2)) + list(range(1, chips, 2))[::-1]
    route = [
        (ring[p] * CORES + core, ring[(p + 1 - 2 * core) % chips] * CORES + core)
        for p in range(chips) for core in range(CORES)
    ]

    def from_chip(block, step):
        return lax.ppermute(block, "ctx", [(i, i ^ (step * CORES)) for i in range(n_ctx)])

    ids = jnp.broadcast_to(expert_ids.astype(jnp.bfloat16), (tok, ROPE))
    block = jnp.concatenate([c_kv, k_rope, ids], axis=1)
    across = from_chip(block, chips // 2)
    near = [block] + [from_chip(block, step) for step in range(1, chips // 2)]
    far = [across] + [from_chip(across, step) for step in range(1, chips // 2)]
    mine = jnp.concatenate(near + far, axis=0)
    other = lax.ppermute(mine, "ctx", siblings)

    own, mine, other = lax.optimization_barrier(((w_gate[0], w_up[0], w_down[0]), mine, other))
    swapped = tuple(lax.ppermute(w, "ctx", siblings) for w in own)
    values, start, hits = attention(
        my_index, q_nope, q_rope, mine, other, w_value, norm_gain
    )
    start, swapped = lax.optimization_barrier((start, swapped))

    def part_of(rows, hop):
        return expert_part(my_index, rows, hits, own, swapped, hop, chips)

    def move(block):
        return lax.ppermute(block, "ctx", route)

    def after(block, first):
        return lax.optimization_barrier((block, first))[0]

    rows = move(start)
    later = move(rows) if chips > 2 else None
    sums = part_of(rows, 1).astype(jnp.bfloat16)
    for hop in range(1, chips):
        arrived = move(sums)
        rows = later
        if hop + 2 < chips:
            later = move(after(rows, sums))
        if hop + 1 < chips:
            sums = (part_of(rows, hop + 1) + arrived.astype(jnp.float32)).astype(jnp.bfloat16)
    expert_out = part_of(after(start, sums), 0) + arrived.astype(jnp.float32)
    gate_weight = gate_fixed.astype(jnp.float32) / 65536.0
    return (values.astype(jnp.float32) + gate_weight * expert_out).astype(jnp.bfloat16)


def solution(mesh):
    in_specs = (
        P(("rep", "ctx"), None),
        P(("rep", "ctx"), None),
        P(("rep", "ctx"), None),
        P(("rep", "ctx"), None),
        P(),
        P(),
        P(("rep", "ctx"), None),
        P(("rep", "ctx"), None),
        P("ctx", None, None),
        P("ctx", None, None),
        P("ctx", None, None),
    )
    out_specs = P(("rep", "ctx"), None)
    return jax.shard_map(local, mesh=mesh, in_specs=in_specs, out_specs=out_specs, check_vma=False)
```

```python
import functools
import math

import jax
import jax.numpy as jnp
from jax import lax
from jax.experimental import pallas as pl
from jax.experimental.pallas import tpu as pltpu
from jax.sharding import PartitionSpec as P

HEADS = 32
LAT = 512
ROPE = 64
VD = 128
SPAN = 8
CORES = 2

SCORE_SCALE = 192.0 ** (-0.5)
NORM_EPS = 1e-06
NEG_FILL = -1e30

HEAD_GROUP = 8
SUB_HEADS = 4
SHARES = 2
LOG2_SCALE = SCORE_SCALE * math.log2(math.e)


def attention_kernel(
    index_ref, q_ref, qr_ref, mine_ref, other_ref, wv_ref, values_ref, hits_ref, stack_ref,
    bias_a_ref, bias_b_ref, *, tok,
):
    group = pl.program_id(0)
    my_index = index_ref[0]
    my_chip, my_core = my_index // CORES, lax.rem(my_index, CORES)
    keys = mine_ref.shape[0]

    @pl.when(group == 0)
    def _():
        row_pos = my_index * tok + lax.broadcasted_iota(jnp.int32, (tok, keys), 0)
        key_iota = lax.broadcasted_iota(jnp.int32, (tok, keys), 1)
        key_chip = (key_iota // tok) ^ my_chip
        key_tok = lax.rem(key_iota, jnp.int32(tok))
        for core, bias_ref in ((my_core, bias_a_ref), (1 - my_core, bias_b_ref)):
            key_pos = (key_chip * CORES + core) * tok + key_tok
            bias_ref[...] = jnp.where(key_pos <= row_pos, 0.0, NEG_FILL)
        last = mine_ref[:, LAT : LAT + 2 * ROPE].astype(jnp.float32)
        lane = lax.broadcasted_iota(jnp.int32, last.shape, 1)
        named = jnp.max(jnp.where(lane >= ROPE, last, -1.0), axis=1, keepdims=True)
        my_expert = (my_index // SPAN).astype(jnp.float32)
        hits = jnp.where(named == my_expert, 1.0, 0.0)
        column = lax.broadcasted_iota(jnp.int32, hits_ref.shape, 1)
        table = jnp.zeros(hits_ref.shape, jnp.float32)
        for place in range(keys // tok):
            table = jnp.where(column == place, hits[place * tok : (place + 1) * tok], table)
        hits_ref[...] = table

    lane = lax.broadcasted_iota(jnp.int32, (tok, 2 * ROPE), 1)
    for head in range(HEAD_GROUP):
        at = pl.ds(head * tok, tok)
        stack_ref[at, 0:LAT] = q_ref[:, head * LAT : (head + 1) * LAT]
        pair = qr_ref[:, (head // 2) * 2 * ROPE : (head // 2 + 1) * 2 * ROPE]
        if head % 2:
            pair = jnp.concatenate([pair[:, ROPE:], pair[:, :ROPE]], axis=1)
        stack_ref[at, LAT : LAT + 2 * ROPE] = jnp.where(lane < ROPE, pair, jnp.zeros_like(pair))

    rows = SUB_HEADS * tok
    parts = []
    for sub in range(HEAD_GROUP // SUB_HEADS):
        queries = stack_ref[sub * rows : (sub + 1) * rows, :]

        def scores_of(keys_ref, bias_ref):
            scores = lax.dot_general(
                queries, keys_ref[...], (((1,), (1,)), ((), ())),
                preferred_element_type=jnp.float32,
            )
            return scores.reshape(SUB_HEADS, tok, keys) * LOG2_SCALE + bias_ref[...][None]

        scores_a = scores_of(mine_ref, bias_a_ref)
        scores_b = scores_of(other_ref, bias_b_ref)
        top = jnp.max(jnp.maximum(scores_a, scores_b), axis=2, keepdims=True)
        weights_a = jnp.exp2(scores_a - top)
        weights_b = jnp.exp2(scores_b - top)
        total = jnp.sum(weights_a + weights_b, axis=2, keepdims=True)
        mixed = jnp.dot(
            weights_a.astype(jnp.bfloat16).reshape(rows, keys), mine_ref[:, 0:LAT],
            preferred_element_type=jnp.float32,
        ) + jnp.dot(
            weights_b.astype(jnp.bfloat16).reshape(rows, keys), other_ref[:, 0:LAT],
            preferred_element_type=jnp.float32,
        )
        latent = (mixed.reshape(SUB_HEADS, tok, LAT) / total).astype(jnp.bfloat16)
        for head in range(0, SUB_HEADS, 2):
            first = sub * SUB_HEADS + head
            pair = jnp.dot(
                latent[head : head + 2].reshape(2 * tok, LAT),
                jnp.concatenate([wv_ref[first], wv_ref[first + 1]], axis=1),
                preferred_element_type=jnp.float32,
            ).astype(jnp.bfloat16)
            parts.extend([pair[:tok, :VD], pair[tok:, VD:]])
    values_ref[...] = jnp.concatenate(parts, axis=1)


def attention(my_index, q_nope, q_rope, mine, other, w_value, share):
    tok = q_nope.shape[0]
    total = mine.shape[0]
    rows = HEAD_GROUP * tok
    steps = HEADS // HEAD_GROUP // SHARES
    first = share * steps
    grid_spec = pltpu.PrefetchScalarGridSpec(
        num_scalar_prefetch=1,
        grid=(steps,),
        in_specs=[
            pl.BlockSpec((tok, HEAD_GROUP * LAT), lambda g, i: (0, g + first)),
            pl.BlockSpec((tok, HEAD_GROUP * ROPE), lambda g, i: (0, g + first)),
            pl.BlockSpec(mine.shape, lambda g, i: (0, 0)),
            pl.BlockSpec(mine.shape, lambda g, i: (0, 0)),
            pl.BlockSpec((HEAD_GROUP, LAT, VD), lambda g, i: (g + first, 0, 0)),
        ],
        out_specs=[
            pl.BlockSpec((tok, HEAD_GROUP * VD), lambda g, i: (0, g)),
            pl.BlockSpec((tok, total // tok), lambda g, i: (0, 0)),
        ],
        scratch_shapes=[
            pltpu.VMEM((rows, LAT + 2 * ROPE), jnp.bfloat16),
            pltpu.VMEM((tok, total), jnp.float32),
            pltpu.VMEM((tok, total), jnp.float32),
        ],
    )
    values_shape = jax.ShapeDtypeStruct((tok, HEADS * VD // SHARES), jnp.bfloat16)
    hits_shape = jax.ShapeDtypeStruct((tok, total // tok), jnp.float32)
    work = HEADS * tok * total * CORES // SHARES
    return pl.pallas_call(
        functools.partial(attention_kernel, tok=tok),
        grid_spec=grid_spec,
        out_shape=[values_shape, hits_shape],
        compiler_params=pltpu.CompilerParams(vmem_limit_bytes=56 << 20),
        cost_estimate=pl.CostEstimate(
            flops=2 * work * (2 * LAT + 2 * ROPE), bytes_accessed=5 << 20, transcendentals=work
        ),
    )(my_index.reshape(1), q_nope, q_rope, mine, other, w_value)


def ring_place(chip, chips):
    return jnp.where(chip % 2 == 0, chip // 2, chips - 1 - chip // 2)


def ring_chip(place, chips):
    return jnp.where(place < chips // 2, 2 * place, 2 * (chips - 1 - place) + 1)


def expert_kernel(
    index_ref, left_ref, right_ref, hits_ref, gain_ref, gate_a, up_a, down_a, gate_hbm, up_hbm,
    down_hbm, left_out, right_out, gate_b, up_b, down_b, sems, *, hop, chips,
):
    copies = [
        pltpu.make_async_copy(there, here, sems.at[i])
        for i, (there, here) in enumerate(((gate_hbm, gate_b), (up_hbm, up_b), (down_hbm, down_b)))
    ]
    for copy in copies:
        copy.start()
    tok, width = left_ref.shape
    my_chip, my_core = index_ref[0] // CORES, lax.rem(index_ref[0], CORES)
    place = ring_place(my_chip, chips) + chips + hop * (2 * my_core - 1)
    source = ring_chip(lax.rem(place, chips), chips) ^ my_chip
    column = lax.broadcasted_iota(jnp.int32, hits_ref.shape, 1)
    keep = jnp.max(jnp.where(column == source, hits_ref[...], 0.0), axis=1, keepdims=True) > 0.0

    left, right = left_ref[...].astype(jnp.float32), right_ref[...].astype(jnp.float32)
    square = jnp.sum(left * left, axis=1, keepdims=True)
    square = square + jnp.sum(right * right, axis=1, keepdims=True)
    scale = lax.rsqrt(square / (2 * width) + NORM_EPS)
    rows = jnp.concatenate(
        [
            (left * scale * gain_ref[:, :width]).astype(jnp.bfloat16),
            (right * scale * gain_ref[:, width:]).astype(jnp.bfloat16),
        ],
        axis=1,
    )

    def hidden(gate_ref, up_ref):
        gate_act = jnp.dot(rows, gate_ref[...], preferred_element_type=jnp.float32)
        up_act = jnp.dot(rows, up_ref[...], preferred_element_type=jnp.float32)
        act = gate_act * (1.0 / (1.0 + jnp.exp(-gate_act))) * up_act
        return jnp.where(keep, act, 0.0).astype(jnp.bfloat16)

    part = jnp.dot(hidden(gate_a, up_a), down_a[...], preferred_element_type=jnp.float32)
    copies[0].wait()
    copies[1].wait()
    hidden_b = hidden(gate_b, up_b)
    copies[2].wait()
    part = part + jnp.dot(hidden_b, down_b[...], preferred_element_type=jnp.float32)
    left_out[...] = part[:, :width]
    right_out[...] = part[:, width:]


def expert_part(my_index, rows, hits, gain, own, swapped, hop, chips):
    tok, width = rows[0].shape
    units = 2 * own[0].shape[1]
    vmem, anywhere = pl.BlockSpec(memory_space=pltpu.VMEM), pl.BlockSpec(memory_space=pl.ANY)
    return pl.pallas_call(
        functools.partial(expert_kernel, hop=hop, chips=chips),
        in_specs=[pl.BlockSpec(memory_space=pltpu.SMEM)] + [vmem] * 7 + [anywhere] * 3,
        out_specs=[vmem] * 2,
        out_shape=[jax.ShapeDtypeStruct((tok, width), jnp.float32)] * 2,
        scratch_shapes=[pltpu.VMEM(w.shape, w.dtype) for w in swapped]
        + [pltpu.SemaphoreType.DMA((3,))],
        compiler_params=pltpu.CompilerParams(vmem_limit_bytes=24 << 20),
        cost_estimate=pl.CostEstimate(
            flops=12 * tok * width * units, bytes_accessed=14 << 20, transcendentals=0
        ),
    )(my_index.reshape(1), *rows, hits, gain, *own, *swapped)


def local(
    q_nope, q_rope, c_kv, k_rope, w_value, norm_gain, expert_ids, gate_fixed, w_gate, w_up, w_down
):
    tok = c_kv.shape[0]
    n_ctx = lax.axis_size("ctx")
    chips = n_ctx // CORES
    my_index = lax.axis_index("ctx")
    siblings = [(i, i ^ 1) for i in range(n_ctx)]
    ring = list(range(0, chips, 2)) + list(range(1, chips, 2))[::-1]
    route = [
        (ring[p] * CORES + core, ring[(p + 1 - 2 * core) % chips] * CORES + core)
        for p in range(chips) for core in range(CORES)
    ]

    def from_chip(block, step):
        return lax.ppermute(block, "ctx", [(i, i ^ (step * CORES)) for i in range(n_ctx)])

    ids = jnp.broadcast_to(expert_ids.astype(jnp.bfloat16), (tok, ROPE))
    block = jnp.concatenate([c_kv, k_rope, ids], axis=1)
    across = from_chip(block, chips // 2)
    near = [block] + [from_chip(block, step) for step in range(1, chips // 2)]
    far = [across] + [from_chip(across, step) for step in range(1, chips // 2)]
    mine = jnp.concatenate(near + far, axis=0)
    other = lax.ppermute(mine, "ctx", siblings)

    own, mine, other = lax.optimization_barrier(((w_gate[0], w_up[0], w_down[0]), mine, other))
    swapped = tuple(lax.ppermute(w, "ctx", siblings) for w in own)
    first, hits = attention(my_index, q_nope, q_rope, mine, other, w_value, 0)
    second, _ = attention(my_index, q_nope, q_rope, mine, other, w_value, 1)
    second, swapped = lax.optimization_barrier((second, swapped))
    start = (first, second)
    gain = norm_gain.reshape(1, HEADS * VD)

    def part_of(rows, hop):
        return expert_part(my_index, rows, hits, gain, own, swapped, hop, chips)

    def move(halves):
        return tuple(lax.ppermute(x, "ctx", route) for x in halves)

    def after(halves, before):
        return tuple(lax.optimization_barrier(pair)[0] for pair in zip(halves, before))

    def added(part, arrived):
        return tuple(x + y.astype(jnp.float32) for x, y in zip(part, arrived))

    def rounded(part):
        return tuple(x.astype(jnp.bfloat16) for x in part)

    rows = move(start)
    later = move(rows) if chips > 2 else None
    sums = rounded(part_of(rows, 1))
    for hop in range(1, chips):
        arrived = move(sums)
        rows = later
        if hop + 2 < chips:
            later = move(after(rows, sums))
        if hop + 1 < chips:
            sums = rounded(added(part_of(rows, hop + 1), arrived))
    expert_out = added(part_of(after(start, sums), 0), arrived)
    gate_weight = gate_fixed.astype(jnp.float32) / 65536.0
    mixed = [x.astype(jnp.float32) + gate_weight * y for x, y in zip(start, expert_out)]
    return jnp.concatenate([x.astype(jnp.bfloat16) for x in mixed], axis=1)


def solution(mesh):
    in_specs = (
        P(("rep", "ctx"), None),
        P(("rep", "ctx"), None),
        P(("rep", "ctx"), None),
        P(("rep", "ctx"), None),
        P(),
        P(),
        P(("rep", "ctx"), None),
        P(("rep", "ctx"), None),
        P("ctx", None, None),
        P("ctx", None, None),
        P("ctx", None, None),
    )
    out_specs = P(("rep", "ctx"), None)
    return jax.shard_map(local, mesh=mesh, in_specs=in_specs, out_specs=out_specs, check_vma=False)
```

```python
import functools
import math

import jax
import jax.numpy as jnp
from jax import lax
from jax.experimental import pallas as pl
from jax.experimental.pallas import tpu as pltpu
from jax.sharding import PartitionSpec as P

HEADS = 32
LAT = 512
ROPE = 64
VD = 128
SPAN = 8
CORES = 2

SCORE_SCALE = 192.0 ** (-0.5)
NORM_EPS = 1e-06
NEG_FILL = -1e30

HEAD_GROUP = 8
SUB_HEADS = 4
LOG2_SCALE = SCORE_SCALE * math.log2(math.e)


def attention_kernel(
    index_ref, q_ref, qr_ref, mine_ref, other_ref, wv_ref, gain_ref, values_ref, up_ref,
    down_ref, hits_ref, stack_ref, bias_a_ref, bias_b_ref, *, tok,
):
    group = pl.program_id(0)
    my_index = index_ref[0]
    my_chip, my_core = my_index // CORES, lax.rem(my_index, CORES)
    keys = mine_ref.shape[0]

    @pl.when(group == 0)
    def _():
        row_pos = my_index * tok + lax.broadcasted_iota(jnp.int32, (tok, keys), 0)
        key_iota = lax.broadcasted_iota(jnp.int32, (tok, keys), 1)
        key_chip = (key_iota // tok) ^ my_chip
        key_tok = lax.rem(key_iota, jnp.int32(tok))
        for core, bias_ref in ((my_core, bias_a_ref), (1 - my_core, bias_b_ref)):
            key_pos = (key_chip * CORES + core) * tok + key_tok
            bias_ref[...] = jnp.where(key_pos <= row_pos, 0.0, NEG_FILL)
        last = mine_ref[:, LAT : LAT + 2 * ROPE].astype(jnp.float32)
        lane = lax.broadcasted_iota(jnp.int32, last.shape, 1)
        named = jnp.max(jnp.where(lane >= ROPE, last, -1.0), axis=1, keepdims=True)
        my_expert = (my_index // SPAN).astype(jnp.float32)
        hits = jnp.where(named == my_expert, 1.0, 0.0)
        column = lax.broadcasted_iota(jnp.int32, hits_ref.shape, 1)
        table = jnp.zeros(hits_ref.shape, jnp.float32)
        for place in range(keys // tok):
            table = jnp.where(column == place, hits[place * tok : (place + 1) * tok], table)
        hits_ref[...] = table

    lane = lax.broadcasted_iota(jnp.int32, (tok, 2 * ROPE), 1)
    for head in range(HEAD_GROUP):
        at = pl.ds(head * tok, tok)
        stack_ref[at, 0:LAT] = q_ref[:, head * LAT : (head + 1) * LAT]
        pair = qr_ref[:, (head // 2) * 2 * ROPE : (head // 2 + 1) * 2 * ROPE]
        if head % 2:
            pair = jnp.concatenate([pair[:, ROPE:], pair[:, :ROPE]], axis=1)
        stack_ref[at, LAT : LAT + 2 * ROPE] = jnp.where(lane < ROPE, pair, jnp.zeros_like(pair))

    rows = SUB_HEADS * tok
    parts = []
    for sub in range(HEAD_GROUP // SUB_HEADS):
        queries = stack_ref[sub * rows : (sub + 1) * rows, :]

        def scores_of(keys_ref, bias_ref):
            scores = lax.dot_general(
                queries, keys_ref[...], (((1,), (1,)), ((), ())),
                preferred_element_type=jnp.float32,
            )
            return scores.reshape(SUB_HEADS, tok, keys) * LOG2_SCALE + bias_ref[...][None]

        scores_a = scores_of(mine_ref, bias_a_ref)
        scores_b = scores_of(other_ref, bias_b_ref)
        top = jnp.max(jnp.maximum(scores_a, scores_b), axis=2, keepdims=True)
        weights_a = jnp.exp2(scores_a - top)
        weights_b = jnp.exp2(scores_b - top)
        total = jnp.sum(weights_a + weights_b, axis=2, keepdims=True)
        mixed = jnp.dot(
            weights_a.astype(jnp.bfloat16).reshape(rows, keys), mine_ref[:, 0:LAT],
            preferred_element_type=jnp.float32,
        ) + jnp.dot(
            weights_b.astype(jnp.bfloat16).reshape(rows, keys), other_ref[:, 0:LAT],
            preferred_element_type=jnp.float32,
        )
        latent = (mixed.reshape(SUB_HEADS, tok, LAT) / total).astype(jnp.bfloat16)
        for head in range(0, SUB_HEADS, 2):
            first = sub * SUB_HEADS + head
            pair = jnp.dot(
                latent[head : head + 2].reshape(2 * tok, LAT),
                jnp.concatenate([wv_ref[first], wv_ref[first + 1]], axis=1),
                preferred_element_type=jnp.float32,
            ).astype(jnp.bfloat16)
            parts.extend([pair[:tok, :VD], pair[tok:, VD:]])
    wide = HEAD_GROUP * VD
    values_ref[:, pl.ds(pl.multiple_of(group * wide, wide), wide)] = jnp.concatenate(parts, axis=1)

    @pl.when(group == HEADS // HEAD_GROUP - 1)
    def _():
        values = values_ref[...].astype(jnp.float32)
        square = jnp.mean(values * values, axis=1, keepdims=True)
        normed = values * lax.rsqrt(square + NORM_EPS) * gain_ref[...]
        normed = normed.astype(jnp.bfloat16)
        up_ref[...] = normed[: tok // 2]
        down_ref[...] = normed[tok // 2 :]


def attention(my_index, q_nope, q_rope, mine, other, w_value, norm_gain):
    tok = q_nope.shape[0]
    total = mine.shape[0]
    rows = HEAD_GROUP * tok
    grid_spec = pltpu.PrefetchScalarGridSpec(
        num_scalar_prefetch=1,
        grid=(HEADS // HEAD_GROUP,),
        in_specs=[
            pl.BlockSpec((tok, HEAD_GROUP * LAT), lambda g, i: (0, g)),
            pl.BlockSpec((tok, HEAD_GROUP * ROPE), lambda g, i: (0, g)),
            pl.BlockSpec(mine.shape, lambda g, i: (0, 0)),
            pl.BlockSpec(mine.shape, lambda g, i: (0, 0)),
            pl.BlockSpec((HEAD_GROUP, LAT, VD), lambda g, i: (g, 0, 0)),
            pl.BlockSpec((1, HEADS * VD), lambda g, i: (0, 0)),
        ],
        out_specs=[
            pl.BlockSpec((tok, HEADS * VD), lambda g, i: (0, 0)),
            pl.BlockSpec((tok // 2, HEADS * VD), lambda g, i: (0, 0)),
            pl.BlockSpec((tok // 2, HEADS * VD), lambda g, i: (0, 0)),
            pl.BlockSpec((tok, total // tok), lambda g, i: (0, 0)),
        ],
        scratch_shapes=[
            pltpu.VMEM((rows, LAT + 2 * ROPE), jnp.bfloat16),
            pltpu.VMEM((tok, total), jnp.float32),
            pltpu.VMEM((tok, total), jnp.float32),
        ],
    )
    shape = jax.ShapeDtypeStruct((tok, HEADS * VD), jnp.bfloat16)
    half_shape = jax.ShapeDtypeStruct((tok // 2, HEADS * VD), jnp.bfloat16)
    hits_shape = jax.ShapeDtypeStruct((tok, total // tok), jnp.float32)
    work = HEADS * tok * total * CORES
    return pl.pallas_call(
        functools.partial(attention_kernel, tok=tok),
        grid_spec=grid_spec,
        out_shape=[shape, half_shape, half_shape, hits_shape],
        compiler_params=pltpu.CompilerParams(vmem_limit_bytes=56 << 20),
        cost_estimate=pl.CostEstimate(
            flops=2 * work * (2 * LAT + 2 * ROPE), bytes_accessed=8 << 20, transcendentals=work
        ),
    )(my_index.reshape(1), q_nope, q_rope, mine, other, w_value, norm_gain.reshape(1, HEADS * VD))


def ring_place(chip, chips):
    return jnp.where(chip % 2 == 0, chip // 2, chips - 1 - chip // 2)


def ring_chip(place, chips):
    return jnp.where(place < chips // 2, 2 * place, 2 * (chips - 1 - place) + 1)


def expert_kernel(
    index_ref, upper_ref, lower_ref, hits_ref, gate_a, up_a, down_a, gate_hbm, up_hbm, down_hbm, upper_out,
    lower_out, gate_b, up_b, down_b, sems, *, hop, chips,
):
    copies = [
        pltpu.make_async_copy(there, here, sems.at[i])
        for i, (there, here) in enumerate(((gate_hbm, gate_b), (up_hbm, up_b), (down_hbm, down_b)))
    ]
    for copy in copies:
        copy.start()
    my_chip, my_core = index_ref[0] // CORES, lax.rem(index_ref[0], CORES)
    place = ring_place(my_chip, chips) + chips + hop * (2 * my_core - 1)
    source = ring_chip(lax.rem(place, chips), chips) ^ my_chip
    column = lax.broadcasted_iota(jnp.int32, hits_ref.shape, 1)
    keep = jnp.max(jnp.where(column == source, hits_ref[...], 0.0), axis=1, keepdims=True) > 0.0
    rows = jnp.concatenate([upper_ref[...], lower_ref[...]], axis=0)

    def hidden(gate_ref, up_ref):
        gate_act = jnp.dot(rows, gate_ref[...], preferred_element_type=jnp.float32)
        up_act = jnp.dot(rows, up_ref[...], preferred_element_type=jnp.float32)
        act = gate_act * (1.0 / (1.0 + jnp.exp(-gate_act))) * up_act
        return jnp.where(keep, act, 0.0).astype(jnp.bfloat16)

    part = jnp.dot(hidden(gate_a, up_a), down_a[...], preferred_element_type=jnp.float32)
    copies[0].wait()
    copies[1].wait()
    hidden_b = hidden(gate_b, up_b)
    copies[2].wait()
    part = part + jnp.dot(hidden_b, down_b[...], preferred_element_type=jnp.float32)
    upper_out[...] = part[: upper_ref.shape[0]]
    lower_out[...] = part[upper_ref.shape[0] :]


def expert_part(my_index, rows, hits, own, swapped, hop, chips):
    tok, features = 2 * rows[0].shape[0], rows[0].shape[1]
    units = 2 * own[0].shape[1]
    vmem, anywhere = pl.BlockSpec(memory_space=pltpu.VMEM), pl.BlockSpec(memory_space=pl.ANY)
    return pl.pallas_call(
        functools.partial(expert_kernel, hop=hop, chips=chips),
        in_specs=[pl.BlockSpec(memory_space=pltpu.SMEM)] + [vmem] * 6 + [anywhere] * 3,
        out_specs=[vmem] * 2,
        out_shape=[jax.ShapeDtypeStruct(x.shape, jnp.float32) for x in rows],
        scratch_shapes=[pltpu.VMEM(w.shape, w.dtype) for w in swapped]
        + [pltpu.SemaphoreType.DMA((3,))],
        compiler_params=pltpu.CompilerParams(vmem_limit_bytes=24 << 20),
        cost_estimate=pl.CostEstimate(
            flops=40 * tok * features * units, bytes_accessed=14 << 20, transcendentals=0
        ),
    )(my_index.reshape(1), *rows, hits, *own, *swapped)


def local(
    q_nope, q_rope, c_kv, k_rope, w_value, norm_gain, expert_ids, gate_fixed, w_gate, w_up, w_down
):
    tok = c_kv.shape[0]
    n_ctx = lax.axis_size("ctx")
    chips = n_ctx // CORES
    my_index = lax.axis_index("ctx")
    siblings = [(i, i ^ 1) for i in range(n_ctx)]
    ring = list(range(0, chips, 2)) + list(range(1, chips, 2))[::-1]
    route = [
        (ring[p] * CORES + core, ring[(p + 1 - 2 * core) % chips] * CORES + core)
        for p in range(chips) for core in range(CORES)
    ]

    def from_chip(block, step):
        return lax.ppermute(block, "ctx", [(i, i ^ (step * CORES)) for i in range(n_ctx)])

    ids = jnp.broadcast_to(expert_ids.astype(jnp.bfloat16), (tok, ROPE))
    block = jnp.concatenate([c_kv, k_rope, ids], axis=1)
    across = from_chip(block, chips // 2)
    near = [block] + [from_chip(block, step) for step in range(1, chips // 2)]
    far = [across] + [from_chip(across, step) for step in range(1, chips // 2)]
    mine = jnp.concatenate(near + far, axis=0)
    other = lax.ppermute(mine, "ctx", siblings)

    own, mine, other = lax.optimization_barrier(((w_gate[0], w_up[0], w_down[0]), mine, other))
    swapped = tuple(lax.ppermute(w, "ctx", siblings) for w in own)
    values, upper, lower, hits = attention(
        my_index, q_nope, q_rope, mine, other, w_value, norm_gain
    )
    start, swapped = lax.optimization_barrier(((upper, lower), swapped))

    def part_of(rows, hop):
        return expert_part(my_index, rows, hits, own, swapped, hop, chips)

    def move(blocks):
        return tuple(lax.ppermute(x, "ctx", route) for x in blocks)

    def after(blocks, first):
        return tuple(lax.optimization_barrier((x, first))[0] for x in blocks)

    def rounded(parts):
        return tuple(x.astype(jnp.bfloat16) for x in parts)

    def added(parts, arrived):
        return tuple(x + y.astype(jnp.float32) for x, y in zip(parts, arrived))

    rows = [start]
    for hop in range(1, min(4, chips)):
        rows.append(move(rows[-1]))
    sums = rounded(part_of(rows[1], 1))
    for hop in range(1, chips):
        arrived = move(sums)
        if hop + 3 < chips:
            rows.append(move(after(rows[hop + 2], sums[0])))
        if hop + 1 < chips:
            sums = rounded(added(part_of(rows[hop + 1], hop + 1), arrived))
    home = part_of(after(start, sums[-1]), 0)
    expert_out = jnp.concatenate(added(home, arrived), axis=0)
    gate_weight = gate_fixed.astype(jnp.float32) / 65536.0
    return (values.astype(jnp.float32) + gate_weight * expert_out).astype(jnp.bfloat16)


def solution(mesh):
    in_specs = (
        P(("rep", "ctx"), None),
        P(("rep", "ctx"), None),
        P(("rep", "ctx"), None),
        P(("rep", "ctx"), None),
        P(),
        P(),
        P(("rep", "ctx"), None),
        P(("rep", "ctx"), None),
        P("ctx", None, None),
        P("ctx", None, None),
        P("ctx", None, None),
    )
    out_specs = P(("rep", "ctx"), None)
    return jax.shard_map(local, mesh=mesh, in_specs=in_specs, out_specs=out_specs, check_vma=False)
```

```python
import functools
import math

import jax
import jax.numpy as jnp
from jax import lax
from jax.experimental import pallas as pl
from jax.experimental.pallas import tpu as pltpu
from jax.sharding import PartitionSpec as P

HEADS = 32
LAT = 512
ROPE = 64
VD = 128
SPAN = 8
CORES = 2

SCORE_SCALE = 192.0 ** (-0.5)
NORM_EPS = 1e-06
NEG_FILL = -1e30

HEAD_GROUP = 16
SUB_HEADS = 4
LOG2_SCALE = SCORE_SCALE * math.log2(math.e)


def attention_kernel(
    index_ref, q_ref, qr_ref, mine_ref, other_ref, wv_ref, gain_ref, values_ref, up_ref,
    down_ref, hits_ref, stack_ref, bias_a_ref, bias_b_ref, *, tok,
):
    group = pl.program_id(0)
    my_index = index_ref[0]
    my_chip, my_core = my_index // CORES, lax.rem(my_index, CORES)
    keys = mine_ref.shape[0]

    @pl.when(group == 0)
    def _():
        row_pos = my_index * tok + lax.broadcasted_iota(jnp.int32, (tok, keys), 0)
        key_iota = lax.broadcasted_iota(jnp.int32, (tok, keys), 1)
        key_chip = (key_iota // tok) ^ my_chip
        key_tok = lax.rem(key_iota, jnp.int32(tok))
        for core, bias_ref in ((my_core, bias_a_ref), (1 - my_core, bias_b_ref)):
            key_pos = (key_chip * CORES + core) * tok + key_tok
            bias_ref[...] = jnp.where(key_pos <= row_pos, 0.0, NEG_FILL)
        last = mine_ref[:, LAT : LAT + 2 * ROPE].astype(jnp.float32)
        lane = lax.broadcasted_iota(jnp.int32, last.shape, 1)
        named = jnp.max(jnp.where(lane >= ROPE, last, -1.0), axis=1, keepdims=True)
        my_expert = (my_index // SPAN).astype(jnp.float32)
        hits = jnp.where(named == my_expert, 1.0, 0.0)
        column = lax.broadcasted_iota(jnp.int32, hits_ref.shape, 1)
        table = jnp.zeros(hits_ref.shape, jnp.float32)
        for place in range(keys // tok):
            table = jnp.where(column == place, hits[place * tok : (place + 1) * tok], table)
        hits_ref[...] = table

    lane = lax.broadcasted_iota(jnp.int32, (tok, 2 * ROPE), 1)
    for head in range(HEAD_GROUP):
        at = pl.ds(head * tok, tok)
        stack_ref[at, 0:LAT] = q_ref[:, head * LAT : (head + 1) * LAT]
        pair = qr_ref[:, (head // 2) * 2 * ROPE : (head // 2 + 1) * 2 * ROPE]
        if head % 2:
            pair = jnp.concatenate([pair[:, ROPE:], pair[:, :ROPE]], axis=1)
        stack_ref[at, LAT : LAT + 2 * ROPE] = jnp.where(lane < ROPE, pair, jnp.zeros_like(pair))

    rows = SUB_HEADS * tok

    def scores_of(sub, keys_ref, bias_ref):
        queries = stack_ref[sub * rows : (sub + 1) * rows, :]
        scores = lax.dot_general(
            queries, keys_ref[...], (((1,), (1,)), ((), ())), preferred_element_type=jnp.float32
        )
        return scores.reshape(SUB_HEADS, tok, keys) * LOG2_SCALE + bias_ref[...][None]

    def both_scores(sub):
        return scores_of(sub, mine_ref, bias_a_ref), scores_of(sub, other_ref, bias_b_ref)

    parts = []
    subs = HEAD_GROUP // SUB_HEADS
    ready = both_scores(0)
    for sub in range(subs):
        scores_a, scores_b = ready
        if sub + 1 < subs:
            ready = both_scores(sub + 1)
        top = jnp.max(jnp.maximum(scores_a, scores_b), axis=2, keepdims=True)
        weights_a = jnp.exp2(scores_a - top)
        weights_b = jnp.exp2(scores_b - top)
        total = jnp.sum(weights_a + weights_b, axis=2, keepdims=True)
        mixed = jnp.dot(
            weights_a.astype(jnp.bfloat16).reshape(rows, keys), mine_ref[:, 0:LAT],
            preferred_element_type=jnp.float32,
        ) + jnp.dot(
            weights_b.astype(jnp.bfloat16).reshape(rows, keys), other_ref[:, 0:LAT],
            preferred_element_type=jnp.float32,
        )
        latent = (mixed.reshape(SUB_HEADS, tok, LAT) / total).astype(jnp.bfloat16)
        for head in range(0, SUB_HEADS, 2):
            first = sub * SUB_HEADS + head
            pair = jnp.dot(
                latent[head : head + 2].reshape(2 * tok, LAT),
                jnp.concatenate([wv_ref[first], wv_ref[first + 1]], axis=1),
                preferred_element_type=jnp.float32,
            ).astype(jnp.bfloat16)
            parts.extend([pair[:tok, :VD], pair[tok:, VD:]])
    wide = HEAD_GROUP * VD
    values_ref[:, pl.ds(pl.multiple_of(group * wide, wide), wide)] = jnp.concatenate(parts, axis=1)

    @pl.when(group == HEADS // HEAD_GROUP - 1)
    def _():
        values = values_ref[...].astype(jnp.float32)
        square = jnp.mean(values * values, axis=1, keepdims=True)
        normed = values * lax.rsqrt(square + NORM_EPS) * gain_ref[...]
        normed = normed.astype(jnp.bfloat16)
        up_ref[...] = normed[: tok // 2]
        down_ref[...] = normed[tok // 2 :]


def attention(my_index, q_nope, q_rope, mine, other, w_value, norm_gain):
    tok = q_nope.shape[0]
    total = mine.shape[0]
    rows = HEAD_GROUP * tok
    grid_spec = pltpu.PrefetchScalarGridSpec(
        num_scalar_prefetch=1,
        grid=(HEADS // HEAD_GROUP,),
        in_specs=[
            pl.BlockSpec((tok, HEAD_GROUP * LAT), lambda g, i: (0, g)),
            pl.BlockSpec((tok, HEAD_GROUP * ROPE), lambda g, i: (0, g)),
            pl.BlockSpec(mine.shape, lambda g, i: (0, 0)),
            pl.BlockSpec(mine.shape, lambda g, i: (0, 0)),
            pl.BlockSpec((HEAD_GROUP, LAT, VD), lambda g, i: (g, 0, 0)),
            pl.BlockSpec((1, HEADS * VD), lambda g, i: (0, 0)),
        ],
        out_specs=[
            pl.BlockSpec((tok, HEADS * VD), lambda g, i: (0, 0)),
            pl.BlockSpec((tok // 2, HEADS * VD), lambda g, i: (0, 0)),
            pl.BlockSpec((tok // 2, HEADS * VD), lambda g, i: (0, 0)),
            pl.BlockSpec((tok, total // tok), lambda g, i: (0, 0)),
        ],
        scratch_shapes=[
            pltpu.VMEM((rows, LAT + 2 * ROPE), jnp.bfloat16),
            pltpu.VMEM((tok, total), jnp.float32),
            pltpu.VMEM((tok, total), jnp.float32),
        ],
    )
    shape = jax.ShapeDtypeStruct((tok, HEADS * VD), jnp.bfloat16)
    half_shape = jax.ShapeDtypeStruct((tok // 2, HEADS * VD), jnp.bfloat16)
    hits_shape = jax.ShapeDtypeStruct((tok, total // tok), jnp.float32)
    work = HEADS * tok * total * CORES
    return pl.pallas_call(
        functools.partial(attention_kernel, tok=tok),
        grid_spec=grid_spec,
        out_shape=[shape, half_shape, half_shape, hits_shape],
        compiler_params=pltpu.CompilerParams(vmem_limit_bytes=56 << 20),
        cost_estimate=pl.CostEstimate(
            flops=2 * work * (2 * LAT + 2 * ROPE), bytes_accessed=8 << 20, transcendentals=work
        ),
    )(my_index.reshape(1), q_nope, q_rope, mine, other, w_value, norm_gain.reshape(1, HEADS * VD))


def ring_place(chip, chips):
    return jnp.where(chip % 2 == 0, chip // 2, chips - 1 - chip // 2)


def ring_chip(place, chips):
    return jnp.where(place < chips // 2, 2 * place, 2 * (chips - 1 - place) + 1)


def expert_kernel(
    index_ref, hits_ref, gate_a, up_a, down_a, gate_hbm, up_hbm, down_hbm, *refs, hop, chips,
):
    *rows_refs, out_ref, gate_b, up_b, down_b, sems = refs
    copies = [
        pltpu.make_async_copy(there, here, sems.at[i])
        for i, (there, here) in enumerate(((gate_hbm, gate_b), (up_hbm, up_b), (down_hbm, down_b)))
    ]
    for copy in copies:
        copy.start()
    my_chip, my_core = index_ref[0] // CORES, lax.rem(index_ref[0], CORES)
    place = ring_place(my_chip, chips) + chips + hop * (2 * my_core - 1)
    source = ring_chip(lax.rem(place, chips), chips) ^ my_chip
    column = lax.broadcasted_iota(jnp.int32, hits_ref.shape, 1)
    keep = jnp.max(jnp.where(column == source, hits_ref[...], 0.0), axis=1, keepdims=True) > 0.0
    rows = jnp.concatenate([ref[...] for ref in rows_refs], axis=0)

    def hidden(gate_ref, up_ref):
        gate_act = jnp.dot(rows, gate_ref[...], preferred_element_type=jnp.float32)
        up_act = jnp.dot(rows, up_ref[...], preferred_element_type=jnp.float32)
        act = gate_act * (1.0 / (1.0 + jnp.exp(-gate_act))) * up_act
        return jnp.where(keep, act, 0.0).astype(jnp.bfloat16)

    part = jnp.dot(hidden(gate_a, up_a), down_a[...], preferred_element_type=jnp.float32)
    copies[0].wait()
    copies[1].wait()
    hidden_b = hidden(gate_b, up_b)
    copies[2].wait()
    out_ref[...] = part + jnp.dot(hidden_b, down_b[...], preferred_element_type=jnp.float32)


def expert_part(my_index, rows, hits, own, swapped, hop, chips):
    tok, features = hits.shape[0], rows[0].shape[1]
    units = 2 * own[0].shape[1]
    vmem, anywhere = pl.BlockSpec(memory_space=pltpu.VMEM), pl.BlockSpec(memory_space=pl.ANY)
    return pl.pallas_call(
        functools.partial(expert_kernel, hop=hop, chips=chips),
        in_specs=[pl.BlockSpec(memory_space=pltpu.SMEM)] + [vmem] * 4 + [anywhere] * 3 + [vmem] * len(rows),
        out_specs=vmem,
        out_shape=jax.ShapeDtypeStruct((tok, features), jnp.float32),
        scratch_shapes=[pltpu.VMEM(w.shape, w.dtype) for w in swapped]
        + [pltpu.SemaphoreType.DMA((3,))],
        compiler_params=pltpu.CompilerParams(vmem_limit_bytes=24 << 20),
        cost_estimate=pl.CostEstimate(
            flops=6 * tok * features * units, bytes_accessed=14 << 20, transcendentals=0
        ),
    )(my_index.reshape(1), hits, *own, *swapped, *rows)


def local(
    q_nope, q_rope, c_kv, k_rope, w_value, norm_gain, expert_ids, gate_fixed, w_gate, w_up, w_down
):
    tok = c_kv.shape[0]
    n_ctx = lax.axis_size("ctx")
    chips = n_ctx // CORES
    my_index = lax.axis_index("ctx")
    siblings = [(i, i ^ 1) for i in range(n_ctx)]
    ring = list(range(0, chips, 2)) + list(range(1, chips, 2))[::-1]
    route = [
        (ring[p] * CORES + core, ring[(p + 1 - 2 * core) % chips] * CORES + core)
        for p in range(chips) for core in range(CORES)
    ]

    def from_chip(block, step):
        return lax.ppermute(block, "ctx", [(i, i ^ (step * CORES)) for i in range(n_ctx)])

    ids = jnp.broadcast_to(expert_ids.astype(jnp.bfloat16), (tok, ROPE))
    block = jnp.concatenate([c_kv, k_rope, ids], axis=1)
    across = from_chip(block, chips // 2)
    near = [block] + [from_chip(block, step) for step in range(1, chips // 2)]
    far = [across] + [from_chip(across, step) for step in range(1, chips // 2)]
    mine = jnp.concatenate(near + far, axis=0)
    other = lax.ppermute(mine, "ctx", siblings)

    own, mine, other = lax.optimization_barrier(((w_gate[0], w_up[0], w_down[0]), mine, other))
    swapped = tuple(lax.ppermute(w, "ctx", siblings) for w in own)
    values, upper, lower, hits = attention(
        my_index, q_nope, q_rope, mine, other, w_value, norm_gain
    )
    start, swapped = lax.optimization_barrier(((upper, lower), swapped))

    def part_of(rows, hop):
        return expert_part(my_index, rows, hits, own, swapped, hop, chips)

    def move(blocks):
        return tuple(lax.ppermute(x, "ctx", route) for x in blocks)

    def after(blocks, first):
        return tuple(lax.optimization_barrier((x, first))[0] for x in blocks)

    rows = [start]
    for hop in range(1, min(4, chips)):
        last = rows[-1]
        rows.append(move((jnp.concatenate(last, axis=0),) if hop == 3 else last))
    sums = part_of(rows[1], 1).astype(jnp.bfloat16)
    for hop in range(1, chips):
        (arrived,) = move((sums,))
        if hop + 3 < chips:
            rows.append(move(after(rows[hop + 2], sums)))
        if hop + 1 < chips:
            part = part_of(rows[hop + 1], hop + 1)
            sums = (part + arrived.astype(jnp.float32)).astype(jnp.bfloat16)
    expert_out = part_of(after(start, sums), 0) + arrived.astype(jnp.float32)
    gate_weight = gate_fixed.astype(jnp.float32) / 65536.0
    return (values.astype(jnp.float32) + gate_weight * expert_out).astype(jnp.bfloat16)


def solution(mesh):
    in_specs = (
        P(("rep", "ctx"), None),
        P(("rep", "ctx"), None),
        P(("rep", "ctx"), None),
        P(("rep", "ctx"), None),
        P(),
        P(),
        P(("rep", "ctx"), None),
        P(("rep", "ctx"), None),
        P("ctx", None, None),
        P("ctx", None, None),
        P("ctx", None, None),
    )
    out_specs = P(("rep", "ctx"), None)
    return jax.shard_map(local, mesh=mesh, in_specs=in_specs, out_specs=out_specs, check_vma=False)
```

```python
import functools
import math

import jax
import jax.numpy as jnp
from jax import lax
from jax.experimental import pallas as pl
from jax.experimental.pallas import tpu as pltpu
from jax.sharding import PartitionSpec as P

HEADS = 32
LAT = 512
ROPE = 64
VD = 128
SPAN = 8
CORES = 2

SCORE_SCALE = 192.0 ** (-0.5)
NORM_EPS = 1e-06
NEG_FILL = -1e30

HEAD_GROUP = 16
SUB_HEADS = 4
SPLIT_HOPS = 2
LOG2_SCALE = SCORE_SCALE * math.log2(math.e)


def attention_kernel(
    index_ref, q_ref, qr_ref, mine_ref, other_ref, wv_ref, gain_ref, values_ref, up_ref,
    down_ref, hits_ref, stack_ref, bias_a_ref, bias_b_ref, *, tok,
):
    group = pl.program_id(0)
    my_index = index_ref[0]
    my_chip, my_core = my_index // CORES, lax.rem(my_index, CORES)
    keys = mine_ref.shape[0]

    @pl.when(group == 0)
    def _():
        row_pos = my_index * tok + lax.broadcasted_iota(jnp.int32, (tok, keys), 0)
        key_iota = lax.broadcasted_iota(jnp.int32, (tok, keys), 1)
        key_chip = (key_iota // tok) ^ my_chip
        key_tok = lax.rem(key_iota, jnp.int32(tok))
        for core, bias_ref in ((my_core, bias_a_ref), (1 - my_core, bias_b_ref)):
            key_pos = (key_chip * CORES + core) * tok + key_tok
            bias_ref[...] = jnp.where(key_pos <= row_pos, 0.0, NEG_FILL)
        last = mine_ref[:, LAT : LAT + 2 * ROPE].astype(jnp.float32)
        lane = lax.broadcasted_iota(jnp.int32, last.shape, 1)
        named = jnp.max(jnp.where(lane >= ROPE, last, -1.0), axis=1, keepdims=True)
        my_expert = (my_index // SPAN).astype(jnp.float32)
        hits = jnp.where(named == my_expert, 1.0, 0.0)
        column = lax.broadcasted_iota(jnp.int32, hits_ref.shape, 1)
        table = jnp.zeros(hits_ref.shape, jnp.float32)
        for place in range(keys // tok):
            table = jnp.where(column == place, hits[place * tok : (place + 1) * tok], table)
        hits_ref[...] = table

    lane = lax.broadcasted_iota(jnp.int32, (tok, 2 * ROPE), 1)
    for head in range(HEAD_GROUP):
        at = pl.ds(head * tok, tok)
        stack_ref[at, 0:LAT] = q_ref[:, head * LAT : (head + 1) * LAT]
        pair = qr_ref[:, (head // 2) * 2 * ROPE : (head // 2 + 1) * 2 * ROPE]
        if head % 2:
            pair = jnp.concatenate([pair[:, ROPE:], pair[:, :ROPE]], axis=1)
        stack_ref[at, LAT : LAT + 2 * ROPE] = jnp.where(lane < ROPE, pair, jnp.zeros_like(pair))

    rows = SUB_HEADS * tok

    def scores_of(sub, keys_ref, bias_ref):
        queries = stack_ref[sub * rows : (sub + 1) * rows, :]
        scores = lax.dot_general(
            queries, keys_ref[...], (((1,), (1,)), ((), ())), preferred_element_type=jnp.float32
        )
        return scores.reshape(SUB_HEADS, tok, keys) * LOG2_SCALE + bias_ref[...][None]

    def both_scores(sub):
        return scores_of(sub, mine_ref, bias_a_ref), scores_of(sub, other_ref, bias_b_ref)

    parts = []
    subs = HEAD_GROUP // SUB_HEADS
    ready = both_scores(0)
    for sub in range(subs):
        scores_a, scores_b = ready
        if sub + 1 < subs:
            ready = both_scores(sub + 1)
        top = jnp.max(jnp.maximum(scores_a, scores_b), axis=2, keepdims=True)
        weights_a = jnp.exp2(scores_a - top)
        weights_b = jnp.exp2(scores_b - top)
        total = jnp.sum(weights_a + weights_b, axis=2, keepdims=True)
        mixed = jnp.dot(
            weights_a.astype(jnp.bfloat16).reshape(rows, keys), mine_ref[:, 0:LAT],
            preferred_element_type=jnp.float32,
        ) + jnp.dot(
            weights_b.astype(jnp.bfloat16).reshape(rows, keys), other_ref[:, 0:LAT],
            preferred_element_type=jnp.float32,
        )
        latent = (mixed.reshape(SUB_HEADS, tok, LAT) / total).astype(jnp.bfloat16)
        for head in range(0, SUB_HEADS, 2):
            first = sub * SUB_HEADS + head
            pair = jnp.dot(
                latent[head : head + 2].reshape(2 * tok, LAT),
                jnp.concatenate([wv_ref[first], wv_ref[first + 1]], axis=1),
                preferred_element_type=jnp.float32,
            ).astype(jnp.bfloat16)
            parts.extend([pair[:tok, :VD], pair[tok:, VD:]])
    wide = HEAD_GROUP * VD
    values_ref[:, pl.ds(pl.multiple_of(group * wide, wide), wide)] = jnp.concatenate(parts, axis=1)

    @pl.when(group == HEADS // HEAD_GROUP - 1)
    def _():
        values = values_ref[...].astype(jnp.float32)
        square = jnp.mean(values * values, axis=1, keepdims=True)
        normed = values * lax.rsqrt(square + NORM_EPS) * gain_ref[...]
        normed = normed.astype(jnp.bfloat16)
        up_ref[...] = normed[: tok // 2]
        down_ref[...] = normed[tok // 2 :]


def attention(my_index, q_nope, q_rope, mine, other, w_value, norm_gain):
    tok = q_nope.shape[0]
    total = mine.shape[0]
    rows = HEAD_GROUP * tok
    grid_spec = pltpu.PrefetchScalarGridSpec(
        num_scalar_prefetch=1,
        grid=(HEADS // HEAD_GROUP,),
        in_specs=[
            pl.BlockSpec((tok, HEAD_GROUP * LAT), lambda g, i: (0, g)),
            pl.BlockSpec((tok, HEAD_GROUP * ROPE), lambda g, i: (0, g)),
            pl.BlockSpec(mine.shape, lambda g, i: (0, 0)),
            pl.BlockSpec(mine.shape, lambda g, i: (0, 0)),
            pl.BlockSpec((HEAD_GROUP, LAT, VD), lambda g, i: (g, 0, 0)),
            pl.BlockSpec((1, HEADS * VD), lambda g, i: (0, 0)),
        ],
        out_specs=[
            pl.BlockSpec((tok, HEADS * VD), lambda g, i: (0, 0)),
            pl.BlockSpec((tok // 2, HEADS * VD), lambda g, i: (0, 0)),
            pl.BlockSpec((tok // 2, HEADS * VD), lambda g, i: (0, 0)),
            pl.BlockSpec((tok, total // tok), lambda g, i: (0, 0)),
        ],
        scratch_shapes=[
            pltpu.VMEM((rows, LAT + 2 * ROPE), jnp.bfloat16),
            pltpu.VMEM((tok, total), jnp.float32),
            pltpu.VMEM((tok, total), jnp.float32),
        ],
    )
    shape = jax.ShapeDtypeStruct((tok, HEADS * VD), jnp.bfloat16)
    half_shape = jax.ShapeDtypeStruct((tok // 2, HEADS * VD), jnp.bfloat16)
    hits_shape = jax.ShapeDtypeStruct((tok, total // tok), jnp.float32)
    work = HEADS * tok * total * CORES
    return pl.pallas_call(
        functools.partial(attention_kernel, tok=tok),
        grid_spec=grid_spec,
        out_shape=[shape, half_shape, half_shape, hits_shape],
        compiler_params=pltpu.CompilerParams(vmem_limit_bytes=56 << 20),
        cost_estimate=pl.CostEstimate(
            flops=2 * work * (2 * LAT + 2 * ROPE), bytes_accessed=8 << 20, transcendentals=work
        ),
    )(my_index.reshape(1), q_nope, q_rope, mine, other, w_value, norm_gain.reshape(1, HEADS * VD))


def ring_place(chip, chips):
    return jnp.where(chip % 2 == 0, chip // 2, chips - 1 - chip // 2)


def ring_chip(place, chips):
    return jnp.where(place < chips // 2, 2 * place, 2 * (chips - 1 - place) + 1)


def expert_kernel(
    index_ref, gate_a, up_a, down_a, hits_hbm, gate_hbm, up_hbm, down_hbm, *refs, hop, chips,
    pieces,
):
    *refs, hits_ref, gate_b, up_b, down_b, sems = refs
    rows_refs, out_refs = refs[:-pieces], refs[-pieces:]
    pairs = ((hits_hbm, hits_ref), (gate_hbm, gate_b), (up_hbm, up_b), (down_hbm, down_b))
    copies = [
        pltpu.make_async_copy(there, here, sems.at[i]) for i, (there, here) in enumerate(pairs)
    ]
    for copy in copies:
        copy.start()
    my_chip, my_core = index_ref[0] // CORES, lax.rem(index_ref[0], CORES)
    place = ring_place(my_chip, chips) + chips + hop * (2 * my_core - 1)
    source = ring_chip(lax.rem(place, chips), chips) ^ my_chip
    rows = jnp.concatenate([ref[...] for ref in rows_refs], axis=0)

    def hidden(gate_ref, up_ref):
        gate_act = jnp.dot(rows, gate_ref[...], preferred_element_type=jnp.float32)
        up_act = jnp.dot(rows, up_ref[...], preferred_element_type=jnp.float32)
        return gate_act * (1.0 / (1.0 + jnp.exp(-gate_act))) * up_act

    def kept(act):
        return jnp.where(keep, act, 0.0).astype(jnp.bfloat16)

    act_a = hidden(gate_a, up_a)
    copies[0].wait()
    column = lax.broadcasted_iota(jnp.int32, hits_ref.shape, 1)
    keep = jnp.max(jnp.where(column == source, hits_ref[...], 0.0), axis=1, keepdims=True) > 0.0
    part = jnp.dot(kept(act_a), down_a[...], preferred_element_type=jnp.float32)
    copies[1].wait()
    copies[2].wait()
    act_b = hidden(gate_b, up_b)
    copies[3].wait()
    part = part + jnp.dot(kept(act_b), down_b[...], preferred_element_type=jnp.float32)
    size = part.shape[0] // pieces
    for i, out_ref in enumerate(out_refs):
        out_ref[...] = part[i * size : (i + 1) * size]


def expert_part(my_index, rows, hits, own, swapped, hop, chips, pieces):
    tok, features = hits.shape[0], rows[0].shape[1]
    units = 2 * own[0].shape[1]
    vmem, anywhere = pl.BlockSpec(memory_space=pltpu.VMEM), pl.BlockSpec(memory_space=pl.ANY)
    return pl.pallas_call(
        functools.partial(expert_kernel, hop=hop, chips=chips, pieces=pieces),
        in_specs=[pl.BlockSpec(memory_space=pltpu.SMEM)] + [vmem] * 3 + [anywhere] * 4 + [vmem] * len(rows),
        out_specs=[vmem] * pieces,
        out_shape=[jax.ShapeDtypeStruct((tok // pieces, features), jnp.float32)] * pieces,
        scratch_shapes=[pltpu.VMEM(w.shape, w.dtype) for w in (hits, *swapped)]
        + [pltpu.SemaphoreType.DMA((4,))],
        compiler_params=pltpu.CompilerParams(vmem_limit_bytes=24 << 20),
        cost_estimate=pl.CostEstimate(
            flops=6 * tok * features * units, bytes_accessed=14 << 20, transcendentals=0
        ),
    )(my_index.reshape(1), *own, hits, *swapped, *rows)


def local(
    q_nope, q_rope, c_kv, k_rope, w_value, norm_gain, expert_ids, gate_fixed, w_gate, w_up, w_down
):
    tok = c_kv.shape[0]
    n_ctx = lax.axis_size("ctx")
    chips = n_ctx // CORES
    my_index = lax.axis_index("ctx")
    siblings = [(i, i ^ 1) for i in range(n_ctx)]
    ring = list(range(0, chips, 2)) + list(range(1, chips, 2))[::-1]
    route = [
        (ring[p] * CORES + core, ring[(p + 1 - 2 * core) % chips] * CORES + core)
        for p in range(chips) for core in range(CORES)
    ]

    def from_chip(block, step):
        return lax.ppermute(block, "ctx", [(i, i ^ (step * CORES)) for i in range(n_ctx)])

    ids = jnp.broadcast_to(expert_ids.astype(jnp.bfloat16), (tok, ROPE))
    block = jnp.concatenate([c_kv, k_rope, ids], axis=1)
    across = from_chip(block, chips // 2)
    near = [block] + [from_chip(block, step) for step in range(1, chips // 2)]
    far = [across] + [from_chip(across, step) for step in range(1, chips // 2)]
    mine = jnp.concatenate(near + far, axis=0)
    other = lax.ppermute(mine, "ctx", siblings)

    own, mine, other = lax.optimization_barrier(((w_gate[0], w_up[0], w_down[0]), mine, other))
    swapped = tuple(lax.ppermute(w, "ctx", siblings) for w in own)
    values, upper, lower, hits = attention(
        my_index, q_nope, q_rope, mine, other, w_value, norm_gain
    )
    start, swapped = lax.optimization_barrier(((upper, lower), swapped))

    def part_of(rows, hop):
        pieces = 1 if 0 < hop < chips - SPLIT_HOPS else 2
        return expert_part(my_index, rows, hits, own, swapped, hop, chips, pieces)

    def move(blocks):
        return tuple(lax.ppermute(x, "ctx", route) for x in blocks)

    def after(blocks, first):
        return tuple(lax.optimization_barrier((x, first))[0] for x in blocks)

    rows = [start]
    for hop in range(1, min(4, chips)):
        last = rows[-1]
        rows.append(move((jnp.concatenate(last, axis=0),) if hop == 3 else last))
    def added(part, arrived):
        if len(part) > len(arrived):
            arrived = (arrived[0][: tok // 2], arrived[0][tok // 2 :])
        return tuple(x + y.astype(jnp.float32) for x, y in zip(part, arrived))

    def rounded(part):
        return tuple(x.astype(jnp.bfloat16) for x in part)

    sums = rounded(part_of(rows[1], 1))
    for hop in range(1, chips):
        arrived = move(sums)
        if hop + 3 < chips:
            rows.append(move(after(rows[hop + 2], sums)))
        if hop + 1 < chips:
            sums = rounded(added(part_of(rows[hop + 1], hop + 1), arrived))
    expert_out = jnp.concatenate(added(part_of(after(start, sums), 0), arrived), axis=0)
    gate_weight = gate_fixed.astype(jnp.float32) / 65536.0
    return (values.astype(jnp.float32) + gate_weight * expert_out).astype(jnp.bfloat16)


def solution(mesh):
    in_specs = (
        P(("rep", "ctx"), None),
        P(("rep", "ctx"), None),
        P(("rep", "ctx"), None),
        P(("rep", "ctx"), None),
        P(),
        P(),
        P(("rep", "ctx"), None),
        P(("rep", "ctx"), None),
        P("ctx", None, None),
        P("ctx", None, None),
        P("ctx", None, None),
    )
    out_specs = P(("rep", "ctx"), None)
    return jax.shard_map(local, mesh=mesh, in_specs=in_specs, out_specs=out_specs, check_vma=False)
```

```python
import functools
import math

import jax
import jax.numpy as jnp
from jax import lax
from jax.experimental import pallas as pl
from jax.experimental.pallas import tpu as pltpu
from jax.sharding import PartitionSpec as P

HEADS = 32
LAT = 512
ROPE = 64
VD = 128
SPAN = 8
CORES = 2

SCORE_SCALE = 192.0 ** (-0.5)
NORM_EPS = 1e-06
NEG_FILL = -1e30

SUB_HEADS = 4
SPLIT_HOPS = 2
LOG2_SCALE = SCORE_SCALE * math.log2(math.e)


def attention_kernel(
    index_ref, mine_hbm, other_hbm, q_hbm, qr_hbm, wv_hbm, gain_ref, values_ref, up_ref, down_ref,
    hits_ref, mine_ref, other_ref, q_ref, qr_ref, wv_ref, stack_ref, bias_a_ref, bias_b_ref,
    sems, *, tok,
):
    copies = []

    def fetch(there, here):
        copies.append(pltpu.make_async_copy(there, here, sems.at[len(copies)]))
        copies[-1].start()
        return copies[-1]

    subs = HEADS // SUB_HEADS
    lanes = [pl.ds(sub * SUB_HEADS * LAT, SUB_HEADS * LAT) for sub in range(subs)]
    heads = [pl.ds(sub * SUB_HEADS, SUB_HEADS) for sub in range(subs)]
    q_copies = [fetch(q_hbm.at[:, lanes[0]], q_ref.at[:, lanes[0]])]
    first_copies = [fetch(qr_hbm, qr_ref), fetch(mine_hbm, mine_ref), fetch(other_hbm, other_ref)]
    wv_copies = []
    for sub in range(subs):
        if sub:
            q_copies.append(fetch(q_hbm.at[:, lanes[sub]], q_ref.at[:, lanes[sub]]))
        wv_copies.append(fetch(wv_hbm.at[heads[sub]], wv_ref.at[heads[sub]]))
    my_index = index_ref[0]
    my_chip, my_core = my_index // CORES, lax.rem(my_index, CORES)
    keys = mine_ref.shape[0]

    row_pos = my_index * tok + lax.broadcasted_iota(jnp.int32, (tok, keys), 0)
    key_iota = lax.broadcasted_iota(jnp.int32, (tok, keys), 1)
    key_chip = (key_iota // tok) ^ my_chip
    key_tok = lax.rem(key_iota, jnp.int32(tok))
    for core, bias_ref in ((my_core, bias_a_ref), (1 - my_core, bias_b_ref)):
        key_pos = (key_chip * CORES + core) * tok + key_tok
        bias_ref[...] = jnp.where(key_pos <= row_pos, 0.0, NEG_FILL)

    rows = SUB_HEADS * tok
    lane = lax.broadcasted_iota(jnp.int32, (tok, 2 * ROPE), 1)

    def scores_of(sub, keys_ref, bias_ref):
        queries = stack_ref[sub * rows : (sub + 1) * rows, :]
        scores = lax.dot_general(
            queries, keys_ref[...], (((1,), (1,)), ((), ())), preferred_element_type=jnp.float32
        )
        return scores.reshape(SUB_HEADS, tok, keys) * LOG2_SCALE + bias_ref[...][None]

    def both_scores(sub):
        q_copies[sub].wait()
        for copy in first_copies if sub == 0 else []:
            copy.wait()
        for head in range(sub * SUB_HEADS, (sub + 1) * SUB_HEADS):
            at = pl.ds(head * tok, tok)
            stack_ref[at, 0:LAT] = q_ref[:, head * LAT : (head + 1) * LAT]
            pair = qr_ref[:, (head // 2) * 2 * ROPE : (head // 2 + 1) * 2 * ROPE]
            if head % 2:
                pair = jnp.concatenate([pair[:, ROPE:], pair[:, :ROPE]], axis=1)
            stack_ref[at, LAT : LAT + 2 * ROPE] = jnp.where(lane < ROPE, pair, jnp.zeros_like(pair))
        return scores_of(sub, mine_ref, bias_a_ref), scores_of(sub, other_ref, bias_b_ref)

    ready = both_scores(0)
    for sub in range(subs):
        scores_a, scores_b = ready
        if sub + 1 < subs:
            ready = both_scores(sub + 1)
        top = jnp.max(jnp.maximum(scores_a, scores_b), axis=2, keepdims=True)
        weights_a = jnp.exp2(scores_a - top)
        weights_b = jnp.exp2(scores_b - top)
        total = jnp.sum(weights_a + weights_b, axis=2, keepdims=True)
        mixed = jnp.dot(
            weights_a.astype(jnp.bfloat16).reshape(rows, keys), mine_ref[:, 0:LAT],
            preferred_element_type=jnp.float32,
        ) + jnp.dot(
            weights_b.astype(jnp.bfloat16).reshape(rows, keys), other_ref[:, 0:LAT],
            preferred_element_type=jnp.float32,
        )
        latent = (mixed.reshape(SUB_HEADS, tok, LAT) / total).astype(jnp.bfloat16)
        wv_copies[sub].wait()
        for head in range(0, SUB_HEADS, 2):
            first = sub * SUB_HEADS + head
            pair = jnp.dot(
                latent[head : head + 2].reshape(2 * tok, LAT),
                jnp.concatenate([wv_ref[first], wv_ref[first + 1]], axis=1),
                preferred_element_type=jnp.float32,
            ).astype(jnp.bfloat16)
            values_ref[:, first * VD : (first + 1) * VD] = pair[:tok, :VD]
            values_ref[:, (first + 1) * VD : (first + 2) * VD] = pair[tok:, VD:]

    values = values_ref[...].astype(jnp.float32)
    square = jnp.mean(values * values, axis=1, keepdims=True)
    normed = values * lax.rsqrt(square + NORM_EPS) * gain_ref[...]
    normed = normed.astype(jnp.bfloat16)
    up_ref[...] = normed[: tok // 2]
    down_ref[...] = normed[tok // 2 :]

    last = mine_ref[:, LAT : LAT + 2 * ROPE].astype(jnp.float32)
    lane = lax.broadcasted_iota(jnp.int32, last.shape, 1)
    named = jnp.max(jnp.where(lane >= ROPE, last, -1.0), axis=1, keepdims=True)
    my_expert = (my_index // SPAN).astype(jnp.float32)
    hits = jnp.where(named == my_expert, 1.0, 0.0)
    column = lax.broadcasted_iota(jnp.int32, hits_ref.shape, 1)
    table = jnp.zeros(hits_ref.shape, jnp.float32)
    for place in range(keys // tok):
        table = jnp.where(column == place, hits[place * tok : (place + 1) * tok], table)
    hits_ref[...] = table


def attention(my_index, q_nope, q_rope, mine, other, w_value, gain):
    tok = q_nope.shape[0]
    total = mine.shape[0]
    rows = HEADS * tok
    vmem, anywhere = pl.BlockSpec(memory_space=pltpu.VMEM), pl.BlockSpec(memory_space=pl.ANY)
    shape = jax.ShapeDtypeStruct((tok, HEADS * VD), jnp.bfloat16)
    half_shape = jax.ShapeDtypeStruct((tok // 2, HEADS * VD), jnp.bfloat16)
    hits_shape = jax.ShapeDtypeStruct((tok, total // tok), jnp.float32)
    work = HEADS * tok * total * CORES
    fetched = (mine, other, q_nope, q_rope, w_value)
    return pl.pallas_call(
        functools.partial(attention_kernel, tok=tok),
        in_specs=[pl.BlockSpec(memory_space=pltpu.SMEM)] + [anywhere] * 5 + [vmem],
        out_specs=[vmem] * 4,
        out_shape=[shape, half_shape, half_shape, hits_shape],
        scratch_shapes=[pltpu.VMEM(x.shape, x.dtype) for x in fetched]
        + [
            pltpu.VMEM((rows, LAT + 2 * ROPE), jnp.bfloat16),
            pltpu.VMEM((tok, total), jnp.float32),
            pltpu.VMEM((tok, total), jnp.float32),
            pltpu.SemaphoreType.DMA((3 + 2 * (HEADS // SUB_HEADS),)),
        ],
        compiler_params=pltpu.CompilerParams(vmem_limit_bytes=56 << 20),
        cost_estimate=pl.CostEstimate(
            flops=2 * work * (2 * LAT + 2 * ROPE), bytes_accessed=8 << 20, transcendentals=work
        ),
    )(my_index.reshape(1), *fetched, gain)


def ring_place(chip, chips):
    return jnp.where(chip % 2 == 0, chip // 2, chips - 1 - chip // 2)


def ring_chip(place, chips):
    return jnp.where(place < chips // 2, 2 * place, 2 * (chips - 1 - place) + 1)


def expert_kernel(
    index_ref, gate_a, up_a, down_a, hits_hbm, gate_hbm, up_hbm, down_hbm, *refs, hop, chips,
    pieces,
):
    *refs, hits_ref, gate_b, up_b, down_b, sems = refs
    rows_refs, out_refs = refs[:-pieces], refs[-pieces:]
    pairs = ((hits_hbm, hits_ref), (gate_hbm, gate_b), (up_hbm, up_b), (down_hbm, down_b))
    copies = [
        pltpu.make_async_copy(there, here, sems.at[i]) for i, (there, here) in enumerate(pairs)
    ]
    for copy in copies:
        copy.start()
    my_chip, my_core = index_ref[0] // CORES, lax.rem(index_ref[0], CORES)
    place = ring_place(my_chip, chips) + chips + hop * (2 * my_core - 1)
    source = ring_chip(lax.rem(place, chips), chips) ^ my_chip
    rows = jnp.concatenate([ref[...] for ref in rows_refs], axis=0)

    def hidden(gate_ref, up_ref):
        gate_act = jnp.dot(rows, gate_ref[...], preferred_element_type=jnp.float32)
        up_act = jnp.dot(rows, up_ref[...], preferred_element_type=jnp.float32)
        return gate_act * (1.0 / (1.0 + jnp.exp(-gate_act))) * up_act

    def kept(act):
        return jnp.where(keep, act, 0.0).astype(jnp.bfloat16)

    act_a = hidden(gate_a, up_a)
    copies[0].wait()
    column = lax.broadcasted_iota(jnp.int32, hits_ref.shape, 1)
    keep = jnp.max(jnp.where(column == source, hits_ref[...], 0.0), axis=1, keepdims=True) > 0.0
    part = jnp.dot(kept(act_a), down_a[...], preferred_element_type=jnp.float32)
    copies[1].wait()
    copies[2].wait()
    act_b = hidden(gate_b, up_b)
    copies[3].wait()
    part = part + jnp.dot(kept(act_b), down_b[...], preferred_element_type=jnp.float32)
    size = part.shape[0] // pieces
    for i, out_ref in enumerate(out_refs):
        out_ref[...] = part[i * size : (i + 1) * size]


def expert_part(my_index, rows, hits, own, swapped, hop, chips, pieces):
    tok, features = hits.shape[0], rows[0].shape[1]
    units = 2 * own[0].shape[1]
    vmem, anywhere = pl.BlockSpec(memory_space=pltpu.VMEM), pl.BlockSpec(memory_space=pl.ANY)
    return pl.pallas_call(
        functools.partial(expert_kernel, hop=hop, chips=chips, pieces=pieces),
        in_specs=[pl.BlockSpec(memory_space=pltpu.SMEM)] + [vmem] * 3 + [anywhere] * 4 + [vmem] * len(rows),
        out_specs=[vmem] * pieces,
        out_shape=[jax.ShapeDtypeStruct((tok // pieces, features), jnp.float32)] * pieces,
        scratch_shapes=[pltpu.VMEM(w.shape, w.dtype) for w in (hits, *swapped)]
        + [pltpu.SemaphoreType.DMA((4,))],
        compiler_params=pltpu.CompilerParams(vmem_limit_bytes=24 << 20),
        cost_estimate=pl.CostEstimate(
            flops=6 * tok * features * units, bytes_accessed=14 << 20, transcendentals=0
        ),
    )(my_index.reshape(1), *own, hits, *swapped, *rows)


def local(
    q_nope, q_rope, c_kv, k_rope, w_value, norm_gain, expert_ids, gate_fixed, w_gate, w_up, w_down
):
    tok = c_kv.shape[0]
    n_ctx = lax.axis_size("ctx")
    chips = n_ctx // CORES
    my_index = lax.axis_index("ctx")
    siblings = [(i, i ^ 1) for i in range(n_ctx)]
    ring = list(range(0, chips, 2)) + list(range(1, chips, 2))[::-1]
    route = [
        (ring[p] * CORES + core, ring[(p + 1 - 2 * core) % chips] * CORES + core)
        for p in range(chips) for core in range(CORES)
    ]

    def from_chip(block, step):
        return lax.ppermute(block, "ctx", [(i, i ^ (step * CORES)) for i in range(n_ctx)])

    ids = jnp.broadcast_to(expert_ids.astype(jnp.bfloat16), (tok, ROPE))
    block = jnp.concatenate([c_kv, k_rope, ids], axis=1)
    across = from_chip(block, chips // 2)
    near = [block] + [from_chip(block, step) for step in range(1, chips // 2)]
    far = [across] + [from_chip(across, step) for step in range(1, chips // 2)]
    mine = jnp.concatenate(near + far, axis=0)
    other = lax.ppermute(mine, "ctx", siblings)

    own, mine, other = lax.optimization_barrier(((w_gate[0], w_up[0], w_down[0]), mine, other))
    swapped = tuple(lax.ppermute(w, "ctx", siblings) for w in own)
    values, upper, lower, hits = attention(
        my_index, q_nope, q_rope, mine, other, w_value, norm_gain.reshape(1, HEADS * VD)
    )
    start, swapped = lax.optimization_barrier(((upper, lower), swapped))

    def part_of(rows, hop):
        pieces = 1 if 0 < hop < chips - SPLIT_HOPS else 2
        return expert_part(my_index, rows, hits, own, swapped, hop, chips, pieces)

    def move(blocks):
        return tuple(lax.ppermute(x, "ctx", route) for x in blocks)

    def after(blocks, first):
        return tuple(lax.optimization_barrier((x, first))[0] for x in blocks)

    rows = [start]
    for hop in range(1, min(4, chips)):
        last = rows[-1]
        rows.append(move((jnp.concatenate(last, axis=0),) if hop == 3 else last))
    def added(part, arrived):
        if len(part) > len(arrived):
            arrived = (arrived[0][: tok // 2], arrived[0][tok // 2 :])
        return tuple(x + y.astype(jnp.float32) for x, y in zip(part, arrived))

    def rounded(part):
        return tuple(x.astype(jnp.bfloat16) for x in part)

    sums = rounded(part_of(rows[1], 1))
    for hop in range(1, chips):
        arrived = move(sums)
        if hop + 3 < chips:
            rows.append(move(after(rows[hop + 2], sums)))
        if hop + 1 < chips:
            sums = rounded(added(part_of(rows[hop + 1], hop + 1), arrived))
    expert_out = jnp.concatenate(added(part_of(after(start, sums), 0), arrived), axis=0)
    gate_weight = gate_fixed.astype(jnp.float32) / 65536.0
    return (values.astype(jnp.float32) + gate_weight * expert_out).astype(jnp.bfloat16)


def solution(mesh):
    in_specs = (
        P(("rep", "ctx"), None),
        P(("rep", "ctx"), None),
        P(("rep", "ctx"), None),
        P(("rep", "ctx"), None),
        P(),
        P(),
        P(("rep", "ctx"), None),
        P(("rep", "ctx"), None),
        P("ctx", None, None),
        P("ctx", None, None),
        P("ctx", None, None),
    )
    out_specs = P(("rep", "ctx"), None)
    return jax.shard_map(local, mesh=mesh, in_specs=in_specs, out_specs=out_specs, check_vma=False)
```

```python
import functools
import math

import jax
import jax.numpy as jnp
from jax import lax
from jax.experimental import pallas as pl
from jax.experimental.pallas import tpu as pltpu
from jax.sharding import PartitionSpec as P

HEADS = 32
LAT = 512
ROPE = 64
VD = 128
SPAN = 8
CORES = 2

SCORE_SCALE = 192.0 ** (-0.5)
NORM_EPS = 1e-06
NEG_FILL = -1e30

HEAD_GROUP = 16
SUB_HEADS = 4
PIECES = 2
LOG2_SCALE = SCORE_SCALE * math.log2(math.e)


def attention_kernel(
    index_ref, q_ref, qr_ref, mine_ref, other_ref, wv_ref, gain_ref, values_ref, normed_ref,
    up_ref, down_ref, hits_ref, stack_ref, bias_a_ref, bias_b_ref, *, tok,
):
    group = pl.program_id(0)
    my_index = index_ref[0]
    my_chip, my_core = my_index // CORES, lax.rem(my_index, CORES)
    keys = mine_ref.shape[0]

    @pl.when(group == 0)
    def _():
        row_pos = my_index * tok + lax.broadcasted_iota(jnp.int32, (tok, keys), 0)
        key_iota = lax.broadcasted_iota(jnp.int32, (tok, keys), 1)
        key_chip = (key_iota // tok) ^ my_chip
        key_tok = lax.rem(key_iota, jnp.int32(tok))
        for core, bias_ref in ((my_core, bias_a_ref), (1 - my_core, bias_b_ref)):
            key_pos = (key_chip * CORES + core) * tok + key_tok
            bias_ref[...] = jnp.where(key_pos <= row_pos, 0.0, NEG_FILL)
        last = mine_ref[:, LAT : LAT + 2 * ROPE].astype(jnp.float32)
        lane = lax.broadcasted_iota(jnp.int32, last.shape, 1)
        named = jnp.max(jnp.where(lane >= ROPE, last, -1.0), axis=1, keepdims=True)
        my_expert = (my_index // SPAN).astype(jnp.float32)
        hits = jnp.where(named == my_expert, 1.0, 0.0)
        column = lax.broadcasted_iota(jnp.int32, hits_ref.shape, 1)
        table = jnp.zeros(hits_ref.shape, jnp.float32)
        for place in range(keys // tok):
            table = jnp.where(column == place, hits[place * tok : (place + 1) * tok], table)
        hits_ref[...] = table

    lane = lax.broadcasted_iota(jnp.int32, (tok, 2 * ROPE), 1)
    for head in range(HEAD_GROUP):
        at = pl.ds(head * tok, tok)
        stack_ref[at, 0:LAT] = q_ref[:, head * LAT : (head + 1) * LAT]
        pair = qr_ref[:, (head // 2) * 2 * ROPE : (head // 2 + 1) * 2 * ROPE]
        if head % 2:
            pair = jnp.concatenate([pair[:, ROPE:], pair[:, :ROPE]], axis=1)
        stack_ref[at, LAT : LAT + 2 * ROPE] = jnp.where(lane < ROPE, pair, jnp.zeros_like(pair))

    rows = SUB_HEADS * tok

    def scores_of(sub, keys_ref, bias_ref):
        queries = stack_ref[sub * rows : (sub + 1) * rows, :]
        scores = lax.dot_general(
            queries, keys_ref[...], (((1,), (1,)), ((), ())), preferred_element_type=jnp.float32
        )
        return scores.reshape(SUB_HEADS, tok, keys) * LOG2_SCALE + bias_ref[...][None]

    def both_scores(sub):
        return scores_of(sub, mine_ref, bias_a_ref), scores_of(sub, other_ref, bias_b_ref)

    parts = []
    subs = HEAD_GROUP // SUB_HEADS
    ready = both_scores(0)
    for sub in range(subs):
        scores_a, scores_b = ready
        if sub + 1 < subs:
            ready = both_scores(sub + 1)
        top = jnp.max(jnp.maximum(scores_a, scores_b), axis=2, keepdims=True)
        weights_a = jnp.exp2(scores_a - top)
        weights_b = jnp.exp2(scores_b - top)
        total = jnp.sum(weights_a + weights_b, axis=2, keepdims=True)
        mixed = jnp.dot(
            weights_a.astype(jnp.bfloat16).reshape(rows, keys), mine_ref[:, 0:LAT],
            preferred_element_type=jnp.float32,
        ) + jnp.dot(
            weights_b.astype(jnp.bfloat16).reshape(rows, keys), other_ref[:, 0:LAT],
            preferred_element_type=jnp.float32,
        )
        latent = (mixed.reshape(SUB_HEADS, tok, LAT) / total).astype(jnp.bfloat16)
        for head in range(0, SUB_HEADS, 2):
            first = sub * SUB_HEADS + head
            pair = jnp.dot(
                latent[head : head + 2].reshape(2 * tok, LAT),
                jnp.concatenate([wv_ref[first], wv_ref[first + 1]], axis=1),
                preferred_element_type=jnp.float32,
            ).astype(jnp.bfloat16)
            parts.extend([pair[:tok, :VD], pair[tok:, VD:]])
    wide = HEAD_GROUP * VD
    values_ref[:, pl.ds(pl.multiple_of(group * wide, wide), wide)] = jnp.concatenate(parts, axis=1)

    @pl.when(group == HEADS // HEAD_GROUP - 1)
    def _():
        values = values_ref[...].astype(jnp.float32)
        square = jnp.mean(values * values, axis=1, keepdims=True)
        normed = values * lax.rsqrt(square + NORM_EPS) * gain_ref[...]
        normed = normed.astype(jnp.bfloat16)
        normed_ref[...] = normed
        up_ref[...] = normed[: tok // 2]
        down_ref[...] = normed[tok // 2 :]


def attention(my_index, q_nope, q_rope, mine, other, w_value, norm_gain):
    tok = q_nope.shape[0]
    total = mine.shape[0]
    rows = HEAD_GROUP * tok
    grid_spec = pltpu.PrefetchScalarGridSpec(
        num_scalar_prefetch=1,
        grid=(HEADS // HEAD_GROUP,),
        in_specs=[
            pl.BlockSpec((tok, HEAD_GROUP * LAT), lambda g, i: (0, g)),
            pl.BlockSpec((tok, HEAD_GROUP * ROPE), lambda g, i: (0, g)),
            pl.BlockSpec(mine.shape, lambda g, i: (0, 0)),
            pl.BlockSpec(mine.shape, lambda g, i: (0, 0)),
            pl.BlockSpec((HEAD_GROUP, LAT, VD), lambda g, i: (g, 0, 0)),
            pl.BlockSpec((1, HEADS * VD), lambda g, i: (0, 0)),
        ],
        out_specs=[
            pl.BlockSpec((tok, HEADS * VD), lambda g, i: (0, 0)),
            pl.BlockSpec((tok, HEADS * VD), lambda g, i: (0, 0)),
            pl.BlockSpec((tok // 2, HEADS * VD), lambda g, i: (0, 0)),
            pl.BlockSpec((tok // 2, HEADS * VD), lambda g, i: (0, 0)),
            pl.BlockSpec((tok, total // tok), lambda g, i: (0, 0)),
        ],
        scratch_shapes=[
            pltpu.VMEM((rows, LAT + 2 * ROPE), jnp.bfloat16),
            pltpu.VMEM((tok, total), jnp.float32),
            pltpu.VMEM((tok, total), jnp.float32),
        ],
    )
    shape = jax.ShapeDtypeStruct((tok, HEADS * VD), jnp.bfloat16)
    half_shape = jax.ShapeDtypeStruct((tok // 2, HEADS * VD), jnp.bfloat16)
    hits_shape = jax.ShapeDtypeStruct((tok, total // tok), jnp.float32)
    work = HEADS * tok * total * CORES
    return pl.pallas_call(
        functools.partial(attention_kernel, tok=tok),
        grid_spec=grid_spec,
        out_shape=[shape, shape, half_shape, half_shape, hits_shape],
        compiler_params=pltpu.CompilerParams(vmem_limit_bytes=56 << 20),
        cost_estimate=pl.CostEstimate(
            flops=2 * work * (2 * LAT + 2 * ROPE), bytes_accessed=8 << 20, transcendentals=work
        ),
    )(my_index.reshape(1), q_nope, q_rope, mine, other, w_value, norm_gain.reshape(1, HEADS * VD))


def ring_place(chip, chips):
    return jnp.where(chip % 2 == 0, chip // 2, chips - 1 - chip // 2)


def ring_chip(place, chips):
    return jnp.where(place < chips // 2, 2 * place, 2 * (chips - 1 - place) + 1)


def expert_kernel(
    index_ref, gate_a, up_a, down_a, hits_hbm, gate_hbm, up_hbm, down_hbm, *refs, hop, chips,
):
    *refs, hits_ref, gate_b, up_b, down_b, sems = refs
    rows_refs, out_refs = refs[:-PIECES], refs[-PIECES:]
    pairs = ((hits_hbm, hits_ref), (gate_hbm, gate_b), (up_hbm, up_b), (down_hbm, down_b))
    copies = [
        pltpu.make_async_copy(there, here, sems.at[i]) for i, (there, here) in enumerate(pairs)
    ]
    for copy in copies:
        copy.start()
    my_chip, my_core = index_ref[0] // CORES, lax.rem(index_ref[0], CORES)
    place = ring_place(my_chip, chips) + chips + hop * (2 * my_core - 1)
    source = ring_chip(lax.rem(place, chips), chips) ^ my_chip
    rows = jnp.concatenate([ref[...] for ref in rows_refs], axis=0)

    def hidden(gate_ref, up_ref):
        gate_act = jnp.dot(rows, gate_ref[...], preferred_element_type=jnp.float32)
        up_act = jnp.dot(rows, up_ref[...], preferred_element_type=jnp.float32)
        return gate_act * (1.0 / (1.0 + jnp.exp(-gate_act))) * up_act

    def kept(act):
        return jnp.where(keep, act, 0.0).astype(jnp.bfloat16)

    act_a = hidden(gate_a, up_a)
    copies[0].wait()
    column = lax.broadcasted_iota(jnp.int32, hits_ref.shape, 1)
    keep = jnp.max(jnp.where(column == source, hits_ref[...], 0.0), axis=1, keepdims=True) > 0.0
    part = jnp.dot(kept(act_a), down_a[...], preferred_element_type=jnp.float32)
    copies[1].wait()
    copies[2].wait()
    act_b = hidden(gate_b, up_b)
    copies[3].wait()
    part = part + jnp.dot(kept(act_b), down_b[...], preferred_element_type=jnp.float32)
    size = part.shape[0] // PIECES
    for i, out_ref in enumerate(out_refs):
        out_ref[...] = part[i * size : (i + 1) * size]


def expert_part(my_index, rows, hits, own, swapped, hop, chips):
    tok, features = hits.shape[0], rows[0].shape[1]
    units = 2 * own[0].shape[1]
    vmem, anywhere = pl.BlockSpec(memory_space=pltpu.VMEM), pl.BlockSpec(memory_space=pl.ANY)
    return pl.pallas_call(
        functools.partial(expert_kernel, hop=hop, chips=chips),
        in_specs=[pl.BlockSpec(memory_space=pltpu.SMEM)] + [vmem] * 3 + [anywhere] * 4 + [vmem] * len(rows),
        out_specs=[vmem] * PIECES,
        out_shape=[jax.ShapeDtypeStruct((tok // PIECES, features), jnp.float32)] * PIECES,
        scratch_shapes=[pltpu.VMEM(w.shape, w.dtype) for w in (hits, *swapped)]
        + [pltpu.SemaphoreType.DMA((4,))],
        compiler_params=pltpu.CompilerParams(vmem_limit_bytes=24 << 20),
        cost_estimate=pl.CostEstimate(
            flops=6 * tok * features * units, bytes_accessed=14 << 20, transcendentals=0
        ),
    )(my_index.reshape(1), *own, hits, *swapped, *rows)


def local(
    q_nope, q_rope, c_kv, k_rope, w_value, norm_gain, expert_ids, gate_fixed, w_gate, w_up, w_down
):
    tok = c_kv.shape[0]
    n_ctx = lax.axis_size("ctx")
    chips = n_ctx // CORES
    my_index = lax.axis_index("ctx")
    siblings = [(i, i ^ 1) for i in range(n_ctx)]
    ring = list(range(0, chips, 2)) + list(range(1, chips, 2))[::-1]
    route = [
        (ring[p] * CORES + core, ring[(p + 1 - 2 * core) % chips] * CORES + core)
        for p in range(chips) for core in range(CORES)
    ]
    back = [(there, here) for here, there in route]

    def from_chip(block, step):
        return lax.ppermute(block, "ctx", [(i, i ^ (step * CORES)) for i in range(n_ctx)])

    ids = jnp.broadcast_to(expert_ids.astype(jnp.bfloat16), (tok, ROPE))
    block = jnp.concatenate([c_kv, k_rope, ids], axis=1)
    across = from_chip(block, chips // 2)
    near = [block] + [from_chip(block, step) for step in range(1, chips // 2)]
    far = [across] + [from_chip(across, step) for step in range(1, chips // 2)]
    mine = jnp.concatenate(near + far, axis=0)
    other = lax.ppermute(mine, "ctx", siblings)

    own, mine, other = lax.optimization_barrier(((w_gate[0], w_up[0], w_down[0]), mine, other))
    swapped = tuple(lax.ppermute(w, "ctx", siblings) for w in own)
    values, normed, upper, lower, hits = attention(
        my_index, q_nope, q_rope, mine, other, w_value, norm_gain
    )
    start, normed, swapped = lax.optimization_barrier(((upper, lower), normed, swapped))

    def part_of(rows, hop):
        return expert_part(my_index, rows, hits, own, swapped, hop, chips)

    def move(blocks, way=route):
        return tuple(lax.ppermute(x, "ctx", way) for x in blocks)

    def after(blocks, first):
        return tuple(lax.optimization_barrier((x, first))[0] for x in blocks)

    rows = {0: start, 1: move(start)}
    rows[2] = move(rows[1])
    joined = (jnp.concatenate(rows[2], axis=0),)
    if chips == 8:
        rows[7] = move(after((normed,), rows[1][-1]), back)
        plan = {1: [(6, 7, back)], 2: [(4, 3, route)], 3: [(5, 6, back)]}
        needs = {2: 7, 4: 6}
    else:
        plan = {hop: [(hop + 3, hop + 2, route)] for hop in range(1, chips - 3)}
        needs = {}
    rows[3] = move(joined)

    def added(part, arrived):
        return tuple(x + y.astype(jnp.float32) for x, y in zip(part, arrived))

    def rounded(part):
        return tuple(x.astype(jnp.bfloat16) for x in part)

    sums = rounded(part_of(rows[1], 1))
    for hop in range(1, chips):
        arrived = move(sums)
        for into, source, way in plan.get(hop, []):
            rows[into] = move(after(rows[source], sums[0]), way)
        if hop + 1 < chips:
            taken = rows[hop + 1]
            if hop + 1 in needs:
                taken = after(taken, rows[needs[hop + 1]][0])
            sums = rounded(added(part_of(taken, hop + 1), arrived))
    expert_out = jnp.concatenate(added(part_of(after(start, sums), 0), arrived), axis=0)
    gate_weight = gate_fixed.astype(jnp.float32) / 65536.0
    return (values.astype(jnp.float32) + gate_weight * expert_out).astype(jnp.bfloat16)


def solution(mesh):
    in_specs = (
        P(("rep", "ctx"), None),
        P(("rep", "ctx"), None),
        P(("rep", "ctx"), None),
        P(("rep", "ctx"), None),
        P(),
        P(),
        P(("rep", "ctx"), None),
        P(("rep", "ctx"), None),
        P("ctx", None, None),
        P("ctx", None, None),
        P("ctx", None, None),
    )
    out_specs = P(("rep", "ctx"), None)
    return jax.shard_map(local, mesh=mesh, in_specs=in_specs, out_specs=out_specs, check_vma=False)
```

```python
import functools
import math

import jax
import jax.numpy as jnp
from jax import lax
from jax.experimental import pallas as pl
from jax.experimental.pallas import tpu as pltpu
from jax.sharding import PartitionSpec as P

HEADS = 32
LAT = 512
ROPE = 64
VD = 128
SPAN = 8
CORES = 2

SCORE_SCALE = 192.0 ** (-0.5)
NORM_EPS = 1e-06
NEG_FILL = -1e30

HEAD_GROUP = 16
SUB_HEADS = 4
PIECES = 2
LOG2_SCALE = SCORE_SCALE * math.log2(math.e)


def attention_kernel(
    index_ref, q_ref, qr_ref, mine_ref, other_ref, wv_ref, gain_ref, values_ref, normed_ref,
    up_ref, down_ref, hits_ref, stack_ref, bias_a_ref, bias_b_ref, *, tok,
):
    group = pl.program_id(0)
    my_index = index_ref[0]
    my_chip, my_core = my_index // CORES, lax.rem(my_index, CORES)
    keys = mine_ref.shape[0]

    @pl.when(group == 0)
    def _():
        row_pos = my_index * tok + lax.broadcasted_iota(jnp.int32, (tok, keys), 0)
        key_iota = lax.broadcasted_iota(jnp.int32, (tok, keys), 1)
        key_chip = (key_iota // tok) ^ my_chip
        key_tok = lax.rem(key_iota, jnp.int32(tok))
        for core, bias_ref in ((my_core, bias_a_ref), (1 - my_core, bias_b_ref)):
            key_pos = (key_chip * CORES + core) * tok + key_tok
            bias_ref[...] = jnp.where(key_pos <= row_pos, 0.0, NEG_FILL)
        last = mine_ref[:, LAT : LAT + 2 * ROPE].astype(jnp.float32)
        lane = lax.broadcasted_iota(jnp.int32, last.shape, 1)
        named = jnp.max(jnp.where(lane >= ROPE, last, -1.0), axis=1, keepdims=True)
        my_expert = (my_index // SPAN).astype(jnp.float32)
        hits = jnp.where(named == my_expert, 1.0, 0.0)
        column = lax.broadcasted_iota(jnp.int32, hits_ref.shape, 1)
        table = jnp.zeros(hits_ref.shape, jnp.float32)
        for place in range(keys // tok):
            table = jnp.where(column == place, hits[place * tok : (place + 1) * tok], table)
        hits_ref[...] = table

    lane = lax.broadcasted_iota(jnp.int32, (tok, 2 * ROPE), 1)
    for head in range(HEAD_GROUP):
        at = pl.ds(head * tok, tok)
        stack_ref[at, 0:LAT] = q_ref[:, head * LAT : (head + 1) * LAT]
        pair = qr_ref[:, (head // 2) * 2 * ROPE : (head // 2 + 1) * 2 * ROPE]
        if head % 2:
            pair = jnp.concatenate([pair[:, ROPE:], pair[:, :ROPE]], axis=1)
        stack_ref[at, LAT : LAT + 2 * ROPE] = jnp.where(lane < ROPE, pair, jnp.zeros_like(pair))

    rows = SUB_HEADS * tok

    def scores_of(sub, keys_ref, bias_ref):
        queries = stack_ref[sub * rows : (sub + 1) * rows, :]
        scores = lax.dot_general(
            queries, keys_ref[...], (((1,), (1,)), ((), ())), preferred_element_type=jnp.float32
        )
        return scores.reshape(SUB_HEADS, tok, keys) * LOG2_SCALE + bias_ref[...][None]

    def both_scores(sub):
        return scores_of(sub, mine_ref, bias_a_ref), scores_of(sub, other_ref, bias_b_ref)

    parts = []
    subs = HEAD_GROUP // SUB_HEADS
    ready = both_scores(0)
    for sub in range(subs):
        scores_a, scores_b = ready
        if sub + 1 < subs:
            ready = both_scores(sub + 1)
        top = jnp.max(jnp.maximum(scores_a, scores_b), axis=2, keepdims=True)
        weights_a = jnp.exp2(scores_a - top)
        weights_b = jnp.exp2(scores_b - top)
        total = jnp.sum(weights_a + weights_b, axis=2, keepdims=True)
        mixed = jnp.dot(
            weights_a.astype(jnp.bfloat16).reshape(rows, keys), mine_ref[:, 0:LAT],
            preferred_element_type=jnp.float32,
        ) + jnp.dot(
            weights_b.astype(jnp.bfloat16).reshape(rows, keys), other_ref[:, 0:LAT],
            preferred_element_type=jnp.float32,
        )
        latent = (mixed.reshape(SUB_HEADS, tok, LAT) / total).astype(jnp.bfloat16)
        for head in range(0, SUB_HEADS, 2):
            first = sub * SUB_HEADS + head
            pair = jnp.dot(
                latent[head : head + 2].reshape(2 * tok, LAT),
                jnp.concatenate([wv_ref[first], wv_ref[first + 1]], axis=1),
                preferred_element_type=jnp.float32,
            ).astype(jnp.bfloat16)
            parts.extend([pair[:tok, :VD], pair[tok:, VD:]])
    wide = HEAD_GROUP * VD
    values_ref[:, pl.ds(pl.multiple_of(group * wide, wide), wide)] = jnp.concatenate(parts, axis=1)

    @pl.when(group == HEADS // HEAD_GROUP - 1)
    def _():
        values = values_ref[...].astype(jnp.float32)
        square = jnp.mean(values * values, axis=1, keepdims=True)
        normed = values * lax.rsqrt(square + NORM_EPS) * gain_ref[...]
        normed = normed.astype(jnp.bfloat16)
        normed_ref[...] = normed
        up_ref[...] = normed[: tok // 2]
        down_ref[...] = normed[tok // 2 :]


def attention(my_index, q_nope, q_rope, mine, other, w_value, norm_gain):
    tok = q_nope.shape[0]
    total = mine.shape[0]
    rows = HEAD_GROUP * tok
    grid_spec = pltpu.PrefetchScalarGridSpec(
        num_scalar_prefetch=1,
        grid=(HEADS // HEAD_GROUP,),
        in_specs=[
            pl.BlockSpec((tok, HEAD_GROUP * LAT), lambda g, i: (0, g)),
            pl.BlockSpec((tok, HEAD_GROUP * ROPE), lambda g, i: (0, g)),
            pl.BlockSpec(mine.shape, lambda g, i: (0, 0)),
            pl.BlockSpec(mine.shape, lambda g, i: (0, 0)),
            pl.BlockSpec((HEAD_GROUP, LAT, VD), lambda g, i: (g, 0, 0)),
            pl.BlockSpec((1, HEADS * VD), lambda g, i: (0, 0)),
        ],
        out_specs=[
            pl.BlockSpec((tok, HEADS * VD), lambda g, i: (0, 0)),
            pl.BlockSpec((tok, HEADS * VD), lambda g, i: (0, 0)),
            pl.BlockSpec((tok // 2, HEADS * VD), lambda g, i: (0, 0)),
            pl.BlockSpec((tok // 2, HEADS * VD), lambda g, i: (0, 0)),
            pl.BlockSpec((tok, total // tok), lambda g, i: (0, 0)),
        ],
        scratch_shapes=[
            pltpu.VMEM((rows, LAT + 2 * ROPE), jnp.bfloat16),
            pltpu.VMEM((tok, total), jnp.float32),
            pltpu.VMEM((tok, total), jnp.float32),
        ],
    )
    shape = jax.ShapeDtypeStruct((tok, HEADS * VD), jnp.bfloat16)
    half_shape = jax.ShapeDtypeStruct((tok // 2, HEADS * VD), jnp.bfloat16)
    hits_shape = jax.ShapeDtypeStruct((tok, total // tok), jnp.float32)
    work = HEADS * tok * total * CORES
    return pl.pallas_call(
        functools.partial(attention_kernel, tok=tok),
        grid_spec=grid_spec,
        out_shape=[shape, shape, half_shape, half_shape, hits_shape],
        compiler_params=pltpu.CompilerParams(vmem_limit_bytes=56 << 20),
        cost_estimate=pl.CostEstimate(
            flops=2 * work * (2 * LAT + 2 * ROPE), bytes_accessed=8 << 20, transcendentals=work
        ),
    )(my_index.reshape(1), q_nope, q_rope, mine, other, w_value, norm_gain.reshape(1, HEADS * VD))


def ring_place(chip, chips):
    return jnp.where(chip % 2 == 0, chip // 2, chips - 1 - chip // 2)


def ring_chip(place, chips):
    return jnp.where(place < chips // 2, 2 * place, 2 * (chips - 1 - place) + 1)


def expert_kernel(
    index_ref, gate_a, up_a, down_a, hits_hbm, gate_hbm, up_hbm, down_hbm, *refs, hops, chips,
):
    *refs, hits_ref, gate_b, up_b, down_b, sems = refs
    outs = PIECES * len(hops)
    rows_refs, out_refs = refs[:-outs], refs[-outs:]
    pairs = ((hits_hbm, hits_ref), (gate_hbm, gate_b), (up_hbm, up_b), (down_hbm, down_b))
    copies = [
        pltpu.make_async_copy(there, here, sems.at[i]) for i, (there, here) in enumerate(pairs)
    ]
    for copy in copies:
        copy.start()
    my_chip, my_core = index_ref[0] // CORES, lax.rem(index_ref[0], CORES)
    rows = jnp.concatenate([ref[...] for ref in rows_refs], axis=0)

    def hit(hop):
        place = ring_place(my_chip, chips) + chips + hop * (2 * my_core - 1)
        source = ring_chip(lax.rem(place, chips), chips) ^ my_chip
        column = lax.broadcasted_iota(jnp.int32, hits_ref.shape, 1)
        return jnp.max(jnp.where(column == source, hits_ref[...], 0.0), axis=1, keepdims=True)

    def hidden(gate_ref, up_ref):
        gate_act = jnp.dot(rows, gate_ref[...], preferred_element_type=jnp.float32)
        up_act = jnp.dot(rows, up_ref[...], preferred_element_type=jnp.float32)
        return gate_act * (1.0 / (1.0 + jnp.exp(-gate_act))) * up_act

    def kept(act):
        return jnp.where(keep, act, 0.0).astype(jnp.bfloat16)

    act_a = hidden(gate_a, up_a)
    copies[0].wait()
    keep = jnp.concatenate([hit(hop) for hop in hops], axis=0) > 0.0
    part = jnp.dot(kept(act_a), down_a[...], preferred_element_type=jnp.float32)
    copies[1].wait()
    copies[2].wait()
    act_b = hidden(gate_b, up_b)
    copies[3].wait()
    part = part + jnp.dot(kept(act_b), down_b[...], preferred_element_type=jnp.float32)
    size = part.shape[0] // outs
    for i, out_ref in enumerate(out_refs):
        out_ref[...] = part[i * size : (i + 1) * size]


def expert_parts(my_index, rows, hits, own, swapped, hops, chips):
    tok, features = hits.shape[0], rows[0].shape[1]
    units = 2 * own[0].shape[1]
    outs = PIECES * len(hops)
    vmem, anywhere = pl.BlockSpec(memory_space=pltpu.VMEM), pl.BlockSpec(memory_space=pl.ANY)
    parts = pl.pallas_call(
        functools.partial(expert_kernel, hops=hops, chips=chips),
        in_specs=[pl.BlockSpec(memory_space=pltpu.SMEM)]
        + [vmem] * 3 + [anywhere] * 4 + [vmem] * len(rows),
        out_specs=[vmem] * outs,
        out_shape=[jax.ShapeDtypeStruct((tok // PIECES, features), jnp.float32)] * outs,
        scratch_shapes=[pltpu.VMEM(w.shape, w.dtype) for w in (hits, *swapped)]
        + [pltpu.SemaphoreType.DMA((4,))],
        compiler_params=pltpu.CompilerParams(vmem_limit_bytes=28 << 20),
        cost_estimate=pl.CostEstimate(
            flops=6 * tok * features * units, bytes_accessed=14 << 20, transcendentals=0
        ),
    )(my_index.reshape(1), *own, hits, *swapped, *rows)
    return [tuple(parts[i : i + PIECES]) for i in range(0, outs, PIECES)]


def local(
    q_nope, q_rope, c_kv, k_rope, w_value, norm_gain, expert_ids, gate_fixed, w_gate, w_up, w_down
):
    tok = c_kv.shape[0]
    n_ctx = lax.axis_size("ctx")
    chips = n_ctx // CORES
    my_index = lax.axis_index("ctx")
    siblings = [(i, i ^ 1) for i in range(n_ctx)]
    ring = list(range(0, chips, 2)) + list(range(1, chips, 2))[::-1]
    route = [
        (ring[p] * CORES + core, ring[(p + 1 - 2 * core) % chips] * CORES + core)
        for p in range(chips) for core in range(CORES)
    ]
    back = [(there, here) for here, there in route]

    def from_chip(block, step):
        return lax.ppermute(block, "ctx", [(i, i ^ (step * CORES)) for i in range(n_ctx)])

    ids = jnp.broadcast_to(expert_ids.astype(jnp.bfloat16), (tok, ROPE))
    block = jnp.concatenate([c_kv, k_rope, ids], axis=1)
    across = from_chip(block, chips // 2)
    near = [block] + [from_chip(block, step) for step in range(1, chips // 2)]
    far = [across] + [from_chip(across, step) for step in range(1, chips // 2)]
    mine = jnp.concatenate(near + far, axis=0)
    other = lax.ppermute(mine, "ctx", siblings)

    own, mine, other = lax.optimization_barrier(((w_gate[0], w_up[0], w_down[0]), mine, other))
    swapped = tuple(lax.ppermute(w, "ctx", siblings) for w in own)
    values, normed, upper, lower, hits = attention(
        my_index, q_nope, q_rope, mine, other, w_value, norm_gain
    )
    start, normed, swapped = lax.optimization_barrier(((upper, lower), normed, swapped))

    def parts_of(rows, hops):
        blocks = [block for hop in hops for block in rows[hop]]
        return expert_parts(my_index, blocks, hits, own, swapped, hops, chips)

    def move(blocks, way=route):
        return tuple(lax.ppermute(x, "ctx", way) for x in blocks)

    def after(blocks, first):
        return tuple(lax.optimization_barrier((x, first))[0] for x in blocks)

    def added(part, arrived):
        return tuple(x + y.astype(jnp.float32) for x, y in zip(part, arrived))

    def rounded(part):
        return tuple(x.astype(jnp.bfloat16) for x in part)

    turn = chips // 2
    rows = {0: start, 1: move(start)}
    rows[2] = move(rows[1])
    rows[chips - 1] = move(after((normed,), rows[1][-1]), back)
    rows[3] = move((jnp.concatenate(rows[2], axis=0),))
    parts = dict(zip((1,), parts_of(rows, (1,))))
    sums = rounded(parts[1])
    for hop in range(1, chips):
        arrived = move(sums)
        here, there = hop + 1, chips - hop
        if here <= turn:
            if 3 < here + 1 <= turn:
                rows[here + 1] = move(after(rows[here], sums[0]))
            if here < turn:
                rows[there - 1] = move(after(rows[there], sums[0]), back)
            hops = (here, there, 0) if hop == 1 else (here, there)
            parts.update(zip(hops, parts_of(rows, hops)))
        if here < chips:
            sums = rounded(added(parts[here], arrived))
    expert_out = jnp.concatenate(added(parts[0], arrived), axis=0)
    gate_weight = gate_fixed.astype(jnp.float32) / 65536.0
    return (values.astype(jnp.float32) + gate_weight * expert_out).astype(jnp.bfloat16)


def solution(mesh):
    in_specs = (
        P(("rep", "ctx"), None),
        P(("rep", "ctx"), None),
        P(("rep", "ctx"), None),
        P(("rep", "ctx"), None),
        P(),
        P(),
        P(("rep", "ctx"), None),
        P(("rep", "ctx"), None),
        P("ctx", None, None),
        P("ctx", None, None),
        P("ctx", None, None),
    )
    out_specs = P(("rep", "ctx"), None)
    return jax.shard_map(local, mesh=mesh, in_specs=in_specs, out_specs=out_specs, check_vma=False)
```

```python
import functools
import math

import jax
import jax.numpy as jnp
from jax import lax
from jax.experimental import pallas as pl
from jax.experimental.pallas import tpu as pltpu
from jax.sharding import PartitionSpec as P

HEADS = 32
LAT = 512
ROPE = 64
VD = 128
SPAN = 8
CORES = 2

SCORE_SCALE = 192.0 ** (-0.5)
NORM_EPS = 1e-06
NEG_FILL = -1e30

HEAD_GROUP = 16
SUB_HEADS = 4
PIECES = 2
LOG2_SCALE = SCORE_SCALE * math.log2(math.e)


def attention_kernel(
    index_ref, q_ref, qr_ref, mine_ref, other_ref, wv_ref, gain_ref, values_ref, normed_ref,
    up_ref, down_ref, hits_ref, stack_ref, bias_a_ref, bias_b_ref, *, tok,
):
    group = pl.program_id(0)
    my_index = index_ref[0]
    my_chip, my_core = my_index // CORES, lax.rem(my_index, CORES)
    keys = mine_ref.shape[0]

    @pl.when(group == 0)
    def _():
        row_pos = my_index * tok + lax.broadcasted_iota(jnp.int32, (tok, keys), 0)
        key_iota = lax.broadcasted_iota(jnp.int32, (tok, keys), 1)
        key_chip = (key_iota // tok) ^ my_chip
        key_tok = lax.rem(key_iota, jnp.int32(tok))
        for core, bias_ref in ((my_core, bias_a_ref), (1 - my_core, bias_b_ref)):
            key_pos = (key_chip * CORES + core) * tok + key_tok
            bias_ref[...] = jnp.where(key_pos <= row_pos, 0.0, NEG_FILL)
        last = mine_ref[:, LAT : LAT + 2 * ROPE].astype(jnp.float32)
        lane = lax.broadcasted_iota(jnp.int32, last.shape, 1)
        named = jnp.max(jnp.where(lane >= ROPE, last, -1.0), axis=1, keepdims=True)
        my_expert = (my_index // SPAN).astype(jnp.float32)
        hits = jnp.where(named == my_expert, 1.0, 0.0)
        column = lax.broadcasted_iota(jnp.int32, hits_ref.shape, 1)
        table = jnp.zeros(hits_ref.shape, jnp.float32)
        for place in range(keys // tok):
            table = jnp.where(column == place, hits[place * tok : (place + 1) * tok], table)
        hits_ref[...] = table

    lane = lax.broadcasted_iota(jnp.int32, (tok, 2 * ROPE), 1)
    for head in range(HEAD_GROUP):
        at = pl.ds(head * tok, tok)
        stack_ref[at, 0:LAT] = q_ref[:, head * LAT : (head + 1) * LAT]
        pair = qr_ref[:, (head // 2) * 2 * ROPE : (head // 2 + 1) * 2 * ROPE]
        if head % 2:
            pair = jnp.concatenate([pair[:, ROPE:], pair[:, :ROPE]], axis=1)
        stack_ref[at, LAT : LAT + 2 * ROPE] = jnp.where(lane < ROPE, pair, jnp.zeros_like(pair))

    rows = SUB_HEADS * tok

    def scores_of(sub, keys_ref, bias_ref):
        queries = stack_ref[sub * rows : (sub + 1) * rows, :]
        scores = lax.dot_general(
            queries, keys_ref[...], (((1,), (1,)), ((), ())), preferred_element_type=jnp.float32
        )
        return scores.reshape(SUB_HEADS, tok, keys) * LOG2_SCALE + bias_ref[...][None]

    def both_scores(sub):
        return scores_of(sub, mine_ref, bias_a_ref), scores_of(sub, other_ref, bias_b_ref)

    parts = []
    subs = HEAD_GROUP // SUB_HEADS
    ready = both_scores(0)
    for sub in range(subs):
        scores_a, scores_b = ready
        if sub + 1 < subs:
            ready = both_scores(sub + 1)
        top = jnp.max(jnp.maximum(scores_a, scores_b), axis=2, keepdims=True)
        weights_a = jnp.exp2(scores_a - top)
        weights_b = jnp.exp2(scores_b - top)
        total = jnp.sum(weights_a + weights_b, axis=2, keepdims=True)
        mixed = jnp.dot(
            weights_a.astype(jnp.bfloat16).reshape(rows, keys), mine_ref[:, 0:LAT],
            preferred_element_type=jnp.float32,
        ) + jnp.dot(
            weights_b.astype(jnp.bfloat16).reshape(rows, keys), other_ref[:, 0:LAT],
            preferred_element_type=jnp.float32,
        )
        latent = (mixed.reshape(SUB_HEADS, tok, LAT) / total).astype(jnp.bfloat16)
        for head in range(0, SUB_HEADS, 2):
            first = sub * SUB_HEADS + head
            pair = jnp.dot(
                latent[head : head + 2].reshape(2 * tok, LAT),
                jnp.concatenate([wv_ref[first], wv_ref[first + 1]], axis=1),
                preferred_element_type=jnp.float32,
            ).astype(jnp.bfloat16)
            parts.extend([pair[:tok, :VD], pair[tok:, VD:]])
    wide = HEAD_GROUP * VD
    values_ref[:, pl.ds(pl.multiple_of(group * wide, wide), wide)] = jnp.concatenate(parts, axis=1)

    @pl.when(group == HEADS // HEAD_GROUP - 1)
    def _():
        values = values_ref[...].astype(jnp.float32)
        square = jnp.mean(values * values, axis=1, keepdims=True)
        normed = values * lax.rsqrt(square + NORM_EPS) * gain_ref[...]
        normed = normed.astype(jnp.bfloat16)
        normed_ref[...] = normed
        up_ref[...] = normed[: tok // 2]
        down_ref[...] = normed[tok // 2 :]


def attention(my_index, q_nope, q_rope, mine, other, w_value, norm_gain):
    tok = q_nope.shape[0]
    total = mine.shape[0]
    rows = HEAD_GROUP * tok
    grid_spec = pltpu.PrefetchScalarGridSpec(
        num_scalar_prefetch=1,
        grid=(HEADS // HEAD_GROUP,),
        in_specs=[
            pl.BlockSpec((tok, HEAD_GROUP * LAT), lambda g, i: (0, g)),
            pl.BlockSpec((tok, HEAD_GROUP * ROPE), lambda g, i: (0, g)),
            pl.BlockSpec(mine.shape, lambda g, i: (0, 0)),
            pl.BlockSpec(mine.shape, lambda g, i: (0, 0)),
            pl.BlockSpec((HEAD_GROUP, LAT, VD), lambda g, i: (g, 0, 0)),
            pl.BlockSpec((1, HEADS * VD), lambda g, i: (0, 0)),
        ],
        out_specs=[
            pl.BlockSpec((tok, HEADS * VD), lambda g, i: (0, 0)),
            pl.BlockSpec((tok, HEADS * VD), lambda g, i: (0, 0)),
            pl.BlockSpec((tok // 2, HEADS * VD), lambda g, i: (0, 0)),
            pl.BlockSpec((tok // 2, HEADS * VD), lambda g, i: (0, 0)),
            pl.BlockSpec((tok, total // tok), lambda g, i: (0, 0)),
        ],
        scratch_shapes=[
            pltpu.VMEM((rows, LAT + 2 * ROPE), jnp.bfloat16),
            pltpu.VMEM((tok, total), jnp.float32),
            pltpu.VMEM((tok, total), jnp.float32),
        ],
    )
    shape = jax.ShapeDtypeStruct((tok, HEADS * VD), jnp.bfloat16)
    half_shape = jax.ShapeDtypeStruct((tok // 2, HEADS * VD), jnp.bfloat16)
    hits_shape = jax.ShapeDtypeStruct((tok, total // tok), jnp.float32)
    work = HEADS * tok * total * CORES
    return pl.pallas_call(
        functools.partial(attention_kernel, tok=tok),
        grid_spec=grid_spec,
        out_shape=[shape, shape, half_shape, half_shape, hits_shape],
        compiler_params=pltpu.CompilerParams(vmem_limit_bytes=56 << 20),
        cost_estimate=pl.CostEstimate(
            flops=2 * work * (2 * LAT + 2 * ROPE), bytes_accessed=8 << 20, transcendentals=work
        ),
    )(my_index.reshape(1), q_nope, q_rope, mine, other, w_value, norm_gain.reshape(1, HEADS * VD))


def ring_place(chip, chips):
    return jnp.where(chip % 2 == 0, chip // 2, chips - 1 - chip // 2)


def ring_chip(place, chips):
    return jnp.where(place < chips // 2, 2 * place, 2 * (chips - 1 - place) + 1)


def expert_kernel(
    index_ref, gate_a, up_a, down_a, hits_hbm, gate_hbm, up_hbm, down_hbm, *refs, hops, chips,
):
    *refs, hits_ref, gate_b, up_b, down_b, sems = refs
    outs = PIECES * len(hops)
    rows_refs, out_refs = refs[:-outs], refs[-outs:]
    pairs = ((hits_hbm, hits_ref), (gate_hbm, gate_b), (up_hbm, up_b), (down_hbm, down_b))
    copies = [
        pltpu.make_async_copy(there, here, sems.at[i]) for i, (there, here) in enumerate(pairs)
    ]
    for copy in copies:
        copy.start()
    my_chip, my_core = index_ref[0] // CORES, lax.rem(index_ref[0], CORES)
    rows = jnp.concatenate([ref[...] for ref in rows_refs], axis=0)

    def hit(hop):
        place = ring_place(my_chip, chips) + chips + hop * (2 * my_core - 1)
        source = ring_chip(lax.rem(place, chips), chips) ^ my_chip
        column = lax.broadcasted_iota(jnp.int32, hits_ref.shape, 1)
        return jnp.max(jnp.where(column == source, hits_ref[...], 0.0), axis=1, keepdims=True)

    def hidden(gate_ref, up_ref):
        gate_act = jnp.dot(rows, gate_ref[...], preferred_element_type=jnp.float32)
        up_act = jnp.dot(rows, up_ref[...], preferred_element_type=jnp.float32)
        return gate_act * (1.0 / (1.0 + jnp.exp(-gate_act))) * up_act

    def kept(act):
        return jnp.where(keep, act, 0.0).astype(jnp.bfloat16)

    act_a = hidden(gate_a, up_a)
    copies[0].wait()
    keep = jnp.concatenate([hit(hop) for hop in hops], axis=0) > 0.0
    part = jnp.dot(kept(act_a), down_a[...], preferred_element_type=jnp.float32)
    copies[1].wait()
    copies[2].wait()
    act_b = hidden(gate_b, up_b)
    copies[3].wait()
    part = part + jnp.dot(kept(act_b), down_b[...], preferred_element_type=jnp.float32)
    size = part.shape[0] // outs
    for i, out_ref in enumerate(out_refs):
        out_ref[...] = part[i * size : (i + 1) * size]


def expert_parts(my_index, rows, hits, own, swapped, hops, chips):
    tok, features = hits.shape[0], rows[0].shape[1]
    units = 2 * own[0].shape[1]
    outs = PIECES * len(hops)
    vmem, anywhere = pl.BlockSpec(memory_space=pltpu.VMEM), pl.BlockSpec(memory_space=pl.ANY)
    parts = pl.pallas_call(
        functools.partial(expert_kernel, hops=hops, chips=chips),
        in_specs=[pl.BlockSpec(memory_space=pltpu.SMEM)]
        + [vmem] * 3 + [anywhere] * 4 + [vmem] * len(rows),
        out_specs=[vmem] * outs,
        out_shape=[jax.ShapeDtypeStruct((tok // PIECES, features), jnp.float32)] * outs,
        scratch_shapes=[pltpu.VMEM(w.shape, w.dtype) for w in (hits, *swapped)]
        + [pltpu.SemaphoreType.DMA((4,))],
        compiler_params=pltpu.CompilerParams(vmem_limit_bytes=28 << 20),
        cost_estimate=pl.CostEstimate(
            flops=6 * tok * features * units, bytes_accessed=14 << 20, transcendentals=0
        ),
    )(my_index.reshape(1), *own, hits, *swapped, *rows)
    return [tuple(parts[i : i + PIECES]) for i in range(0, outs, PIECES)]


def local(
    q_nope, q_rope, c_kv, k_rope, w_value, norm_gain, expert_ids, gate_fixed, w_gate, w_up, w_down
):
    tok = c_kv.shape[0]
    n_ctx = lax.axis_size("ctx")
    chips = n_ctx // CORES
    my_index = lax.axis_index("ctx")
    siblings = [(i, i ^ 1) for i in range(n_ctx)]
    ring = list(range(0, chips, 2)) + list(range(1, chips, 2))[::-1]
    route = [
        (ring[p] * CORES + core, ring[(p + 1 - 2 * core) % chips] * CORES + core)
        for p in range(chips) for core in range(CORES)
    ]
    back = [(there, here) for here, there in route]

    def from_chip(block, step):
        return lax.ppermute(block, "ctx", [(i, i ^ (step * CORES)) for i in range(n_ctx)])

    ids = jnp.broadcast_to(expert_ids.astype(jnp.bfloat16), (tok, ROPE))
    block = jnp.concatenate([c_kv, k_rope, ids], axis=1)
    across = from_chip(block, chips // 2)
    near = [block] + [from_chip(block, step) for step in range(1, chips // 2)]
    far = [across] + [from_chip(across, step) for step in range(1, chips // 2)]
    mine = jnp.concatenate(near + far, axis=0)
    other = lax.ppermute(mine, "ctx", siblings)

    own, mine, other = lax.optimization_barrier(((w_gate[0], w_up[0], w_down[0]), mine, other))
    swapped = tuple(lax.ppermute(w, "ctx", siblings) for w in own)
    values, normed, upper, lower, hits = attention(
        my_index, q_nope, q_rope, mine, other, w_value, norm_gain
    )
    start, normed, swapped = lax.optimization_barrier(((upper, lower), normed, swapped))

    def parts_of(rows, hops):
        blocks = [block for hop in hops for block in rows[hop]]
        return expert_parts(my_index, blocks, table, own, swapped, hops, chips)

    def move(blocks, way=route):
        return tuple(lax.ppermute(x, "ctx", way) for x in blocks)

    def after(blocks, first):
        return tuple(lax.optimization_barrier((x, first))[0] for x in blocks)

    def added(part, arrived):
        return tuple(x + y.astype(jnp.float32) for x, y in zip(part, arrived))

    def rounded(part):
        return tuple(x.astype(jnp.bfloat16) for x in part)

    turn = chips // 2
    rows = {0: start, 1: move(start)}
    table = jnp.where(hits > 0.5, 1.0, 0.0)
    rows[2] = move(after(rows[1], table))
    rows[chips - 1] = move(after((normed,), rows[1][-1]), back)
    rows[3] = move((jnp.concatenate(rows[2], axis=0),))
    parts = dict(zip((1,), parts_of(rows, (1,))))
    sums = rounded(parts[1])
    for hop in range(1, chips):
        arrived = move(sums)
        here, there = hop + 1, chips - hop
        if here <= turn:
            if 3 < here + 1 <= turn:
                rows[here + 1] = move(after(rows[here], sums[0]))
            if here < turn:
                rows[there - 1] = move(after(rows[there], sums[0]), back)
            hops = (here, there, 0) if hop == 1 else (here, there)
            parts.update(zip(hops, parts_of(rows, hops)))
        if here < chips:
            sums = rounded(added(parts[here], arrived))
    gate_weight = gate_fixed.astype(jnp.float32) / 65536.0
    mixed = values
    for piece, total in enumerate(added(parts[0], arrived)):
        first = piece * (tok // PIECES)
        at = slice(first, first + tok // PIECES)
        done = values[at].astype(jnp.float32) + gate_weight[at] * total
        mixed = lax.dynamic_update_slice(mixed, done.astype(jnp.bfloat16), (first, 0))
    return mixed


def solution(mesh):
    in_specs = (
        P(("rep", "ctx"), None),
        P(("rep", "ctx"), None),
        P(("rep", "ctx"), None),
        P(("rep", "ctx"), None),
        P(),
        P(),
        P(("rep", "ctx"), None),
        P(("rep", "ctx"), None),
        P("ctx", None, None),
        P("ctx", None, None),
        P("ctx", None, None),
    )
    out_specs = P(("rep", "ctx"), None)
    return jax.shard_map(local, mesh=mesh, in_specs=in_specs, out_specs=out_specs, check_vma=False)
```

```python
import functools
import math

import jax
import jax.numpy as jnp
from jax import lax
from jax.experimental import pallas as pl
from jax.experimental.pallas import tpu as pltpu
from jax.sharding import PartitionSpec as P

HEADS = 32
LAT = 512
ROPE = 64
VD = 128
SPAN = 8
CORES = 2

SCORE_SCALE = 192.0 ** (-0.5)
NORM_EPS = 1e-06
NEG_FILL = -1e30

HEAD_GROUP = 16
SUB_HEADS = 4
PIECES = 2
LOG2_SCALE = SCORE_SCALE * math.log2(math.e)


def attention_kernel(
    index_ref, q_ref, qr_ref, mine_ref, other_ref, wv_ref, gain_ref, values_ref, normed_ref,
    up_ref, down_ref, hits_ref, stack_ref, bias_a_ref, bias_b_ref, *, tok,
):
    group = pl.program_id(0)
    my_index = index_ref[0]
    my_chip, my_core = my_index // CORES, lax.rem(my_index, CORES)
    keys = mine_ref.shape[0]

    @pl.when(group == 0)
    def _():
        row_pos = my_index * tok + lax.broadcasted_iota(jnp.int32, (tok, keys), 0)
        key_iota = lax.broadcasted_iota(jnp.int32, (tok, keys), 1)
        key_chip = (key_iota // tok) ^ my_chip
        key_tok = lax.rem(key_iota, jnp.int32(tok))
        for core, bias_ref in ((my_core, bias_a_ref), (1 - my_core, bias_b_ref)):
            key_pos = (key_chip * CORES + core) * tok + key_tok
            bias_ref[...] = jnp.where(key_pos <= row_pos, 0.0, NEG_FILL)
        last = mine_ref[:, LAT : LAT + 2 * ROPE].astype(jnp.float32)
        lane = lax.broadcasted_iota(jnp.int32, last.shape, 1)
        named = jnp.max(jnp.where(lane >= ROPE, last, -1.0), axis=1, keepdims=True)
        my_expert = (my_index // SPAN).astype(jnp.float32)
        hits = jnp.where(named == my_expert, 1.0, 0.0)
        column = lax.broadcasted_iota(jnp.int32, hits_ref.shape, 1)
        table = jnp.zeros(hits_ref.shape, jnp.float32)
        for place in range(keys // tok):
            table = jnp.where(column == place, hits[place * tok : (place + 1) * tok], table)
        hits_ref[...] = table

    lane = lax.broadcasted_iota(jnp.int32, (tok, 2 * ROPE), 1)
    for head in range(HEAD_GROUP):
        at = pl.ds(head * tok, tok)
        stack_ref[at, 0:LAT] = q_ref[:, head * LAT : (head + 1) * LAT]
        pair = qr_ref[:, (head // 2) * 2 * ROPE : (head // 2 + 1) * 2 * ROPE]
        if head % 2:
            pair = jnp.concatenate([pair[:, ROPE:], pair[:, :ROPE]], axis=1)
        stack_ref[at, LAT : LAT + 2 * ROPE] = jnp.where(lane < ROPE, pair, jnp.zeros_like(pair))

    rows = SUB_HEADS * tok

    def scores_of(sub, keys_ref, bias_ref):
        queries = stack_ref[sub * rows : (sub + 1) * rows, :]
        scores = lax.dot_general(
            queries, keys_ref[...], (((1,), (1,)), ((), ())), preferred_element_type=jnp.float32
        )
        return scores.reshape(SUB_HEADS, tok, keys) * LOG2_SCALE + bias_ref[...][None]

    def both_scores(sub):
        return scores_of(sub, mine_ref, bias_a_ref), scores_of(sub, other_ref, bias_b_ref)

    parts = []
    subs = HEAD_GROUP // SUB_HEADS
    ready = both_scores(0)
    for sub in range(subs):
        scores_a, scores_b = ready
        if sub + 1 < subs:
            ready = both_scores(sub + 1)
        top = jnp.max(jnp.maximum(scores_a, scores_b), axis=2, keepdims=True)
        weights_a = jnp.exp2(scores_a - top)
        weights_b = jnp.exp2(scores_b - top)
        total = jnp.sum(weights_a + weights_b, axis=2, keepdims=True)
        mixed = jnp.dot(
            weights_a.astype(jnp.bfloat16).reshape(rows, keys), mine_ref[:, 0:LAT],
            preferred_element_type=jnp.float32,
        ) + jnp.dot(
            weights_b.astype(jnp.bfloat16).reshape(rows, keys), other_ref[:, 0:LAT],
            preferred_element_type=jnp.float32,
        )
        latent = (mixed.reshape(SUB_HEADS, tok, LAT) / total).astype(jnp.bfloat16)
        for head in range(0, SUB_HEADS, 2):
            first = sub * SUB_HEADS + head
            pair = jnp.dot(
                latent[head : head + 2].reshape(2 * tok, LAT),
                jnp.concatenate([wv_ref[first], wv_ref[first + 1]], axis=1),
                preferred_element_type=jnp.float32,
            ).astype(jnp.bfloat16)
            parts.extend([pair[:tok, :VD], pair[tok:, VD:]])
    wide = HEAD_GROUP * VD
    values_ref[:, pl.ds(pl.multiple_of(group * wide, wide), wide)] = jnp.concatenate(parts, axis=1)

    @pl.when(group == HEADS // HEAD_GROUP - 1)
    def _():
        values = values_ref[...].astype(jnp.float32)
        square = jnp.mean(values * values, axis=1, keepdims=True)
        normed = values * lax.rsqrt(square + NORM_EPS) * gain_ref[...]
        normed = normed.astype(jnp.bfloat16)
        normed_ref[...] = normed
        up_ref[...] = normed[: tok // 2]
        down_ref[...] = normed[tok // 2 :]


def attention(my_index, q_nope, q_rope, mine, other, w_value, norm_gain):
    tok = q_nope.shape[0]
    total = mine.shape[0]
    rows = HEAD_GROUP * tok
    grid_spec = pltpu.PrefetchScalarGridSpec(
        num_scalar_prefetch=1,
        grid=(HEADS // HEAD_GROUP,),
        in_specs=[
            pl.BlockSpec((tok, HEAD_GROUP * LAT), lambda g, i: (0, g)),
            pl.BlockSpec((tok, HEAD_GROUP * ROPE), lambda g, i: (0, g)),
            pl.BlockSpec(mine.shape, lambda g, i: (0, 0)),
            pl.BlockSpec(mine.shape, lambda g, i: (0, 0)),
            pl.BlockSpec((HEAD_GROUP, LAT, VD), lambda g, i: (g, 0, 0)),
            pl.BlockSpec((1, HEADS * VD), lambda g, i: (0, 0)),
        ],
        out_specs=[
            pl.BlockSpec((tok, HEADS * VD), lambda g, i: (0, 0)),
            pl.BlockSpec((tok, HEADS * VD), lambda g, i: (0, 0)),
            pl.BlockSpec((tok // 2, HEADS * VD), lambda g, i: (0, 0)),
            pl.BlockSpec((tok // 2, HEADS * VD), lambda g, i: (0, 0)),
            pl.BlockSpec((tok, total // tok), lambda g, i: (0, 0)),
        ],
        scratch_shapes=[
            pltpu.VMEM((rows, LAT + 2 * ROPE), jnp.bfloat16),
            pltpu.VMEM((tok, total), jnp.float32),
            pltpu.VMEM((tok, total), jnp.float32),
        ],
    )
    shape = jax.ShapeDtypeStruct((tok, HEADS * VD), jnp.bfloat16)
    half_shape = jax.ShapeDtypeStruct((tok // 2, HEADS * VD), jnp.bfloat16)
    hits_shape = jax.ShapeDtypeStruct((tok, total // tok), jnp.float32)
    work = HEADS * tok * total * CORES
    return pl.pallas_call(
        functools.partial(attention_kernel, tok=tok),
        grid_spec=grid_spec,
        out_shape=[shape, shape, half_shape, half_shape, hits_shape],
        compiler_params=pltpu.CompilerParams(vmem_limit_bytes=56 << 20),
        cost_estimate=pl.CostEstimate(
            flops=2 * work * (2 * LAT + 2 * ROPE), bytes_accessed=8 << 20, transcendentals=work
        ),
    )(my_index.reshape(1), q_nope, q_rope, mine, other, w_value, norm_gain.reshape(1, HEADS * VD))


def ring_place(chip, chips):
    return jnp.where(chip % 2 == 0, chip // 2, chips - 1 - chip // 2)


def ring_chip(place, chips):
    return jnp.where(place < chips // 2, 2 * place, 2 * (chips - 1 - place) + 1)


def expert_kernel(
    index_ref, gate_a, up_a, down_a, hits_hbm, gate_hbm, up_hbm, down_hbm, *refs, hops, chips,
):
    *refs, hits_ref, gate_b, up_b, down_b, sems = refs
    outs = PIECES * len(hops)
    rows_refs, out_refs = refs[:-outs], refs[-outs:]
    pairs = ((hits_hbm, hits_ref), (gate_hbm, gate_b), (up_hbm, up_b), (down_hbm, down_b))
    copies = [
        pltpu.make_async_copy(there, here, sems.at[i]) for i, (there, here) in enumerate(pairs)
    ]
    for copy in copies:
        copy.start()
    my_chip, my_core = index_ref[0] // CORES, lax.rem(index_ref[0], CORES)
    rows = jnp.concatenate([ref[...] for ref in rows_refs], axis=0)

    def hit(hop):
        place = ring_place(my_chip, chips) + chips + hop * (2 * my_core - 1)
        source = ring_chip(lax.rem(place, chips), chips) ^ my_chip
        column = lax.broadcasted_iota(jnp.int32, hits_ref.shape, 1)
        return jnp.max(jnp.where(column == source, hits_ref[...], 0.0), axis=1, keepdims=True)

    def hidden(gate_ref, up_ref):
        gate_act = jnp.dot(rows, gate_ref[...], preferred_element_type=jnp.float32)
        up_act = jnp.dot(rows, up_ref[...], preferred_element_type=jnp.float32)
        return gate_act * (1.0 / (1.0 + jnp.exp(-gate_act))) * up_act

    def kept(act):
        return jnp.where(keep, act, 0.0).astype(jnp.bfloat16)

    act_a = hidden(gate_a, up_a)
    copies[0].wait()
    keep = jnp.concatenate([hit(hop) for hop in hops], axis=0) > 0.0
    part = jnp.dot(kept(act_a), down_a[...], preferred_element_type=jnp.float32)
    copies[1].wait()
    copies[2].wait()
    act_b = hidden(gate_b, up_b)
    copies[3].wait()
    part = part + jnp.dot(kept(act_b), down_b[...], preferred_element_type=jnp.float32)
    size = part.shape[0] // outs
    for i, out_ref in enumerate(out_refs):
        out_ref[...] = part[i * size : (i + 1) * size]


def expert_parts(my_index, rows, hits, own, swapped, hops, chips):
    tok, features = hits.shape[0], rows[0].shape[1]
    units = 2 * own[0].shape[1]
    outs = PIECES * len(hops)
    vmem, anywhere = pl.BlockSpec(memory_space=pltpu.VMEM), pl.BlockSpec(memory_space=pl.ANY)
    parts = pl.pallas_call(
        functools.partial(expert_kernel, hops=hops, chips=chips),
        in_specs=[pl.BlockSpec(memory_space=pltpu.SMEM)]
        + [vmem] * 3 + [anywhere] * 4 + [vmem] * len(rows),
        out_specs=[vmem] * outs,
        out_shape=[jax.ShapeDtypeStruct((tok // PIECES, features), jnp.float32)] * outs,
        scratch_shapes=[pltpu.VMEM(w.shape, w.dtype) for w in (hits, *swapped)]
        + [pltpu.SemaphoreType.DMA((4,))],
        compiler_params=pltpu.CompilerParams(vmem_limit_bytes=28 << 20),
        cost_estimate=pl.CostEstimate(
            flops=6 * tok * features * units, bytes_accessed=14 << 20, transcendentals=0
        ),
    )(my_index.reshape(1), *own, hits, *swapped, *rows)
    return [tuple(parts[i : i + PIECES]) for i in range(0, outs, PIECES)]


def local(
    q_nope, q_rope, c_kv, k_rope, w_value, norm_gain, expert_ids, gate_fixed, w_gate, w_up, w_down
):
    tok = c_kv.shape[0]
    n_ctx = lax.axis_size("ctx")
    chips = n_ctx // CORES
    my_index = lax.axis_index("ctx")
    siblings = [(i, i ^ 1) for i in range(n_ctx)]
    ring = list(range(0, chips, 2)) + list(range(1, chips, 2))[::-1]
    route = [
        (ring[p] * CORES + core, ring[(p + 1 - 2 * core) % chips] * CORES + core)
        for p in range(chips) for core in range(CORES)
    ]
    back = [(there, here) for here, there in route]

    def from_chip(block, step):
        return lax.ppermute(block, "ctx", [(i, i ^ (step * CORES)) for i in range(n_ctx)])

    ids = jnp.broadcast_to(expert_ids.astype(jnp.bfloat16), (tok, ROPE))
    block = jnp.concatenate([c_kv, k_rope, ids], axis=1)
    across = from_chip(block, chips // 2)
    near = [block] + [from_chip(block, step) for step in range(1, chips // 2)]
    far = [across] + [from_chip(across, step) for step in range(1, chips // 2)]
    mine = jnp.concatenate(near + far, axis=0)
    other = lax.ppermute(mine, "ctx", siblings)

    own, mine, other = lax.optimization_barrier(((w_gate[0], w_up[0], w_down[0]), mine, other))
    swapped = tuple(lax.ppermute(w, "ctx", siblings) for w in own)
    values, normed, upper, lower, hits = attention(
        my_index, q_nope, q_rope, mine, other, w_value, norm_gain
    )
    start, normed, swapped = lax.optimization_barrier(((upper, lower), normed, swapped))

    def parts_of(rows, hops):
        blocks = [block for hop in hops for block in rows[hop]]
        return expert_parts(my_index, blocks, hits, own, swapped, hops, chips)

    def move(blocks, way=route):
        return tuple(lax.ppermute(x, "ctx", way) for x in blocks)

    def after(blocks, first):
        return tuple(lax.optimization_barrier((x, first))[0] for x in blocks)

    def added(part, arrived):
        return tuple(x + y.astype(jnp.float32) for x, y in zip(part, arrived))

    def rounded(part):
        return tuple(x.astype(jnp.bfloat16) for x in part)

    turn = chips // 2
    rows = {0: start, 1: move(start)}
    rows[2] = move(rows[1])
    rows[chips - 1] = move(after((normed,), rows[1][-1]), back)
    rows[3] = move((jnp.concatenate(rows[2], axis=0),))
    hops = (2, chips - 1, 1)
    parts = dict(zip(hops, parts_of(rows, hops)))
    sums = rounded(parts[2])
    rows[chips - 2] = move(rows[chips - 1], back)
    direct = []
    for hop in range(2, chips):
        arrived = move(sums)
        here, there = hop + 1, chips - hop
        if here <= turn:
            if here < turn:
                rows[here + 1] = move(after(rows[here], sums[0]))
                rows[there - 1] = move(after(rows[there], sums[0]), back)
            hops = (here, there, 0) if hop == 2 else (here, there)
            parts.update(zip(hops, parts_of(rows, hops)))
        elif len(direct) < PIECES:
            piece = parts[1][len(direct)].astype(jnp.bfloat16)
            direct += move(after((piece,), sums[0]), back)
        if here < chips:
            sums = rounded(added(parts[here], arrived))
    expert_out = jnp.concatenate(added(added(parts[0], direct), arrived), axis=0)
    gate_weight = gate_fixed.astype(jnp.float32) / 65536.0
    return (values.astype(jnp.float32) + gate_weight * expert_out).astype(jnp.bfloat16)


def solution(mesh):
    in_specs = (
        P(("rep", "ctx"), None),
        P(("rep", "ctx"), None),
        P(("rep", "ctx"), None),
        P(("rep", "ctx"), None),
        P(),
        P(),
        P(("rep", "ctx"), None),
        P(("rep", "ctx"), None),
        P("ctx", None, None),
        P("ctx", None, None),
        P("ctx", None, None),
    )
    out_specs = P(("rep", "ctx"), None)
    return jax.shard_map(local, mesh=mesh, in_specs=in_specs, out_specs=out_specs, check_vma=False)
```

```python
import functools
import math

import jax
import jax.numpy as jnp
from jax import lax
from jax.experimental import pallas as pl
from jax.experimental.pallas import tpu as pltpu
from jax.sharding import PartitionSpec as P

HEADS = 32
LAT = 512
ROPE = 64
VD = 128
SPAN = 8
CORES = 2

SCORE_SCALE = 192.0 ** (-0.5)
NORM_EPS = 1e-06
NEG_FILL = -1e30

HEAD_GROUP = 16
SUB_HEADS = 8
PIECES = 2
LOG2_SCALE = SCORE_SCALE * math.log2(math.e)


def attention_kernel(
    index_ref, q_ref, qr_ref, mine_ref, other_ref, wv_ref, gain_ref, values_ref, normed_ref,
    up_ref, down_ref, hits_ref, stack_ref, bias_a_ref, bias_b_ref, *, tok,
):
    group = pl.program_id(0)
    my_index = index_ref[0]
    my_chip, my_core = my_index // CORES, lax.rem(my_index, CORES)
    keys = mine_ref.shape[0]

    @pl.when(group == 0)
    def _():
        row_pos = my_index * tok + lax.broadcasted_iota(jnp.int32, (tok, keys), 0)
        key_iota = lax.broadcasted_iota(jnp.int32, (tok, keys), 1)
        key_chip = (key_iota // tok) ^ my_chip
        key_tok = lax.rem(key_iota, jnp.int32(tok))
        for core, bias_ref in ((my_core, bias_a_ref), (1 - my_core, bias_b_ref)):
            key_pos = (key_chip * CORES + core) * tok + key_tok
            bias_ref[...] = jnp.where(key_pos <= row_pos, 0.0, NEG_FILL)
        last = mine_ref[:, LAT : LAT + 2 * ROPE].astype(jnp.float32)
        lane = lax.broadcasted_iota(jnp.int32, last.shape, 1)
        named = jnp.max(jnp.where(lane >= ROPE, last, -1.0), axis=1, keepdims=True)
        my_expert = (my_index // SPAN).astype(jnp.float32)
        hits = jnp.where(named == my_expert, 1.0, 0.0)
        column = lax.broadcasted_iota(jnp.int32, hits_ref.shape, 1)
        table = jnp.zeros(hits_ref.shape, jnp.float32)
        for place in range(keys // tok):
            table = jnp.where(column == place, hits[place * tok : (place + 1) * tok], table)
        hits_ref[...] = table

    lane = lax.broadcasted_iota(jnp.int32, (tok, 2 * ROPE), 1)
    for head in range(HEAD_GROUP):
        at = pl.ds(head * tok, tok)
        stack_ref[at, 0:LAT] = q_ref[:, head * LAT : (head + 1) * LAT]
        pair = qr_ref[:, (head // 2) * 2 * ROPE : (head // 2 + 1) * 2 * ROPE]
        if head % 2:
            pair = jnp.concatenate([pair[:, ROPE:], pair[:, :ROPE]], axis=1)
        stack_ref[at, LAT : LAT + 2 * ROPE] = jnp.where(lane < ROPE, pair, jnp.zeros_like(pair))

    rows = SUB_HEADS * tok

    def scores_of(sub, keys_ref, bias_ref):
        queries = stack_ref[sub * rows : (sub + 1) * rows, :]
        scores = lax.dot_general(
            queries, keys_ref[...], (((1,), (1,)), ((), ())), preferred_element_type=jnp.float32
        )
        return scores.reshape(SUB_HEADS, tok, keys) * LOG2_SCALE + bias_ref[...][None]

    def both_scores(sub):
        return scores_of(sub, mine_ref, bias_a_ref), scores_of(sub, other_ref, bias_b_ref)

    parts = []
    subs = HEAD_GROUP // SUB_HEADS
    ready = both_scores(0)
    for sub in range(subs):
        scores_a, scores_b = ready
        if sub + 1 < subs:
            ready = both_scores(sub + 1)
        top = jnp.max(jnp.maximum(scores_a, scores_b), axis=2, keepdims=True)
        weights_a = jnp.exp2(scores_a - top)
        weights_b = jnp.exp2(scores_b - top)
        total = jnp.sum(weights_a + weights_b, axis=2, keepdims=True)
        mixed = jnp.dot(
            weights_a.astype(jnp.bfloat16).reshape(rows, keys), mine_ref[:, 0:LAT],
            preferred_element_type=jnp.float32,
        ) + jnp.dot(
            weights_b.astype(jnp.bfloat16).reshape(rows, keys), other_ref[:, 0:LAT],
            preferred_element_type=jnp.float32,
        )
        latent = (mixed.reshape(SUB_HEADS, tok, LAT) / total).astype(jnp.bfloat16)
        for head in range(0, SUB_HEADS, 2):
            first = sub * SUB_HEADS + head
            pair = jnp.dot(
                latent[head : head + 2].reshape(2 * tok, LAT),
                jnp.concatenate([wv_ref[first], wv_ref[first + 1]], axis=1),
                preferred_element_type=jnp.float32,
            ).astype(jnp.bfloat16)
            parts.extend([pair[:tok, :VD], pair[tok:, VD:]])
    wide = HEAD_GROUP * VD
    values_ref[:, pl.ds(pl.multiple_of(group * wide, wide), wide)] = jnp.concatenate(parts, axis=1)

    @pl.when(group == HEADS // HEAD_GROUP - 1)
    def _():
        values = values_ref[...].astype(jnp.float32)
        square = jnp.mean(values * values, axis=1, keepdims=True)
        normed = values * lax.rsqrt(square + NORM_EPS) * gain_ref[...]
        normed = normed.astype(jnp.bfloat16)
        normed_ref[...] = normed
        up_ref[...] = normed[: tok // 2]
        down_ref[...] = normed[tok // 2 :]


def attention(my_index, q_nope, q_rope, mine, other, w_value, norm_gain):
    tok = q_nope.shape[0]
    total = mine.shape[0]
    rows = HEAD_GROUP * tok
    grid_spec = pltpu.PrefetchScalarGridSpec(
        num_scalar_prefetch=1,
        grid=(HEADS // HEAD_GROUP,),
        in_specs=[
            pl.BlockSpec((tok, HEAD_GROUP * LAT), lambda g, i: (0, g)),
            pl.BlockSpec((tok, HEAD_GROUP * ROPE), lambda g, i: (0, g)),
            pl.BlockSpec(mine.shape, lambda g, i: (0, 0)),
            pl.BlockSpec(mine.shape, lambda g, i: (0, 0)),
            pl.BlockSpec((HEAD_GROUP, LAT, VD), lambda g, i: (g, 0, 0)),
            pl.BlockSpec((1, HEADS * VD), lambda g, i: (0, 0)),
        ],
        out_specs=[
            pl.BlockSpec((tok, HEADS * VD), lambda g, i: (0, 0)),
            pl.BlockSpec((tok, HEADS * VD), lambda g, i: (0, 0)),
            pl.BlockSpec((tok // 2, HEADS * VD), lambda g, i: (0, 0)),
            pl.BlockSpec((tok // 2, HEADS * VD), lambda g, i: (0, 0)),
            pl.BlockSpec((tok, total // tok), lambda g, i: (0, 0)),
        ],
        scratch_shapes=[
            pltpu.VMEM((rows, LAT + 2 * ROPE), jnp.bfloat16),
            pltpu.VMEM((tok, total), jnp.float32),
            pltpu.VMEM((tok, total), jnp.float32),
        ],
    )
    shape = jax.ShapeDtypeStruct((tok, HEADS * VD), jnp.bfloat16)
    half_shape = jax.ShapeDtypeStruct((tok // 2, HEADS * VD), jnp.bfloat16)
    hits_shape = jax.ShapeDtypeStruct((tok, total // tok), jnp.float32)
    work = HEADS * tok * total * CORES
    return pl.pallas_call(
        functools.partial(attention_kernel, tok=tok),
        grid_spec=grid_spec,
        out_shape=[shape, shape, half_shape, half_shape, hits_shape],
        compiler_params=pltpu.CompilerParams(vmem_limit_bytes=56 << 20),
        cost_estimate=pl.CostEstimate(
            flops=2 * work * (2 * LAT + 2 * ROPE), bytes_accessed=8 << 20, transcendentals=work
        ),
    )(my_index.reshape(1), q_nope, q_rope, mine, other, w_value, norm_gain.reshape(1, HEADS * VD))


def ring_place(chip, chips):
    return jnp.where(chip % 2 == 0, chip // 2, chips - 1 - chip // 2)


def ring_chip(place, chips):
    return jnp.where(place < chips // 2, 2 * place, 2 * (chips - 1 - place) + 1)


def expert_kernel(
    index_ref, gate_a, up_a, down_a, hits_hbm, gate_hbm, up_hbm, down_hbm, *refs, hops, chips,
):
    *refs, hits_ref, gate_b, up_b, down_b, sems = refs
    outs = PIECES * len(hops)
    rows_refs, out_refs = refs[:-outs], refs[-outs:]
    pairs = ((hits_hbm, hits_ref), (gate_hbm, gate_b), (up_hbm, up_b), (down_hbm, down_b))
    copies = [
        pltpu.make_async_copy(there, here, sems.at[i]) for i, (there, here) in enumerate(pairs)
    ]
    for copy in copies:
        copy.start()
    my_chip, my_core = index_ref[0] // CORES, lax.rem(index_ref[0], CORES)
    rows = jnp.concatenate([ref[...] for ref in rows_refs], axis=0)

    def hit(hop):
        place = ring_place(my_chip, chips) + chips + hop * (2 * my_core - 1)
        source = ring_chip(lax.rem(place, chips), chips) ^ my_chip
        column = lax.broadcasted_iota(jnp.int32, hits_ref.shape, 1)
        return jnp.max(jnp.where(column == source, hits_ref[...], 0.0), axis=1, keepdims=True)

    def hidden(gate_ref, up_ref):
        gate_act = jnp.dot(rows, gate_ref[...], preferred_element_type=jnp.float32)
        up_act = jnp.dot(rows, up_ref[...], preferred_element_type=jnp.float32)
        return gate_act * (1.0 / (1.0 + jnp.exp(-gate_act))) * up_act

    def kept(act):
        return jnp.where(keep, act, 0.0).astype(jnp.bfloat16)

    act_a = hidden(gate_a, up_a)
    copies[0].wait()
    keep = jnp.concatenate([hit(hop) for hop in hops], axis=0) > 0.0
    part = jnp.dot(kept(act_a), down_a[...], preferred_element_type=jnp.float32)
    copies[1].wait()
    copies[2].wait()
    act_b = hidden(gate_b, up_b)
    copies[3].wait()
    part = part + jnp.dot(kept(act_b), down_b[...], preferred_element_type=jnp.float32)
    size = part.shape[0] // outs
    for i, out_ref in enumerate(out_refs):
        out_ref[...] = part[i * size : (i + 1) * size]


def expert_parts(my_index, rows, hits, own, swapped, hops, chips):
    tok, features = hits.shape[0], rows[0].shape[1]
    units = 2 * own[0].shape[1]
    outs = PIECES * len(hops)
    vmem, anywhere = pl.BlockSpec(memory_space=pltpu.VMEM), pl.BlockSpec(memory_space=pl.ANY)
    parts = pl.pallas_call(
        functools.partial(expert_kernel, hops=hops, chips=chips),
        in_specs=[pl.BlockSpec(memory_space=pltpu.SMEM)]
        + [vmem] * 3 + [anywhere] * 4 + [vmem] * len(rows),
        out_specs=[vmem] * outs,
        out_shape=[jax.ShapeDtypeStruct((tok // PIECES, features), jnp.float32)] * outs,
        scratch_shapes=[pltpu.VMEM(w.shape, w.dtype) for w in (hits, *swapped)]
        + [pltpu.SemaphoreType.DMA((4,))],
        compiler_params=pltpu.CompilerParams(vmem_limit_bytes=28 << 20),
        cost_estimate=pl.CostEstimate(
            flops=6 * tok * features * units, bytes_accessed=14 << 20, transcendentals=0
        ),
    )(my_index.reshape(1), *own, hits, *swapped, *rows)
    return [tuple(parts[i : i + PIECES]) for i in range(0, outs, PIECES)]


def local(
    q_nope, q_rope, c_kv, k_rope, w_value, norm_gain, expert_ids, gate_fixed, w_gate, w_up, w_down
):
    tok = c_kv.shape[0]
    n_ctx = lax.axis_size("ctx")
    chips = n_ctx // CORES
    my_index = lax.axis_index("ctx")
    siblings = [(i, i ^ 1) for i in range(n_ctx)]
    ring = list(range(0, chips, 2)) + list(range(1, chips, 2))[::-1]
    route = [
        (ring[p] * CORES + core, ring[(p + 1 - 2 * core) % chips] * CORES + core)
        for p in range(chips) for core in range(CORES)
    ]
    back = [(there, here) for here, there in route]

    def from_chip(block, step):
        return lax.ppermute(block, "ctx", [(i, i ^ (step * CORES)) for i in range(n_ctx)])

    ids = jnp.broadcast_to(expert_ids.astype(jnp.bfloat16), (tok, ROPE))
    block = jnp.concatenate([c_kv, k_rope, ids], axis=1)
    across = from_chip(block, chips // 2)
    near = [block] + [from_chip(block, step) for step in range(1, chips // 2)]
    far = [across] + [from_chip(across, step) for step in range(1, chips // 2)]
    mine = jnp.concatenate(near + far, axis=0)
    other = lax.ppermute(mine, "ctx", siblings)

    own, mine, other = lax.optimization_barrier(((w_gate[0], w_up[0], w_down[0]), mine, other))
    swapped = tuple(lax.ppermute(w, "ctx", siblings) for w in own)
    values, normed, upper, lower, hits = attention(
        my_index, q_nope, q_rope, mine, other, w_value, norm_gain
    )
    start, normed, swapped = lax.optimization_barrier(((upper, lower), normed, swapped))

    def parts_of(rows, hops):
        blocks = [block for hop in hops for block in rows[hop]]
        return expert_parts(my_index, blocks, table, own, swapped, hops, chips)

    def move(blocks, way=route):
        return tuple(lax.ppermute(x, "ctx", way) for x in blocks)

    def after(blocks, first):
        return tuple(lax.optimization_barrier((x, first))[0] for x in blocks)

    def added(part, arrived):
        return tuple(x + y.astype(jnp.float32) for x, y in zip(part, arrived))

    def rounded(part):
        return tuple(x.astype(jnp.bfloat16) for x in part)

    turn = chips // 2
    rows = {0: start, 1: move(start)}
    table = jnp.where(hits > 0.5, 1.0, 0.0)
    rows[2] = move(after(rows[1][:1], table)) + move(rows[1][1:])
    rows[chips - 1] = move(after((normed,), rows[1][-1]), back)
    rows[3] = move((jnp.concatenate(rows[2], axis=0),))
    parts = dict(zip((1,), parts_of(rows, (1,))))
    sums = rounded(parts[1])
    for hop in range(1, chips):
        arrived = move(sums)
        here, there = hop + 1, chips - hop
        if here <= turn:
            if 3 < here + 1 <= turn:
                rows[here + 1] = move(after(rows[here], sums[0]))
            if here < turn:
                rows[there - 1] = move(after(rows[there], sums[0]), back)
            hops = (here, there, 0) if hop == 1 else (here, there)
            parts.update(zip(hops, parts_of(rows, hops)))
        if here < chips:
            sums = rounded(added(parts[here], arrived))
    expert_out = jnp.concatenate(added(parts[0], arrived), axis=0)
    gate_weight = gate_fixed.astype(jnp.float32) / 65536.0
    return (values.astype(jnp.float32) + gate_weight * expert_out).astype(jnp.bfloat16)


def solution(mesh):
    in_specs = (
        P(("rep", "ctx"), None),
        P(("rep", "ctx"), None),
        P(("rep", "ctx"), None),
        P(("rep", "ctx"), None),
        P(),
        P(),
        P(("rep", "ctx"), None),
        P(("rep", "ctx"), None),
        P("ctx", None, None),
        P("ctx", None, None),
        P("ctx", None, None),
    )
    out_specs = P(("rep", "ctx"), None)
    return jax.shard_map(local, mesh=mesh, in_specs=in_specs, out_specs=out_specs, check_vma=False)
```

```python
import functools
import math

import jax
import jax.numpy as jnp
from jax import lax
from jax.experimental import pallas as pl
from jax.experimental.pallas import tpu as pltpu
from jax.sharding import PartitionSpec as P

HEADS = 32
LAT = 512
ROPE = 64
VD = 128
SPAN = 8
CORES = 2

SCORE_SCALE = 192.0 ** (-0.5)
NORM_EPS = 1e-06
NEG_FILL = -1e30

HEAD_GROUP = 16
SUB_HEADS = 8
PIECES = 2
LOG2_SCALE = SCORE_SCALE * math.log2(math.e)


def attention_kernel(
    index_ref, q_ref, qr_ref, mine_ref, other_ref, wv_ref, gain_ref, values_ref, normed_ref,
    up_ref, down_ref, hits_ref, stack_ref, bias_a_ref, bias_b_ref, *, tok,
):
    group = pl.program_id(0)
    my_index = index_ref[0]
    my_chip, my_core = my_index // CORES, lax.rem(my_index, CORES)
    keys = mine_ref.shape[0]

    @pl.when(group == 0)
    def _():
        row_pos = my_index * tok + lax.broadcasted_iota(jnp.int32, (tok, keys), 0)
        key_iota = lax.broadcasted_iota(jnp.int32, (tok, keys), 1)
        key_chip = (key_iota // tok) ^ my_chip
        key_tok = lax.rem(key_iota, jnp.int32(tok))
        for core, bias_ref in ((my_core, bias_a_ref), (1 - my_core, bias_b_ref)):
            key_pos = (key_chip * CORES + core) * tok + key_tok
            bias_ref[...] = jnp.where(key_pos <= row_pos, 0.0, NEG_FILL)
        last = mine_ref[:, LAT : LAT + 2 * ROPE].astype(jnp.float32)
        lane = lax.broadcasted_iota(jnp.int32, last.shape, 1)
        named = jnp.max(jnp.where(lane >= ROPE, last, -1.0), axis=1, keepdims=True)
        my_expert = (my_index // SPAN).astype(jnp.float32)
        hits = jnp.where(named == my_expert, 1.0, 0.0)
        column = lax.broadcasted_iota(jnp.int32, hits_ref.shape, 1)
        table = jnp.zeros(hits_ref.shape, jnp.float32)
        for place in range(keys // tok):
            table = jnp.where(column == place, hits[place * tok : (place + 1) * tok], table)
        hits_ref[...] = table

    lane = lax.broadcasted_iota(jnp.int32, (tok, 2 * ROPE), 1)
    for head in range(HEAD_GROUP):
        at = pl.ds(head * tok, tok)
        stack_ref[at, 0:LAT] = q_ref[:, head * LAT : (head + 1) * LAT]
        pair = qr_ref[:, (head // 2) * 2 * ROPE : (head // 2 + 1) * 2 * ROPE]
        if head % 2:
            pair = jnp.concatenate([pair[:, ROPE:], pair[:, :ROPE]], axis=1)
        stack_ref[at, LAT : LAT + 2 * ROPE] = jnp.where(lane < ROPE, pair, jnp.zeros_like(pair))

    rows = SUB_HEADS * tok

    def scores_of(sub, keys_ref, bias_ref):
        queries = stack_ref[sub * rows : (sub + 1) * rows, :]
        scores = lax.dot_general(
            queries, keys_ref[...], (((1,), (1,)), ((), ())), preferred_element_type=jnp.float32
        )
        return scores.reshape(SUB_HEADS, tok, keys) * LOG2_SCALE + bias_ref[...][None]

    def both_scores(sub):
        return scores_of(sub, mine_ref, bias_a_ref), scores_of(sub, other_ref, bias_b_ref)

    parts = []
    subs = HEAD_GROUP // SUB_HEADS
    ready = both_scores(0)
    for sub in range(subs):
        scores_a, scores_b = ready
        if sub + 1 < subs:
            ready = both_scores(sub + 1)
        top = jnp.max(jnp.maximum(scores_a, scores_b), axis=2, keepdims=True)
        weights_a = jnp.exp2(scores_a - top)
        weights_b = jnp.exp2(scores_b - top)
        total = jnp.sum(weights_a + weights_b, axis=2, keepdims=True)
        mixed = jnp.dot(
            weights_a.astype(jnp.bfloat16).reshape(rows, keys), mine_ref[:, 0:LAT],
            preferred_element_type=jnp.float32,
        ) + jnp.dot(
            weights_b.astype(jnp.bfloat16).reshape(rows, keys), other_ref[:, 0:LAT],
            preferred_element_type=jnp.float32,
        )
        latent = (mixed.reshape(SUB_HEADS, tok, LAT) / total).astype(jnp.bfloat16)
        for head in range(0, SUB_HEADS, 2):
            first = sub * SUB_HEADS + head
            pair = jnp.dot(
                latent[head : head + 2].reshape(2 * tok, LAT),
                jnp.concatenate([wv_ref[first], wv_ref[first + 1]], axis=1),
                preferred_element_type=jnp.float32,
            ).astype(jnp.bfloat16)
            parts.extend([pair[:tok, :VD], pair[tok:, VD:]])
    wide = HEAD_GROUP * VD
    values_ref[:, pl.ds(pl.multiple_of(group * wide, wide), wide)] = jnp.concatenate(parts, axis=1)

    @pl.when(group == HEADS // HEAD_GROUP - 1)
    def _():
        values = values_ref[...].astype(jnp.float32)
        square = jnp.mean(values * values, axis=1, keepdims=True)
        normed = values * lax.rsqrt(square + NORM_EPS) * gain_ref[...]
        normed = normed.astype(jnp.bfloat16)
        normed_ref[...] = normed
        up_ref[...] = normed[: tok // 2]
        down_ref[...] = normed[tok // 2 :]


def attention(my_index, q_nope, q_rope, mine, other, w_value, norm_gain):
    tok = q_nope.shape[0]
    total = mine.shape[0]
    rows = HEAD_GROUP * tok
    grid_spec = pltpu.PrefetchScalarGridSpec(
        num_scalar_prefetch=1,
        grid=(HEADS // HEAD_GROUP,),
        in_specs=[
            pl.BlockSpec((tok, HEAD_GROUP * LAT), lambda g, i: (0, g)),
            pl.BlockSpec((tok, HEAD_GROUP * ROPE), lambda g, i: (0, g)),
            pl.BlockSpec(mine.shape, lambda g, i: (0, 0)),
            pl.BlockSpec(mine.shape, lambda g, i: (0, 0)),
            pl.BlockSpec((HEAD_GROUP, LAT, VD), lambda g, i: (g, 0, 0)),
            pl.BlockSpec((1, HEADS * VD), lambda g, i: (0, 0)),
        ],
        out_specs=[
            pl.BlockSpec((tok, HEADS * VD), lambda g, i: (0, 0)),
            pl.BlockSpec((tok, HEADS * VD), lambda g, i: (0, 0)),
            pl.BlockSpec((tok // 2, HEADS * VD), lambda g, i: (0, 0)),
            pl.BlockSpec((tok // 2, HEADS * VD), lambda g, i: (0, 0)),
            pl.BlockSpec((tok, total // tok), lambda g, i: (0, 0)),
        ],
        scratch_shapes=[
            pltpu.VMEM((rows, LAT + 2 * ROPE), jnp.bfloat16),
            pltpu.VMEM((tok, total), jnp.float32),
            pltpu.VMEM((tok, total), jnp.float32),
        ],
    )
    shape = jax.ShapeDtypeStruct((tok, HEADS * VD), jnp.bfloat16)
    half_shape = jax.ShapeDtypeStruct((tok // 2, HEADS * VD), jnp.bfloat16)
    hits_shape = jax.ShapeDtypeStruct((tok, total // tok), jnp.float32)
    work = HEADS * tok * total * CORES
    return pl.pallas_call(
        functools.partial(attention_kernel, tok=tok),
        grid_spec=grid_spec,
        out_shape=[shape, shape, half_shape, half_shape, hits_shape],
        compiler_params=pltpu.CompilerParams(vmem_limit_bytes=56 << 20),
        cost_estimate=pl.CostEstimate(
            flops=2 * work * (2 * LAT + 2 * ROPE), bytes_accessed=8 << 20, transcendentals=work
        ),
    )(my_index.reshape(1), q_nope, q_rope, mine, other, w_value, norm_gain.reshape(1, HEADS * VD))


def ring_place(chip, chips):
    return jnp.where(chip % 2 == 0, chip // 2, chips - 1 - chip // 2)


def ring_chip(place, chips):
    return jnp.where(place < chips // 2, 2 * place, 2 * (chips - 1 - place) + 1)


def expert_kernel(
    index_ref, gate_a, up_a, down_a, hits_hbm, gate_hbm, up_hbm, down_hbm, *refs, hops, chips,
):
    *refs, hits_ref, gate_b, up_b, down_b, sems = refs
    outs = PIECES * len(hops)
    rows_refs, out_refs = refs[:-outs], refs[-outs:]
    pairs = ((hits_hbm, hits_ref), (gate_hbm, gate_b), (up_hbm, up_b), (down_hbm, down_b))
    copies = [
        pltpu.make_async_copy(there, here, sems.at[i]) for i, (there, here) in enumerate(pairs)
    ]
    for copy in copies:
        copy.start()
    my_chip, my_core = index_ref[0] // CORES, lax.rem(index_ref[0], CORES)
    rows = jnp.concatenate([ref[...] for ref in rows_refs], axis=0)

    def hit(hop):
        place = ring_place(my_chip, chips) + chips + hop * (2 * my_core - 1)
        source = ring_chip(lax.rem(place, chips), chips) ^ my_chip
        column = lax.broadcasted_iota(jnp.int32, hits_ref.shape, 1)
        return jnp.max(jnp.where(column == source, hits_ref[...], 0.0), axis=1, keepdims=True)

    def hidden(gate_ref, up_ref):
        gate_act = jnp.dot(rows, gate_ref[...], preferred_element_type=jnp.float32)
        up_act = jnp.dot(rows, up_ref[...], preferred_element_type=jnp.float32)
        return gate_act * (1.0 / (1.0 + jnp.exp(-gate_act))) * up_act

    def kept(act):
        return jnp.where(keep, act, 0.0).astype(jnp.bfloat16)

    act_a = hidden(gate_a, up_a)
    copies[0].wait()
    keep = jnp.concatenate([hit(hop) for hop in hops], axis=0) > 0.0
    part = jnp.dot(kept(act_a), down_a[...], preferred_element_type=jnp.float32)
    copies[1].wait()
    copies[2].wait()
    act_b = hidden(gate_b, up_b)
    copies[3].wait()
    part = part + jnp.dot(kept(act_b), down_b[...], preferred_element_type=jnp.float32)
    size = part.shape[0] // outs
    for i, out_ref in enumerate(out_refs):
        out_ref[...] = part[i * size : (i + 1) * size]


def expert_parts(my_index, rows, hits, own, swapped, hops, chips):
    tok, features = hits.shape[0], rows[0].shape[1]
    units = 2 * own[0].shape[1]
    outs = PIECES * len(hops)
    vmem, anywhere = pl.BlockSpec(memory_space=pltpu.VMEM), pl.BlockSpec(memory_space=pl.ANY)
    parts = pl.pallas_call(
        functools.partial(expert_kernel, hops=hops, chips=chips),
        in_specs=[pl.BlockSpec(memory_space=pltpu.SMEM)]
        + [vmem] * 3 + [anywhere] * 4 + [vmem] * len(rows),
        out_specs=[vmem] * outs,
        out_shape=[jax.ShapeDtypeStruct((tok // PIECES, features), jnp.float32)] * outs,
        scratch_shapes=[pltpu.VMEM(w.shape, w.dtype) for w in (hits, *swapped)]
        + [pltpu.SemaphoreType.DMA((4,))],
        compiler_params=pltpu.CompilerParams(vmem_limit_bytes=28 << 20),
        cost_estimate=pl.CostEstimate(
            flops=6 * tok * features * units, bytes_accessed=14 << 20, transcendentals=0
        ),
    )(my_index.reshape(1), *own, hits, *swapped, *rows)
    return [tuple(parts[i : i + PIECES]) for i in range(0, outs, PIECES)]


def local(
    q_nope, q_rope, c_kv, k_rope, w_value, norm_gain, expert_ids, gate_fixed, w_gate, w_up, w_down
):
    tok = c_kv.shape[0]
    n_ctx = lax.axis_size("ctx")
    chips = n_ctx // CORES
    my_index = lax.axis_index("ctx")
    siblings = [(i, i ^ 1) for i in range(n_ctx)]
    ring = list(range(0, chips, 2)) + list(range(1, chips, 2))[::-1]
    route = [
        (ring[p] * CORES + core, ring[(p + 1 - 2 * core) % chips] * CORES + core)
        for p in range(chips) for core in range(CORES)
    ]
    back = [(there, here) for here, there in route]

    def from_chip(block, step):
        return lax.ppermute(block, "ctx", [(i, i ^ (step * CORES)) for i in range(n_ctx)])

    ids = jnp.broadcast_to(expert_ids.astype(jnp.bfloat16), (tok, ROPE))
    block = jnp.concatenate([c_kv, k_rope, ids], axis=1)
    across = from_chip(block, chips // 2)
    near = [block] + [from_chip(block, step) for step in range(1, chips // 2)]
    far = [across] + [from_chip(across, step) for step in range(1, chips // 2)]
    mine = jnp.concatenate(near + far, axis=0)
    other = lax.ppermute(mine, "ctx", siblings)

    own, mine, other = lax.optimization_barrier(((w_gate[0], w_up[0], w_down[0]), mine, other))
    swapped = tuple(lax.ppermute(w, "ctx", siblings) for w in own)
    values, normed, upper, lower, hits = attention(
        my_index, q_nope, q_rope, mine, other, w_value, norm_gain
    )
    start, normed, swapped = lax.optimization_barrier(((upper, lower), normed, swapped))

    def parts_of(rows, hops):
        blocks = [block for hop in hops for block in rows[hop]]
        return expert_parts(my_index, blocks, table, own, swapped, hops, chips)

    def move(blocks, way=route):
        return tuple(lax.ppermute(x, "ctx", way) for x in blocks)

    def after(blocks, first):
        return tuple(lax.optimization_barrier((x, first))[0] for x in blocks)

    def added(part, arrived):
        return tuple(x + y.astype(jnp.float32) for x, y in zip(part, arrived))

    def rounded(part):
        return tuple(x.astype(jnp.bfloat16) for x in part)

    rows = {0: start, 1: move(start)}
    table = jnp.where(hits > 0.5, 1.0, 0.0)
    rows[2] = move(after(rows[1][:1], table)) + move(rows[1][1:])
    rows[chips - 1] = move(after((normed,), rows[1][-1]), back)
    rows[3] = move((jnp.concatenate(rows[2], axis=0),))
    parts = dict(zip((1,), parts_of(rows, (1,))))
    sums = rounded(parts[1])
    for hop in range(1, chips):
        arrived = move(sums)
        here = hop + 1
        if hop + 3 < chips - 1:
            rows[hop + 3] = move(after(rows[hop + 2], sums[0]))
        if here < chips - 1:
            hops = (here, chips - 1, 0) if hop == 1 else (here,)
            parts.update(zip(hops, parts_of(rows, hops)))
        if here < chips:
            sums = rounded(added(parts[here], arrived))
    expert_out = jnp.concatenate(added(parts[0], arrived), axis=0)
    gate_weight = gate_fixed.astype(jnp.float32) / 65536.0
    return (values.astype(jnp.float32) + gate_weight * expert_out).astype(jnp.bfloat16)


def solution(mesh):
    in_specs = (
        P(("rep", "ctx"), None),
        P(("rep", "ctx"), None),
        P(("rep", "ctx"), None),
        P(("rep", "ctx"), None),
        P(),
        P(),
        P(("rep", "ctx"), None),
        P(("rep", "ctx"), None),
        P("ctx", None, None),
        P("ctx", None, None),
        P("ctx", None, None),
    )
    out_specs = P(("rep", "ctx"), None)
    return jax.shard_map(local, mesh=mesh, in_specs=in_specs, out_specs=out_specs, check_vma=False)
```

```python
import functools
import math

import jax
import jax.numpy as jnp
from jax import lax
from jax.experimental import pallas as pl
from jax.experimental.pallas import tpu as pltpu
from jax.sharding import PartitionSpec as P

HEADS = 32
LAT = 512
ROPE = 64
VD = 128
SPAN = 8
CORES = 2

SCORE_SCALE = 192.0 ** (-0.5)
NORM_EPS = 1e-06
NEG_FILL = -1e30

HEAD_GROUP = 16
SUB_HEADS = 8
PIECES = 2
LOG2_SCALE = SCORE_SCALE * math.log2(math.e)


def attention_kernel(
    index_ref, q_ref, qr_ref, mine_ref, other_ref, wv_ref, gain_ref, values_ref, normed_ref,
    up_ref, down_ref, hits_ref, stack_ref, bias_a_ref, bias_b_ref, *, tok,
):
    group = pl.program_id(0)
    my_index = index_ref[0]
    my_chip, my_core = my_index // CORES, lax.rem(my_index, CORES)
    keys = mine_ref.shape[0]

    @pl.when(group == 0)
    def _():
        row_pos = my_index * tok + lax.broadcasted_iota(jnp.int32, (tok, keys), 0)
        key_iota = lax.broadcasted_iota(jnp.int32, (tok, keys), 1)
        key_chip = (key_iota // tok) ^ my_chip
        key_tok = lax.rem(key_iota, jnp.int32(tok))
        for core, bias_ref in ((my_core, bias_a_ref), (1 - my_core, bias_b_ref)):
            key_pos = (key_chip * CORES + core) * tok + key_tok
            bias_ref[...] = jnp.where(key_pos <= row_pos, 0.0, NEG_FILL)
        last = mine_ref[:, LAT : LAT + 2 * ROPE].astype(jnp.float32)
        lane = lax.broadcasted_iota(jnp.int32, last.shape, 1)
        named = jnp.max(jnp.where(lane >= ROPE, last, -1.0), axis=1, keepdims=True)
        my_expert = (my_index // SPAN).astype(jnp.float32)
        hits = jnp.where(named == my_expert, 1.0, 0.0)
        column = lax.broadcasted_iota(jnp.int32, hits_ref.shape, 1)
        table = jnp.zeros(hits_ref.shape, jnp.float32)
        for place in range(keys // tok):
            table = jnp.where(column == place, hits[place * tok : (place + 1) * tok], table)
        hits_ref[...] = table

    lane = lax.broadcasted_iota(jnp.int32, (tok, 2 * ROPE), 1)
    for head in range(HEAD_GROUP):
        at = pl.ds(head * tok, tok)
        stack_ref[at, 0:LAT] = q_ref[:, head * LAT : (head + 1) * LAT]
        pair = qr_ref[:, (head // 2) * 2 * ROPE : (head // 2 + 1) * 2 * ROPE]
        if head % 2:
            pair = jnp.concatenate([pair[:, ROPE:], pair[:, :ROPE]], axis=1)
        stack_ref[at, LAT : LAT + 2 * ROPE] = jnp.where(lane < ROPE, pair, jnp.zeros_like(pair))

    rows = SUB_HEADS * tok

    def scores_of(sub, keys_ref, bias_ref):
        queries = stack_ref[sub * rows : (sub + 1) * rows, :]
        scores = lax.dot_general(
            queries, keys_ref[...], (((1,), (1,)), ((), ())), preferred_element_type=jnp.float32
        )
        return scores.reshape(SUB_HEADS, tok, keys) * LOG2_SCALE + bias_ref[...][None]

    def both_scores(sub):
        return scores_of(sub, mine_ref, bias_a_ref), scores_of(sub, other_ref, bias_b_ref)

    parts = []
    subs = HEAD_GROUP // SUB_HEADS
    ready = both_scores(0)
    for sub in range(subs):
        scores_a, scores_b = ready
        if sub + 1 < subs:
            ready = both_scores(sub + 1)
        top = jnp.max(jnp.maximum(scores_a, scores_b), axis=2, keepdims=True)
        weights_a = jnp.exp2(scores_a - top)
        weights_b = jnp.exp2(scores_b - top)
        total = jnp.sum(weights_a + weights_b, axis=2, keepdims=True)
        mixed = jnp.dot(
            weights_a.astype(jnp.bfloat16).reshape(rows, keys), mine_ref[:, 0:LAT],
            preferred_element_type=jnp.float32,
        ) + jnp.dot(
            weights_b.astype(jnp.bfloat16).reshape(rows, keys), other_ref[:, 0:LAT],
            preferred_element_type=jnp.float32,
        )
        latent = (mixed.reshape(SUB_HEADS, tok, LAT) / total).astype(jnp.bfloat16)
        for head in range(0, SUB_HEADS, 2):
            first = sub * SUB_HEADS + head
            pair = jnp.dot(
                latent[head : head + 2].reshape(2 * tok, LAT),
                jnp.concatenate([wv_ref[first], wv_ref[first + 1]], axis=1),
                preferred_element_type=jnp.float32,
            ).astype(jnp.bfloat16)
            parts.extend([pair[:tok, :VD], pair[tok:, VD:]])
    wide = HEAD_GROUP * VD
    values_ref[:, pl.ds(pl.multiple_of(group * wide, wide), wide)] = jnp.concatenate(parts, axis=1)

    @pl.when(group == HEADS // HEAD_GROUP - 1)
    def _():
        values = values_ref[...].astype(jnp.float32)
        square = jnp.mean(values * values, axis=1, keepdims=True)
        normed = values * lax.rsqrt(square + NORM_EPS) * gain_ref[...]
        normed = normed.astype(jnp.bfloat16)
        normed_ref[...] = normed
        up_ref[...] = normed[: tok // 2]
        down_ref[...] = normed[tok // 2 :]


def attention(my_index, q_nope, q_rope, mine, other, w_value, norm_gain):
    tok = q_nope.shape[0]
    total = mine.shape[0]
    rows = HEAD_GROUP * tok
    grid_spec = pltpu.PrefetchScalarGridSpec(
        num_scalar_prefetch=1,
        grid=(HEADS // HEAD_GROUP,),
        in_specs=[
            pl.BlockSpec((tok, HEAD_GROUP * LAT), lambda g, i: (0, g)),
            pl.BlockSpec((tok, HEAD_GROUP * ROPE), lambda g, i: (0, g)),
            pl.BlockSpec(mine.shape, lambda g, i: (0, 0)),
            pl.BlockSpec(mine.shape, lambda g, i: (0, 0)),
            pl.BlockSpec((HEAD_GROUP, LAT, VD), lambda g, i: (g, 0, 0)),
            pl.BlockSpec((1, HEADS * VD), lambda g, i: (0, 0)),
        ],
        out_specs=[
            pl.BlockSpec((tok, HEADS * VD), lambda g, i: (0, 0)),
            pl.BlockSpec((tok, HEADS * VD), lambda g, i: (0, 0)),
            pl.BlockSpec((tok // 2, HEADS * VD), lambda g, i: (0, 0)),
            pl.BlockSpec((tok // 2, HEADS * VD), lambda g, i: (0, 0)),
            pl.BlockSpec((tok, total // tok), lambda g, i: (0, 0)),
        ],
        scratch_shapes=[
            pltpu.VMEM((rows, LAT + 2 * ROPE), jnp.bfloat16),
            pltpu.VMEM((tok, total), jnp.float32),
            pltpu.VMEM((tok, total), jnp.float32),
        ],
    )
    shape = jax.ShapeDtypeStruct((tok, HEADS * VD), jnp.bfloat16)
    half_shape = jax.ShapeDtypeStruct((tok // 2, HEADS * VD), jnp.bfloat16)
    hits_shape = jax.ShapeDtypeStruct((tok, total // tok), jnp.float32)
    work = HEADS * tok * total * CORES
    return pl.pallas_call(
        functools.partial(attention_kernel, tok=tok),
        grid_spec=grid_spec,
        out_shape=[shape, shape, half_shape, half_shape, hits_shape],
        compiler_params=pltpu.CompilerParams(vmem_limit_bytes=56 << 20),
        cost_estimate=pl.CostEstimate(
            flops=2 * work * (2 * LAT + 2 * ROPE), bytes_accessed=8 << 20, transcendentals=work
        ),
    )(my_index.reshape(1), q_nope, q_rope, mine, other, w_value, norm_gain.reshape(1, HEADS * VD))


def ring_place(chip, chips):
    return jnp.where(chip % 2 == 0, chip // 2, chips - 1 - chip // 2)


def ring_chip(place, chips):
    return jnp.where(place < chips // 2, 2 * place, 2 * (chips - 1 - place) + 1)


def expert_kernel(
    index_ref, gate_a, up_a, down_a, hits_hbm, gate_hbm, up_hbm, down_hbm, *refs, hops, chips,
):
    *refs, hits_ref, gate_b, up_b, down_b, sems = refs
    outs = PIECES * len(hops)
    rows_refs, out_refs = refs[:-outs], refs[-outs:]
    pairs = ((hits_hbm, hits_ref), (gate_hbm, gate_b), (up_hbm, up_b), (down_hbm, down_b))
    copies = [
        pltpu.make_async_copy(there, here, sems.at[i]) for i, (there, here) in enumerate(pairs)
    ]
    for copy in copies:
        copy.start()
    my_chip, my_core = index_ref[0] // CORES, lax.rem(index_ref[0], CORES)
    rows = jnp.concatenate([ref[...] for ref in rows_refs], axis=0)

    def hit(hop):
        place = ring_place(my_chip, chips) + chips + hop * (2 * my_core - 1)
        source = ring_chip(lax.rem(place, chips), chips) ^ my_chip
        column = lax.broadcasted_iota(jnp.int32, hits_ref.shape, 1)
        return jnp.max(jnp.where(column == source, hits_ref[...], 0.0), axis=1, keepdims=True)

    def hidden(gate_ref, up_ref):
        gate_act = jnp.dot(rows, gate_ref[...], preferred_element_type=jnp.float32)
        up_act = jnp.dot(rows, up_ref[...], preferred_element_type=jnp.float32)
        return gate_act * (1.0 / (1.0 + jnp.exp(-gate_act))) * up_act

    def kept(act):
        return jnp.where(keep, act, 0.0).astype(jnp.bfloat16)

    act_a = hidden(gate_a, up_a)
    copies[0].wait()
    keep = jnp.concatenate([hit(hop) for hop in hops], axis=0) > 0.0
    part = jnp.dot(kept(act_a), down_a[...], preferred_element_type=jnp.float32)
    copies[1].wait()
    copies[2].wait()
    act_b = hidden(gate_b, up_b)
    copies[3].wait()
    part = part + jnp.dot(kept(act_b), down_b[...], preferred_element_type=jnp.float32)
    size = part.shape[0] // outs
    for i, out_ref in enumerate(out_refs):
        out_ref[...] = part[i * size : (i + 1) * size]


def expert_parts(my_index, rows, hits, own, swapped, hops, chips):
    tok, features = hits.shape[0], rows[0].shape[1]
    units = 2 * own[0].shape[1]
    outs = PIECES * len(hops)
    vmem, anywhere = pl.BlockSpec(memory_space=pltpu.VMEM), pl.BlockSpec(memory_space=pl.ANY)
    parts = pl.pallas_call(
        functools.partial(expert_kernel, hops=hops, chips=chips),
        in_specs=[pl.BlockSpec(memory_space=pltpu.SMEM)]
        + [vmem] * 3 + [anywhere] * 4 + [vmem] * len(rows),
        out_specs=[vmem] * outs,
        out_shape=[jax.ShapeDtypeStruct((tok // PIECES, features), jnp.float32)] * outs,
        scratch_shapes=[pltpu.VMEM(w.shape, w.dtype) for w in (hits, *swapped)]
        + [pltpu.SemaphoreType.DMA((4,))],
        compiler_params=pltpu.CompilerParams(vmem_limit_bytes=28 << 20),
        cost_estimate=pl.CostEstimate(
            flops=6 * tok * features * units, bytes_accessed=14 << 20, transcendentals=0
        ),
    )(my_index.reshape(1), *own, hits, *swapped, *rows)
    return [tuple(parts[i : i + PIECES]) for i in range(0, outs, PIECES)]


def local(
    q_nope, q_rope, c_kv, k_rope, w_value, norm_gain, expert_ids, gate_fixed, w_gate, w_up, w_down
):
    tok = c_kv.shape[0]
    n_ctx = lax.axis_size("ctx")
    chips = n_ctx // CORES
    my_index = lax.axis_index("ctx")
    siblings = [(i, i ^ 1) for i in range(n_ctx)]
    ring = list(range(0, chips, 2)) + list(range(1, chips, 2))[::-1]
    route = [
        (ring[p] * CORES + core, ring[(p + 1 - 2 * core) % chips] * CORES + core)
        for p in range(chips) for core in range(CORES)
    ]
    back = [(there, here) for here, there in route]

    def from_chip(block, step):
        return lax.ppermute(block, "ctx", [(i, i ^ (step * CORES)) for i in range(n_ctx)])

    ids = jnp.broadcast_to(expert_ids.astype(jnp.bfloat16), (tok, ROPE))
    block = jnp.concatenate([c_kv, k_rope, ids], axis=1)
    across = from_chip(block, chips // 2)
    near = [block] + [from_chip(block, step) for step in range(1, chips // 2)]
    far = [across] + [from_chip(across, step) for step in range(1, chips // 2)]
    mine = jnp.concatenate(near + far, axis=0)
    other = lax.ppermute(mine, "ctx", siblings)

    own, mine, other = lax.optimization_barrier(((w_gate[0], w_up[0], w_down[0]), mine, other))
    swapped = tuple(lax.ppermute(w, "ctx", siblings) for w in own)
    values, normed, upper, lower, hits = attention(
        my_index, q_nope, q_rope, mine, other, w_value, norm_gain
    )
    start, normed, swapped = lax.optimization_barrier(((upper, lower), normed, swapped))

    def parts_of(rows, hops):
        blocks = [block for hop in hops for block in rows[hop]]
        return expert_parts(my_index, blocks, table, own, swapped, hops, chips)

    def move(blocks, way=route):
        return tuple(lax.ppermute(x, "ctx", way) for x in blocks)

    def after(blocks, first):
        return tuple(lax.optimization_barrier((x, first))[0] for x in blocks)

    def added(part, arrived):
        return tuple(x + y.astype(jnp.float32) for x, y in zip(part, arrived))

    def rounded(part):
        return tuple(x.astype(jnp.bfloat16) for x in part)

    rows = {0: start, 1: move(start)}
    table = jnp.where(hits > 0.5, 1.0, 0.0)
    rows[2] = move(after(rows[1][:1], table)) + move(rows[1][1:])
    rows[chips - 1] = move(after((normed,), rows[1][-1]), back)
    rows[3] = move((jnp.concatenate(rows[2], axis=0),))
    parts = dict(zip((1,), parts_of(rows, (1,))))
    sums = rounded(parts[1])
    for hop in range(1, chips):
        arrived = move(sums)
        here = hop + 1
        if hop + 3 < chips - 2:
            rows[hop + 3] = move(after(rows[hop + 2], sums[0]))
        if hop == 3:
            rows[chips - 2] = move(after(rows[chips - 1], sums[0]), back)
        if here < chips - 2:
            hops = {1: (2, chips - 1, 0), chips - 4: (here, here + 1)}.get(hop, (here,))
            parts.update(zip(hops, parts_of(rows, hops)))
        if here < chips:
            sums = rounded(added(parts[here], arrived))
    expert_out = jnp.concatenate(added(parts[0], arrived), axis=0)
    gate_weight = gate_fixed.astype(jnp.float32) / 65536.0
    return (values.astype(jnp.float32) + gate_weight * expert_out).astype(jnp.bfloat16)


def solution(mesh):
    in_specs = (
        P(("rep", "ctx"), None),
        P(("rep", "ctx"), None),
        P(("rep", "ctx"), None),
        P(("rep", "ctx"), None),
        P(),
        P(),
        P(("rep", "ctx"), None),
        P(("rep", "ctx"), None),
        P("ctx", None, None),
        P("ctx", None, None),
        P("ctx", None, None),
    )
    out_specs = P(("rep", "ctx"), None)
    return jax.shard_map(local, mesh=mesh, in_specs=in_specs, out_specs=out_specs, check_vma=False)
```

```python
import functools
import math

import jax
import jax.numpy as jnp
from jax import lax
from jax.experimental import pallas as pl
from jax.experimental.pallas import tpu as pltpu
from jax.sharding import PartitionSpec as P

HEADS = 32
LAT = 512
ROPE = 64
VD = 128
SPAN = 8
CORES = 2

SCORE_SCALE = 192.0 ** (-0.5)
NORM_EPS = 1e-06
NEG_FILL = -1e30

HEAD_GROUP = 16
SUB_HEADS = 8
PIECES = 2
LOG2_SCALE = SCORE_SCALE * math.log2(math.e)


def attention_kernel(
    index_ref, q_ref, qr_ref, mine_ref, other_ref, wv_ref, gain_ref, values_ref, normed_ref,
    up_ref, down_ref, hits_ref, stack_ref, bias_a_ref, bias_b_ref, *, tok,
):
    group = pl.program_id(0)
    my_index = index_ref[0]
    my_chip, my_core = my_index // CORES, lax.rem(my_index, CORES)
    keys = mine_ref.shape[0]

    @pl.when(group == 0)
    def _():
        row_pos = my_index * tok + lax.broadcasted_iota(jnp.int32, (tok, keys), 0)
        key_iota = lax.broadcasted_iota(jnp.int32, (tok, keys), 1)
        key_chip = (key_iota // tok) ^ my_chip
        key_tok = lax.rem(key_iota, jnp.int32(tok))
        for core, bias_ref in ((my_core, bias_a_ref), (1 - my_core, bias_b_ref)):
            key_pos = (key_chip * CORES + core) * tok + key_tok
            bias_ref[...] = jnp.where(key_pos <= row_pos, 0.0, NEG_FILL)
        last = mine_ref[:, LAT : LAT + 2 * ROPE].astype(jnp.float32)
        lane = lax.broadcasted_iota(jnp.int32, last.shape, 1)
        named = jnp.max(jnp.where(lane >= ROPE, last, -1.0), axis=1, keepdims=True)
        my_expert = (my_index // SPAN).astype(jnp.float32)
        hits = jnp.where(named == my_expert, 1.0, 0.0)
        column = lax.broadcasted_iota(jnp.int32, hits_ref.shape, 1)
        table = jnp.zeros(hits_ref.shape, jnp.float32)
        for place in range(keys // tok):
            table = jnp.where(column == place, hits[place * tok : (place + 1) * tok], table)
        hits_ref[...] = table

    lane = lax.broadcasted_iota(jnp.int32, (tok, 2 * ROPE), 1)
    for head in range(HEAD_GROUP):
        at = pl.ds(head * tok, tok)
        stack_ref[at, 0:LAT] = q_ref[:, head * LAT : (head + 1) * LAT]
        pair = qr_ref[:, (head // 2) * 2 * ROPE : (head // 2 + 1) * 2 * ROPE]
        if head % 2:
            pair = jnp.concatenate([pair[:, ROPE:], pair[:, :ROPE]], axis=1)
        stack_ref[at, LAT : LAT + 2 * ROPE] = jnp.where(lane < ROPE, pair, jnp.zeros_like(pair))

    rows = SUB_HEADS * tok

    def scores_of(sub, keys_ref, bias_ref):
        queries = stack_ref[sub * rows : (sub + 1) * rows, :]
        scores = lax.dot_general(
            queries, keys_ref[...], (((1,), (1,)), ((), ())), preferred_element_type=jnp.float32
        )
        return scores.reshape(SUB_HEADS, tok, keys) * LOG2_SCALE + bias_ref[...][None]

    def both_scores(sub):
        return scores_of(sub, mine_ref, bias_a_ref), scores_of(sub, other_ref, bias_b_ref)

    parts = []
    subs = HEAD_GROUP // SUB_HEADS
    ready = both_scores(0)
    for sub in range(subs):
        scores_a, scores_b = ready
        if sub + 1 < subs:
            ready = both_scores(sub + 1)
        top = jnp.max(jnp.maximum(scores_a, scores_b), axis=2, keepdims=True)
        weights_a = jnp.exp2(scores_a - top)
        weights_b = jnp.exp2(scores_b - top)
        total = jnp.sum(weights_a + weights_b, axis=2, keepdims=True)
        mixed = jnp.dot(
            weights_a.astype(jnp.bfloat16).reshape(rows, keys), mine_ref[:, 0:LAT],
            preferred_element_type=jnp.float32,
        ) + jnp.dot(
            weights_b.astype(jnp.bfloat16).reshape(rows, keys), other_ref[:, 0:LAT],
            preferred_element_type=jnp.float32,
        )
        latent = (mixed.reshape(SUB_HEADS, tok, LAT) / total).astype(jnp.bfloat16)
        for head in range(0, SUB_HEADS, 2):
            first = sub * SUB_HEADS + head
            pair = jnp.dot(
                latent[head : head + 2].reshape(2 * tok, LAT),
                jnp.concatenate([wv_ref[first], wv_ref[first + 1]], axis=1),
                preferred_element_type=jnp.float32,
            ).astype(jnp.bfloat16)
            parts.extend([pair[:tok, :VD], pair[tok:, VD:]])
    wide = HEAD_GROUP * VD
    values_ref[:, pl.ds(pl.multiple_of(group * wide, wide), wide)] = jnp.concatenate(parts, axis=1)

    @pl.when(group == HEADS // HEAD_GROUP - 1)
    def _():
        values = values_ref[...].astype(jnp.float32)
        square = jnp.mean(values * values, axis=1, keepdims=True)
        normed = values * lax.rsqrt(square + NORM_EPS) * gain_ref[...]
        normed = normed.astype(jnp.bfloat16)
        normed_ref[...] = normed
        up_ref[...] = normed[: tok // 2]
        down_ref[...] = normed[tok // 2 :]


def attention(my_index, q_nope, q_rope, mine, other, w_value, norm_gain):
    tok = q_nope.shape[0]
    total = mine.shape[0]
    rows = HEAD_GROUP * tok
    grid_spec = pltpu.PrefetchScalarGridSpec(
        num_scalar_prefetch=1,
        grid=(HEADS // HEAD_GROUP,),
        in_specs=[
            pl.BlockSpec((tok, HEAD_GROUP * LAT), lambda g, i: (0, g)),
            pl.BlockSpec((tok, HEAD_GROUP * ROPE), lambda g, i: (0, g)),
            pl.BlockSpec(mine.shape, lambda g, i: (0, 0)),
            pl.BlockSpec(mine.shape, lambda g, i: (0, 0)),
            pl.BlockSpec((HEAD_GROUP, LAT, VD), lambda g, i: (g, 0, 0)),
            pl.BlockSpec((1, HEADS * VD), lambda g, i: (0, 0)),
        ],
        out_specs=[
            pl.BlockSpec((tok, HEADS * VD), lambda g, i: (0, 0)),
            pl.BlockSpec((tok, HEADS * VD), lambda g, i: (0, 0)),
            pl.BlockSpec((tok // 2, HEADS * VD), lambda g, i: (0, 0)),
            pl.BlockSpec((tok // 2, HEADS * VD), lambda g, i: (0, 0)),
            pl.BlockSpec((tok, total // tok), lambda g, i: (0, 0)),
        ],
        scratch_shapes=[
            pltpu.VMEM((rows, LAT + 2 * ROPE), jnp.bfloat16),
            pltpu.VMEM((tok, total), jnp.float32),
            pltpu.VMEM((tok, total), jnp.float32),
        ],
    )
    shape = jax.ShapeDtypeStruct((tok, HEADS * VD), jnp.bfloat16)
    half_shape = jax.ShapeDtypeStruct((tok // 2, HEADS * VD), jnp.bfloat16)
    hits_shape = jax.ShapeDtypeStruct((tok, total // tok), jnp.float32)
    work = HEADS * tok * total * CORES
    return pl.pallas_call(
        functools.partial(attention_kernel, tok=tok),
        grid_spec=grid_spec,
        out_shape=[shape, shape, half_shape, half_shape, hits_shape],
        compiler_params=pltpu.CompilerParams(vmem_limit_bytes=56 << 20),
        cost_estimate=pl.CostEstimate(
            flops=2 * work * (2 * LAT + 2 * ROPE), bytes_accessed=8 << 20, transcendentals=work
        ),
    )(my_index.reshape(1), q_nope, q_rope, mine, other, w_value, norm_gain.reshape(1, HEADS * VD))


def ring_place(chip, chips):
    return jnp.where(chip % 2 == 0, chip // 2, chips - 1 - chip // 2)


def ring_chip(place, chips):
    return jnp.where(place < chips // 2, 2 * place, 2 * (chips - 1 - place) + 1)


def expert_kernel(
    index_ref, gate_a, up_a, down_a, hits_hbm, gate_hbm, up_hbm, down_hbm, *refs, hops, chips,
):
    *refs, hits_ref, gate_b, up_b, down_b, sems = refs
    outs = PIECES * len(hops)
    rows_refs, out_refs = refs[:-outs], refs[-outs:]
    pairs = ((hits_hbm, hits_ref), (gate_hbm, gate_b), (up_hbm, up_b), (down_hbm, down_b))
    copies = [
        pltpu.make_async_copy(there, here, sems.at[i]) for i, (there, here) in enumerate(pairs)
    ]
    for copy in copies:
        copy.start()
    my_chip, my_core = index_ref[0] // CORES, lax.rem(index_ref[0], CORES)
    rows = jnp.concatenate([ref[...] for ref in rows_refs], axis=0)

    def hit(hop):
        place = ring_place(my_chip, chips) + chips + hop * (2 * my_core - 1)
        source = ring_chip(lax.rem(place, chips), chips) ^ my_chip
        column = lax.broadcasted_iota(jnp.int32, hits_ref.shape, 1)
        return jnp.max(jnp.where(column == source, hits_ref[...], 0.0), axis=1, keepdims=True)

    def hidden(gate_ref, up_ref):
        gate_act = jnp.dot(rows, gate_ref[...], preferred_element_type=jnp.float32)
        up_act = jnp.dot(rows, up_ref[...], preferred_element_type=jnp.float32)
        return gate_act * (1.0 / (1.0 + jnp.exp(-gate_act))) * up_act

    def kept(act):
        return jnp.where(keep, act, 0.0).astype(jnp.bfloat16)

    act_a = hidden(gate_a, up_a)
    copies[0].wait()
    keep = jnp.concatenate([hit(hop) for hop in hops], axis=0) > 0.0
    part = jnp.dot(kept(act_a), down_a[...], preferred_element_type=jnp.float32)
    copies[1].wait()
    copies[2].wait()
    act_b = hidden(gate_b, up_b)
    copies[3].wait()
    part = part + jnp.dot(kept(act_b), down_b[...], preferred_element_type=jnp.float32)
    size = part.shape[0] // outs
    for i, out_ref in enumerate(out_refs):
        out_ref[...] = part[i * size : (i + 1) * size]


def expert_parts(my_index, rows, hits, own, swapped, hops, chips):
    tok, features = hits.shape[0], rows[0].shape[1]
    units = 2 * own[0].shape[1]
    outs = PIECES * len(hops)
    vmem, anywhere = pl.BlockSpec(memory_space=pltpu.VMEM), pl.BlockSpec(memory_space=pl.ANY)
    parts = pl.pallas_call(
        functools.partial(expert_kernel, hops=hops, chips=chips),
        in_specs=[pl.BlockSpec(memory_space=pltpu.SMEM)]
        + [vmem] * 3 + [anywhere] * 4 + [vmem] * len(rows),
        out_specs=[vmem] * outs,
        out_shape=[jax.ShapeDtypeStruct((tok // PIECES, features), jnp.float32)] * outs,
        scratch_shapes=[pltpu.VMEM(w.shape, w.dtype) for w in (hits, *swapped)]
        + [pltpu.SemaphoreType.DMA((4,))],
        compiler_params=pltpu.CompilerParams(vmem_limit_bytes=28 << 20),
        cost_estimate=pl.CostEstimate(
            flops=6 * tok * features * units, bytes_accessed=14 << 20, transcendentals=0
        ),
    )(my_index.reshape(1), *own, hits, *swapped, *rows)
    return [tuple(parts[i : i + PIECES]) for i in range(0, outs, PIECES)]


def local(
    q_nope, q_rope, c_kv, k_rope, w_value, norm_gain, expert_ids, gate_fixed, w_gate, w_up, w_down
):
    tok = c_kv.shape[0]
    n_ctx = lax.axis_size("ctx")
    chips = n_ctx // CORES
    my_index = lax.axis_index("ctx")
    siblings = [(i, i ^ 1) for i in range(n_ctx)]
    ring = list(range(0, chips, 2)) + list(range(1, chips, 2))[::-1]
    route = [
        (ring[p] * CORES + core, ring[(p + 1 - 2 * core) % chips] * CORES + core)
        for p in range(chips) for core in range(CORES)
    ]
    back = [(there, here) for here, there in route]

    def from_chip(block, step):
        return lax.ppermute(block, "ctx", [(i, i ^ (step * CORES)) for i in range(n_ctx)])

    ids = jnp.broadcast_to(expert_ids.astype(jnp.bfloat16), (tok, ROPE))
    block = jnp.concatenate([c_kv, k_rope, ids], axis=1)
    across = from_chip(block, chips // 2)
    near = [block] + [from_chip(block, step) for step in range(1, chips // 2)]
    far = [across] + [from_chip(across, step) for step in range(1, chips // 2)]
    mine = jnp.concatenate(near + far, axis=0)
    other = lax.ppermute(mine, "ctx", siblings)

    own, mine, other = lax.optimization_barrier(((w_gate[0], w_up[0], w_down[0]), mine, other))
    swapped = tuple(lax.ppermute(w, "ctx", siblings) for w in own)
    values, normed, upper, lower, hits = attention(
        my_index, q_nope, q_rope, mine, other, w_value, norm_gain
    )
    start, normed, swapped = lax.optimization_barrier(((upper, lower), normed, swapped))

    def parts_of(rows, hops):
        blocks = [block for hop in hops for block in rows[hop]]
        return expert_parts(my_index, blocks, table, own, swapped, hops, chips)

    def move(blocks, way=route):
        return tuple(lax.ppermute(x, "ctx", way) for x in blocks)

    def after(blocks, first):
        return tuple(lax.optimization_barrier((x, first))[0] for x in blocks)

    def added(part, arrived):
        return tuple(x + y.astype(jnp.float32) for x, y in zip(part, arrived))

    def rounded(part):
        return tuple(x.astype(jnp.bfloat16) for x in part)

    rows = {0: start, 1: move(start)}
    table = jnp.where(hits > 0.5, 1.0, 0.0)
    rows[2] = move(after(rows[1][:1], table)) + move(rows[1][1:])
    rows[chips - 1] = move(after((normed,), rows[1][-1]), back)
    rows[3] = move((jnp.concatenate(rows[2], axis=0),))
    parts = dict(zip((1,), parts_of(rows, (1,))))
    sums = rounded(parts[1])
    for hop in range(1, chips):
        arrived = move(sums)
        here = hop + 1
        if hop + 3 < chips - 2:
            rows[hop + 3] = move(after(rows[hop + 2], sums[0]))
        if hop == chips - 4:
            rows[chips - 2] = move(after(rows[chips - 1], sums[0]), back)
        if here < chips - 1:
            hops = (here, chips - 1, 0) if hop == 1 else (here,)
            parts.update(zip(hops, parts_of(rows, hops)))
        if here < chips:
            sums = rounded(added(parts[here], arrived))
    expert_out = jnp.concatenate(added(parts[0], arrived), axis=0)
    gate_weight = gate_fixed.astype(jnp.float32) / 65536.0
    return (values.astype(jnp.float32) + gate_weight * expert_out).astype(jnp.bfloat16)


def solution(mesh):
    in_specs = (
        P(("rep", "ctx"), None),
        P(("rep", "ctx"), None),
        P(("rep", "ctx"), None),
        P(("rep", "ctx"), None),
        P(),
        P(),
        P(("rep", "ctx"), None),
        P(("rep", "ctx"), None),
        P("ctx", None, None),
        P("ctx", None, None),
        P("ctx", None, None),
    )
    out_specs = P(("rep", "ctx"), None)
    return jax.shard_map(local, mesh=mesh, in_specs=in_specs, out_specs=out_specs, check_vma=False)
```

```python
import functools
import math

import jax
import jax.numpy as jnp
from jax import lax
from jax.experimental import pallas as pl
from jax.experimental.pallas import tpu as pltpu
from jax.sharding import PartitionSpec as P

HEADS = 32
LAT = 512
ROPE = 64
VD = 128
SPAN = 8
CORES = 2

SCORE_SCALE = 192.0 ** (-0.5)
NORM_EPS = 1e-06
NEG_FILL = -1e30

HEAD_GROUP = 16
SUB_HEADS = 8
PIECES = 2
LOG2_SCALE = SCORE_SCALE * math.log2(math.e)


def attention_kernel(
    index_ref, q_ref, qr_ref, mine_ref, other_ref, wv_ref, gain_ref, values_ref, normed_ref,
    up_ref, down_ref, hits_ref, stack_ref, bias_a_ref, bias_b_ref, *, tok,
):
    group = pl.program_id(0)
    my_index = index_ref[0]
    my_chip, my_core = my_index // CORES, lax.rem(my_index, CORES)
    keys = mine_ref.shape[0]

    @pl.when(group == 0)
    def _():
        row_pos = my_index * tok + lax.broadcasted_iota(jnp.int32, (tok, keys), 0)
        key_iota = lax.broadcasted_iota(jnp.int32, (tok, keys), 1)
        key_chip = (key_iota // tok) ^ my_chip
        key_tok = lax.rem(key_iota, jnp.int32(tok))
        for core, bias_ref in ((my_core, bias_a_ref), (1 - my_core, bias_b_ref)):
            key_pos = (key_chip * CORES + core) * tok + key_tok
            bias_ref[...] = jnp.where(key_pos <= row_pos, 0.0, NEG_FILL)
        last = mine_ref[:, LAT : LAT + 2 * ROPE].astype(jnp.float32)
        lane = lax.broadcasted_iota(jnp.int32, last.shape, 1)
        named = jnp.max(jnp.where(lane >= ROPE, last, -1.0), axis=1, keepdims=True)
        my_expert = (my_index // SPAN).astype(jnp.float32)
        hits = jnp.where(named == my_expert, 1.0, 0.0)
        column = lax.broadcasted_iota(jnp.int32, hits_ref.shape, 1)
        table = jnp.zeros(hits_ref.shape, jnp.float32)
        for place in range(keys // tok):
            table = jnp.where(column == place, hits[place * tok : (place + 1) * tok], table)
        hits_ref[...] = table

    lane = lax.broadcasted_iota(jnp.int32, (tok, 2 * ROPE), 1)
    for head in range(HEAD_GROUP):
        at = pl.ds(head * tok, tok)
        stack_ref[at, 0:LAT] = q_ref[:, head * LAT : (head + 1) * LAT]
        pair = qr_ref[:, (head // 2) * 2 * ROPE : (head // 2 + 1) * 2 * ROPE]
        if head % 2:
            pair = jnp.concatenate([pair[:, ROPE:], pair[:, :ROPE]], axis=1)
        stack_ref[at, LAT : LAT + 2 * ROPE] = jnp.where(lane < ROPE, pair, jnp.zeros_like(pair))

    rows = SUB_HEADS * tok

    def scores_of(sub, keys_ref, bias_ref):
        queries = stack_ref[sub * rows : (sub + 1) * rows, :]
        scores = lax.dot_general(
            queries, keys_ref[...], (((1,), (1,)), ((), ())), preferred_element_type=jnp.float32
        )
        return scores.reshape(SUB_HEADS, tok, keys) * LOG2_SCALE + bias_ref[...][None]

    def both_scores(sub):
        return scores_of(sub, mine_ref, bias_a_ref), scores_of(sub, other_ref, bias_b_ref)

    parts = []
    subs = HEAD_GROUP // SUB_HEADS
    ready = both_scores(0)
    for sub in range(subs):
        scores_a, scores_b = ready
        if sub + 1 < subs:
            ready = both_scores(sub + 1)
        top = jnp.max(jnp.maximum(scores_a, scores_b), axis=2, keepdims=True)
        weights_a = jnp.exp2(scores_a - top)
        weights_b = jnp.exp2(scores_b - top)
        total = jnp.sum(weights_a + weights_b, axis=2, keepdims=True)
        mixed = jnp.dot(
            weights_a.astype(jnp.bfloat16).reshape(rows, keys), mine_ref[:, 0:LAT],
            preferred_element_type=jnp.float32,
        ) + jnp.dot(
            weights_b.astype(jnp.bfloat16).reshape(rows, keys), other_ref[:, 0:LAT],
            preferred_element_type=jnp.float32,
        )
        latent = (mixed.reshape(SUB_HEADS, tok, LAT) / total).astype(jnp.bfloat16)
        for head in range(0, SUB_HEADS, 2):
            first = sub * SUB_HEADS + head
            pair = jnp.dot(
                latent[head : head + 2].reshape(2 * tok, LAT),
                jnp.concatenate([wv_ref[first], wv_ref[first + 1]], axis=1),
                preferred_element_type=jnp.float32,
            ).astype(jnp.bfloat16)
            parts.extend([pair[:tok, :VD], pair[tok:, VD:]])
    wide = HEAD_GROUP * VD
    values_ref[:, pl.ds(pl.multiple_of(group * wide, wide), wide)] = jnp.concatenate(parts, axis=1)

    @pl.when(group == HEADS // HEAD_GROUP - 1)
    def _():
        values = values_ref[...].astype(jnp.float32)
        square = jnp.mean(values * values, axis=1, keepdims=True)
        normed = values * lax.rsqrt(square + NORM_EPS) * gain_ref[...]
        normed = normed.astype(jnp.bfloat16)
        normed_ref[...] = normed
        up_ref[...] = normed[: tok // 2]
        down_ref[...] = normed[tok // 2 :]


def attention(my_index, q_nope, q_rope, mine, other, w_value, norm_gain):
    tok = q_nope.shape[0]
    total = mine.shape[0]
    rows = HEAD_GROUP * tok
    grid_spec = pltpu.PrefetchScalarGridSpec(
        num_scalar_prefetch=1,
        grid=(HEADS // HEAD_GROUP,),
        in_specs=[
            pl.BlockSpec((tok, HEAD_GROUP * LAT), lambda g, i: (0, g)),
            pl.BlockSpec((tok, HEAD_GROUP * ROPE), lambda g, i: (0, g)),
            pl.BlockSpec(mine.shape, lambda g, i: (0, 0)),
            pl.BlockSpec(mine.shape, lambda g, i: (0, 0)),
            pl.BlockSpec((HEAD_GROUP, LAT, VD), lambda g, i: (g, 0, 0)),
            pl.BlockSpec((1, HEADS * VD), lambda g, i: (0, 0)),
        ],
        out_specs=[
            pl.BlockSpec((tok, HEADS * VD), lambda g, i: (0, 0)),
            pl.BlockSpec((tok, HEADS * VD), lambda g, i: (0, 0)),
            pl.BlockSpec((tok // 2, HEADS * VD), lambda g, i: (0, 0)),
            pl.BlockSpec((tok // 2, HEADS * VD), lambda g, i: (0, 0)),
            pl.BlockSpec((tok, total // tok), lambda g, i: (0, 0)),
        ],
        scratch_shapes=[
            pltpu.VMEM((rows, LAT + 2 * ROPE), jnp.bfloat16),
            pltpu.VMEM((tok, total), jnp.float32),
            pltpu.VMEM((tok, total), jnp.float32),
        ],
    )
    shape = jax.ShapeDtypeStruct((tok, HEADS * VD), jnp.bfloat16)
    half_shape = jax.ShapeDtypeStruct((tok // 2, HEADS * VD), jnp.bfloat16)
    hits_shape = jax.ShapeDtypeStruct((tok, total // tok), jnp.float32)
    work = HEADS * tok * total * CORES
    return pl.pallas_call(
        functools.partial(attention_kernel, tok=tok),
        grid_spec=grid_spec,
        out_shape=[shape, shape, half_shape, half_shape, hits_shape],
        compiler_params=pltpu.CompilerParams(vmem_limit_bytes=56 << 20),
        cost_estimate=pl.CostEstimate(
            flops=2 * work * (2 * LAT + 2 * ROPE), bytes_accessed=8 << 20, transcendentals=work
        ),
    )(my_index.reshape(1), q_nope, q_rope, mine, other, w_value, norm_gain.reshape(1, HEADS * VD))


def ring_place(chip, chips):
    return jnp.where(chip % 2 == 0, chip // 2, chips - 1 - chip // 2)


def ring_chip(place, chips):
    return jnp.where(place < chips // 2, 2 * place, 2 * (chips - 1 - place) + 1)


def expert_kernel(
    index_ref, gate_a, up_a, down_a, hits_hbm, gate_hbm, up_hbm, down_hbm, *refs, hops, chips,
):
    *refs, hits_ref, gate_b, up_b, down_b, sems = refs
    outs = PIECES * len(hops)
    rows_refs, out_refs = refs[:-outs], refs[-outs:]
    pairs = ((hits_hbm, hits_ref), (gate_hbm, gate_b), (up_hbm, up_b), (down_hbm, down_b))
    copies = [
        pltpu.make_async_copy(there, here, sems.at[i]) for i, (there, here) in enumerate(pairs)
    ]
    for copy in copies:
        copy.start()
    my_chip, my_core = index_ref[0] // CORES, lax.rem(index_ref[0], CORES)
    copies_of = 2 if len(hops) == 1 else 1
    rows = jnp.concatenate([ref[...] for ref in rows_refs] * copies_of, axis=0)

    def hit(hop):
        place = ring_place(my_chip, chips) + chips + hop * (2 * my_core - 1)
        source = ring_chip(lax.rem(place, chips), chips) ^ my_chip
        column = lax.broadcasted_iota(jnp.int32, hits_ref.shape, 1)
        return jnp.max(jnp.where(column == source, hits_ref[...], 0.0), axis=1, keepdims=True)

    def hidden(gate_ref, up_ref):
        gate_act = jnp.dot(rows, gate_ref[...], preferred_element_type=jnp.float32)
        up_act = jnp.dot(rows, up_ref[...], preferred_element_type=jnp.float32)
        return gate_act * (1.0 / (1.0 + jnp.exp(-gate_act))) * up_act

    def kept(act):
        return jnp.where(keep, act, 0.0).astype(jnp.bfloat16)

    act_a = hidden(gate_a, up_a)
    copies[0].wait()
    keep = jnp.concatenate([hit(hop) for hop in hops] * copies_of, axis=0) > 0.0
    part = jnp.dot(kept(act_a), down_a[...], preferred_element_type=jnp.float32)
    copies[1].wait()
    copies[2].wait()
    act_b = hidden(gate_b, up_b)
    copies[3].wait()
    part = part + jnp.dot(kept(act_b), down_b[...], preferred_element_type=jnp.float32)
    size = part.shape[0] // copies_of // outs
    for i, out_ref in enumerate(out_refs):
        out_ref[...] = part[i * size : (i + 1) * size]


def expert_parts(my_index, rows, hits, own, swapped, hops, chips):
    tok, features = hits.shape[0], rows[0].shape[1]
    units = 2 * own[0].shape[1]
    outs = PIECES * len(hops)
    vmem, anywhere = pl.BlockSpec(memory_space=pltpu.VMEM), pl.BlockSpec(memory_space=pl.ANY)
    parts = pl.pallas_call(
        functools.partial(expert_kernel, hops=hops, chips=chips),
        in_specs=[pl.BlockSpec(memory_space=pltpu.SMEM)]
        + [vmem] * 3 + [anywhere] * 4 + [vmem] * len(rows),
        out_specs=[vmem] * outs,
        out_shape=[jax.ShapeDtypeStruct((tok // PIECES, features), jnp.float32)] * outs,
        scratch_shapes=[pltpu.VMEM(w.shape, w.dtype) for w in (hits, *swapped)]
        + [pltpu.SemaphoreType.DMA((4,))],
        compiler_params=pltpu.CompilerParams(vmem_limit_bytes=28 << 20),
        cost_estimate=pl.CostEstimate(
            flops=6 * tok * features * units, bytes_accessed=14 << 20, transcendentals=0
        ),
    )(my_index.reshape(1), *own, hits, *swapped, *rows)
    return [tuple(parts[i : i + PIECES]) for i in range(0, outs, PIECES)]


def local(
    q_nope, q_rope, c_kv, k_rope, w_value, norm_gain, expert_ids, gate_fixed, w_gate, w_up, w_down
):
    tok = c_kv.shape[0]
    n_ctx = lax.axis_size("ctx")
    chips = n_ctx // CORES
    my_index = lax.axis_index("ctx")
    siblings = [(i, i ^ 1) for i in range(n_ctx)]
    ring = list(range(0, chips, 2)) + list(range(1, chips, 2))[::-1]
    route = [
        (ring[p] * CORES + core, ring[(p + 1 - 2 * core) % chips] * CORES + core)
        for p in range(chips) for core in range(CORES)
    ]
    back = [(there, here) for here, there in route]

    def from_chip(block, step):
        return lax.ppermute(block, "ctx", [(i, i ^ (step * CORES)) for i in range(n_ctx)])

    ids = jnp.broadcast_to(expert_ids.astype(jnp.bfloat16), (tok, ROPE))
    block = jnp.concatenate([c_kv, k_rope, ids], axis=1)
    across = from_chip(block, chips // 2)
    near = [block] + [from_chip(block, step) for step in range(1, chips // 2)]
    far = [across] + [from_chip(across, step) for step in range(1, chips // 2)]
    mine = jnp.concatenate(near + far, axis=0)
    other = lax.ppermute(mine, "ctx", siblings)

    own, mine, other = lax.optimization_barrier(((w_gate[0], w_up[0], w_down[0]), mine, other))
    swapped = tuple(lax.ppermute(w, "ctx", siblings) for w in own)
    values, normed, upper, lower, hits = attention(
        my_index, q_nope, q_rope, mine, other, w_value, norm_gain
    )
    start, normed, swapped = lax.optimization_barrier(((upper, lower), normed, swapped))

    def parts_of(rows, hops):
        blocks = [block for hop in hops for block in rows[hop]]
        return expert_parts(my_index, blocks, table, own, swapped, hops, chips)

    def move(blocks, way=route):
        return tuple(lax.ppermute(x, "ctx", way) for x in blocks)

    def after(blocks, first):
        return tuple(lax.optimization_barrier((x, first))[0] for x in blocks)

    def added(part, arrived):
        return tuple(x + y.astype(jnp.float32) for x, y in zip(part, arrived))

    def rounded(part):
        return tuple(x.astype(jnp.bfloat16) for x in part)

    rows = {0: start, 1: move(start)}
    table = jnp.where(hits > 0.5, 1.0, 0.0)
    rows[2] = move(after(rows[1][:1], table)) + move(rows[1][1:])
    rows[chips - 1] = move(after((normed,), rows[1][-1]), back)
    rows[3] = move((jnp.concatenate(rows[2], axis=0),))
    parts = dict(zip((1,), parts_of(rows, (1,))))
    sums = rounded(parts[1])
    for hop in range(1, chips):
        arrived = move(sums)
        here = hop + 1
        if hop + 3 < chips - 1:
            rows[hop + 3] = move(after(rows[hop + 2], sums[0]))
        if here < chips - 1:
            hops = (here, chips - 1, 0) if hop == 1 else (here,)
            parts.update(zip(hops, parts_of(rows, hops)))
        if here < chips:
            sums = rounded(added(parts[here], arrived))
    expert_out = jnp.concatenate(added(parts[0], arrived), axis=0)
    gate_weight = gate_fixed.astype(jnp.float32) / 65536.0
    return (values.astype(jnp.float32) + gate_weight * expert_out).astype(jnp.bfloat16)


def solution(mesh):
    in_specs = (
        P(("rep", "ctx"), None),
        P(("rep", "ctx"), None),
        P(("rep", "ctx"), None),
        P(("rep", "ctx"), None),
        P(),
        P(),
        P(("rep", "ctx"), None),
        P(("rep", "ctx"), None),
        P("ctx", None, None),
        P("ctx", None, None),
        P("ctx", None, None),
    )
    out_specs = P(("rep", "ctx"), None)
    return jax.shard_map(local, mesh=mesh, in_specs=in_specs, out_specs=out_specs, check_vma=False)
```

```python
import functools
import math

import jax
import jax.numpy as jnp
from jax import lax
from jax.experimental import pallas as pl
from jax.experimental.pallas import tpu as pltpu
from jax.sharding import PartitionSpec as P

HEADS = 32
LAT = 512
ROPE = 64
VD = 128
SPAN = 8
CORES = 2

SCORE_SCALE = 192.0 ** (-0.5)
NORM_EPS = 1e-06
NEG_FILL = -1e30

HEAD_GROUP = 16
SUB_HEADS = 8
PIECES = 2
LOG2_SCALE = SCORE_SCALE * math.log2(math.e)


def attention_kernel(
    index_ref, q_ref, qr_ref, mine_ref, other_ref, wv_ref, gain_ref, values_ref, normed_ref,
    up_ref, down_ref, hits_ref, stack_ref, bias_a_ref, bias_b_ref, *, tok,
):
    group = pl.program_id(0)
    my_index = index_ref[0]
    my_chip, my_core = my_index // CORES, lax.rem(my_index, CORES)
    keys = mine_ref.shape[0]

    @pl.when(group == 0)
    def _():
        row_pos = my_index * tok + lax.broadcasted_iota(jnp.int32, (tok, keys), 0)
        key_iota = lax.broadcasted_iota(jnp.int32, (tok, keys), 1)
        key_chip = (key_iota // tok) ^ my_chip
        key_tok = lax.rem(key_iota, jnp.int32(tok))
        for core, bias_ref in ((my_core, bias_a_ref), (1 - my_core, bias_b_ref)):
            key_pos = (key_chip * CORES + core) * tok + key_tok
            bias_ref[...] = jnp.where(key_pos <= row_pos, 0.0, NEG_FILL)
        last = mine_ref[:, LAT : LAT + 2 * ROPE].astype(jnp.float32)
        lane = lax.broadcasted_iota(jnp.int32, last.shape, 1)
        named = jnp.max(jnp.where(lane >= ROPE, last, -1.0), axis=1, keepdims=True)
        my_expert = (my_index // SPAN).astype(jnp.float32)
        hits = jnp.where(named == my_expert, 1.0, 0.0)
        column = lax.broadcasted_iota(jnp.int32, hits_ref.shape, 1)
        table = jnp.zeros(hits_ref.shape, jnp.float32)
        for place in range(keys // tok):
            table = jnp.where(column == place, hits[place * tok : (place + 1) * tok], table)
        hits_ref[...] = table

    lane = lax.broadcasted_iota(jnp.int32, (tok, 2 * ROPE), 1)
    for head in range(HEAD_GROUP):
        at = pl.ds(head * tok, tok)
        stack_ref[at, 0:LAT] = q_ref[:, head * LAT : (head + 1) * LAT]
        pair = qr_ref[:, (head // 2) * 2 * ROPE : (head // 2 + 1) * 2 * ROPE]
        if head % 2:
            pair = jnp.concatenate([pair[:, ROPE:], pair[:, :ROPE]], axis=1)
        stack_ref[at, LAT : LAT + 2 * ROPE] = jnp.where(lane < ROPE, pair, jnp.zeros_like(pair))

    rows = SUB_HEADS * tok

    def scores_of(sub, keys_ref, bias_ref):
        queries = stack_ref[sub * rows : (sub + 1) * rows, :]
        scores = lax.dot_general(
            queries, keys_ref[...], (((1,), (1,)), ((), ())), preferred_element_type=jnp.float32
        )
        return scores.reshape(SUB_HEADS, tok, keys) * LOG2_SCALE + bias_ref[...][None]

    def both_scores(sub):
        return scores_of(sub, mine_ref, bias_a_ref), scores_of(sub, other_ref, bias_b_ref)

    parts = []
    subs = HEAD_GROUP // SUB_HEADS
    ready = both_scores(0)
    for sub in range(subs):
        scores_a, scores_b = ready
        if sub + 1 < subs:
            ready = both_scores(sub + 1)
        top = jnp.max(jnp.maximum(scores_a, scores_b), axis=2, keepdims=True)
        weights_a = jnp.exp2(scores_a - top)
        weights_b = jnp.exp2(scores_b - top)
        total = jnp.sum(weights_a + weights_b, axis=2, keepdims=True)
        mixed = jnp.dot(
            weights_a.astype(jnp.bfloat16).reshape(rows, keys), mine_ref[:, 0:LAT],
            preferred_element_type=jnp.float32,
        ) + jnp.dot(
            weights_b.astype(jnp.bfloat16).reshape(rows, keys), other_ref[:, 0:LAT],
            preferred_element_type=jnp.float32,
        )
        latent = (mixed.reshape(SUB_HEADS, tok, LAT) * (1.0 / total)).astype(jnp.bfloat16)
        for head in range(0, SUB_HEADS, 2):
            first = sub * SUB_HEADS + head
            pair = jnp.dot(
                latent[head : head + 2].reshape(2 * tok, LAT),
                jnp.concatenate([wv_ref[first], wv_ref[first + 1]], axis=1),
                preferred_element_type=jnp.float32,
            ).astype(jnp.bfloat16)
            parts.extend([pair[:tok, :VD], pair[tok:, VD:]])
    wide = HEAD_GROUP * VD
    values_ref[:, pl.ds(pl.multiple_of(group * wide, wide), wide)] = jnp.concatenate(parts, axis=1)

    @pl.when(group == HEADS // HEAD_GROUP - 1)
    def _():
        values = values_ref[...].astype(jnp.float32)
        square = jnp.mean(values * values, axis=1, keepdims=True)
        normed = values * lax.rsqrt(square + NORM_EPS) * gain_ref[...]
        normed = normed.astype(jnp.bfloat16)
        normed_ref[...] = normed
        up_ref[...] = normed[: tok // 2]
        down_ref[...] = normed[tok // 2 :]


def attention(my_index, q_nope, q_rope, mine, other, w_value, norm_gain):
    tok = q_nope.shape[0]
    total = mine.shape[0]
    rows = HEAD_GROUP * tok
    grid_spec = pltpu.PrefetchScalarGridSpec(
        num_scalar_prefetch=1,
        grid=(HEADS // HEAD_GROUP,),
        in_specs=[
            pl.BlockSpec((tok, HEAD_GROUP * LAT), lambda g, i: (0, g)),
            pl.BlockSpec((tok, HEAD_GROUP * ROPE), lambda g, i: (0, g)),
            pl.BlockSpec(mine.shape, lambda g, i: (0, 0)),
            pl.BlockSpec(mine.shape, lambda g, i: (0, 0)),
            pl.BlockSpec((HEAD_GROUP, LAT, VD), lambda g, i: (g, 0, 0)),
            pl.BlockSpec((1, HEADS * VD), lambda g, i: (0, 0)),
        ],
        out_specs=[
            pl.BlockSpec((tok, HEADS * VD), lambda g, i: (0, 0)),
            pl.BlockSpec((tok, HEADS * VD), lambda g, i: (0, 0)),
            pl.BlockSpec((tok // 2, HEADS * VD), lambda g, i: (0, 0)),
            pl.BlockSpec((tok // 2, HEADS * VD), lambda g, i: (0, 0)),
            pl.BlockSpec((tok, total // tok), lambda g, i: (0, 0)),
        ],
        scratch_shapes=[
            pltpu.VMEM((rows, LAT + 2 * ROPE), jnp.bfloat16),
            pltpu.VMEM((tok, total), jnp.float32),
            pltpu.VMEM((tok, total), jnp.float32),
        ],
    )
    shape = jax.ShapeDtypeStruct((tok, HEADS * VD), jnp.bfloat16)
    half_shape = jax.ShapeDtypeStruct((tok // 2, HEADS * VD), jnp.bfloat16)
    hits_shape = jax.ShapeDtypeStruct((tok, total // tok), jnp.float32)
    work = HEADS * tok * total * CORES
    return pl.pallas_call(
        functools.partial(attention_kernel, tok=tok),
        grid_spec=grid_spec,
        out_shape=[shape, shape, half_shape, half_shape, hits_shape],
        compiler_params=pltpu.CompilerParams(vmem_limit_bytes=56 << 20),
        cost_estimate=pl.CostEstimate(
            flops=2 * work * (2 * LAT + 2 * ROPE), bytes_accessed=8 << 20, transcendentals=work
        ),
    )(my_index.reshape(1), q_nope, q_rope, mine, other, w_value, norm_gain.reshape(1, HEADS * VD))


def ring_place(chip, chips):
    return jnp.where(chip % 2 == 0, chip // 2, chips - 1 - chip // 2)


def ring_chip(place, chips):
    return jnp.where(place < chips // 2, 2 * place, 2 * (chips - 1 - place) + 1)


def expert_kernel(
    index_ref, gate_a, up_a, down_a, hits_hbm, gate_hbm, up_hbm, down_hbm, *refs, hops, chips,
):
    *refs, hits_ref, gate_b, up_b, down_b, sems = refs
    outs = PIECES * len(hops)
    rows_refs, out_refs = refs[:-outs], refs[-outs:]
    pairs = ((hits_hbm, hits_ref), (gate_hbm, gate_b), (up_hbm, up_b), (down_hbm, down_b))
    copies = [
        pltpu.make_async_copy(there, here, sems.at[i]) for i, (there, here) in enumerate(pairs)
    ]
    for copy in copies:
        copy.start()
    my_chip, my_core = index_ref[0] // CORES, lax.rem(index_ref[0], CORES)
    copies_of = 2 if len(hops) == 1 else 1
    rows = jnp.concatenate([ref[...] for ref in rows_refs] * copies_of, axis=0)

    def hit(hop):
        place = ring_place(my_chip, chips) + chips + hop * (2 * my_core - 1)
        source = ring_chip(lax.rem(place, chips), chips) ^ my_chip
        column = lax.broadcasted_iota(jnp.int32, hits_ref.shape, 1)
        return jnp.max(jnp.where(column == source, hits_ref[...], 0.0), axis=1, keepdims=True)

    def hidden(gate_ref, up_ref):
        gate_act = jnp.dot(rows, gate_ref[...], preferred_element_type=jnp.float32)
        up_act = jnp.dot(rows, up_ref[...], preferred_element_type=jnp.float32)
        return gate_act * (1.0 / (1.0 + jnp.exp(-gate_act))) * up_act

    def kept(act):
        return jnp.where(keep, act, 0.0).astype(jnp.bfloat16)

    act_a = hidden(gate_a, up_a)
    copies[0].wait()
    keep = jnp.concatenate([hit(hop) for hop in hops] * copies_of, axis=0) > 0.0
    part = jnp.dot(kept(act_a), down_a[...], preferred_element_type=jnp.float32)
    copies[1].wait()
    copies[2].wait()
    act_b = hidden(gate_b, up_b)
    copies[3].wait()
    part = part + jnp.dot(kept(act_b), down_b[...], preferred_element_type=jnp.float32)
    size = part.shape[0] // copies_of // outs
    for i, out_ref in enumerate(out_refs):
        out_ref[...] = part[i * size : (i + 1) * size]


def expert_parts(my_index, rows, hits, own, swapped, hops, chips):
    tok, features = hits.shape[0], rows[0].shape[1]
    units = 2 * own[0].shape[1]
    outs = PIECES * len(hops)
    vmem, anywhere = pl.BlockSpec(memory_space=pltpu.VMEM), pl.BlockSpec(memory_space=pl.ANY)
    parts = pl.pallas_call(
        functools.partial(expert_kernel, hops=hops, chips=chips),
        in_specs=[pl.BlockSpec(memory_space=pltpu.SMEM)]
        + [vmem] * 3 + [anywhere] * 4 + [vmem] * len(rows),
        out_specs=[vmem] * outs,
        out_shape=[jax.ShapeDtypeStruct((tok // PIECES, features), jnp.float32)] * outs,
        scratch_shapes=[pltpu.VMEM(w.shape, w.dtype) for w in (hits, *swapped)]
        + [pltpu.SemaphoreType.DMA((4,))],
        compiler_params=pltpu.CompilerParams(vmem_limit_bytes=28 << 20),
        cost_estimate=pl.CostEstimate(
            flops=6 * tok * features * units, bytes_accessed=14 << 20, transcendentals=0
        ),
    )(my_index.reshape(1), *own, hits, *swapped, *rows)
    return [tuple(parts[i : i + PIECES]) for i in range(0, outs, PIECES)]


def local(
    q_nope, q_rope, c_kv, k_rope, w_value, norm_gain, expert_ids, gate_fixed, w_gate, w_up, w_down
):
    tok = c_kv.shape[0]
    n_ctx = lax.axis_size("ctx")
    chips = n_ctx // CORES
    my_index = lax.axis_index("ctx")
    siblings = [(i, i ^ 1) for i in range(n_ctx)]
    ring = list(range(0, chips, 2)) + list(range(1, chips, 2))[::-1]
    route = [
        (ring[p] * CORES + core, ring[(p + 1 - 2 * core) % chips] * CORES + core)
        for p in range(chips) for core in range(CORES)
    ]
    back = [(there, here) for here, there in route]

    def from_chip(block, step):
        return lax.ppermute(block, "ctx", [(i, i ^ (step * CORES)) for i in range(n_ctx)])

    ids = jnp.broadcast_to(expert_ids.astype(jnp.bfloat16), (tok, ROPE))
    block = jnp.concatenate([c_kv, k_rope, ids], axis=1)
    across = from_chip(block, chips // 2)
    near = [block] + [from_chip(block, step) for step in range(1, chips // 2)]
    far = [across] + [from_chip(across, step) for step in range(1, chips // 2)]
    mine = jnp.concatenate(near + far, axis=0)
    other = lax.ppermute(mine, "ctx", siblings)

    own, mine, other = lax.optimization_barrier(((w_gate[0], w_up[0], w_down[0]), mine, other))
    swapped = tuple(lax.ppermute(w, "ctx", siblings) for w in own)
    values, normed, upper, lower, hits = attention(
        my_index, q_nope, q_rope, mine, other, w_value, norm_gain
    )
    start, normed, swapped = lax.optimization_barrier(((upper, lower), normed, swapped))

    def parts_of(rows, hops):
        blocks = [block for hop in hops for block in rows[hop]]
        return expert_parts(my_index, blocks, table, own, swapped, hops, chips)

    def move(blocks, way=route):
        return tuple(lax.ppermute(x, "ctx", way) for x in blocks)

    def after(blocks, first):
        return tuple(lax.optimization_barrier((x, first))[0] for x in blocks)

    def added(part, arrived):
        return tuple(x + y.astype(jnp.float32) for x, y in zip(part, arrived))

    def rounded(part):
        return tuple(x.astype(jnp.bfloat16) for x in part)

    rows = {0: start, 1: move(start)}
    table = jnp.where(hits > 0.5, 1.0, 0.0)
    rows[2] = move(after(rows[1][:1], table)) + move(rows[1][1:])
    rows[chips - 1] = move(after((normed,), rows[1][-1]), back)
    rows[3] = move((jnp.concatenate(rows[2], axis=0),))
    parts = dict(zip((1,), parts_of(rows, (1,))))
    sums = rounded(parts[1])
    for hop in range(1, chips):
        arrived = move(sums)
        here = hop + 1
        if hop + 3 < chips - 1:
            rows[hop + 3] = move(after(rows[hop + 2], sums[0]))
        if here < chips - 1:
            hops = (here, chips - 1, 0) if hop == 1 else (here,)
            parts.update(zip(hops, parts_of(rows, hops)))
        if here < chips:
            sums = rounded(added(parts[here], arrived))
    expert_out = jnp.concatenate(added(parts[0], arrived), axis=0)
    gate_weight = gate_fixed.astype(jnp.float32) / 65536.0
    return (values.astype(jnp.float32) + gate_weight * expert_out).astype(jnp.bfloat16)


def solution(mesh):
    in_specs = (
        P(("rep", "ctx"), None),
        P(("rep", "ctx"), None),
        P(("rep", "ctx"), None),
        P(("rep", "ctx"), None),
        P(),
        P(),
        P(("rep", "ctx"), None),
        P(("rep", "ctx"), None),
        P("ctx", None, None),
        P("ctx", None, None),
        P("ctx", None, None),
    )
    out_specs = P(("rep", "ctx"), None)
    return jax.shard_map(local, mesh=mesh, in_specs=in_specs, out_specs=out_specs, check_vma=False)
```
